256 devices in a mesh: vec: 32 (over y, x, core), row: 8 (over z).
Axes of the slice: x: 4, y: 4, z: 8, core: 2. Of those that a mesh axis runs over, the one named last changes fastest.
Arguments:
- blocks: bfloat16 [8192, 1024, 128], P('vec', 'row'), may hold values from -6 to 6
- block_vector: int32 [8, 8192], P('row', 'vec'), may hold values from 0 to 127, as said below
- block_pair: int32 [8, 8192], P('row', 'vec'), may hold values from 0 to 71
- block_count: int32 [8, 32], P('row', 'vec'), may hold values from 8 to 256, as said below
- occ_order: int32 [288], replicated, may hold values from 0 to 287, each once
- occ_coeffs: bfloat16 [3072, 288], P('row'), may hold values from -0.109375 to 0.109375
- vir_coeffs: bfloat16 [3072, 2688], P('row'), may hold values from -0.109375 to 0.109375
Outputs:
- ov_blocks: bfloat16 [2688, 288, 128], P('row', 'vec')
- oo_blocks: bfloat16 [288, 288, 128], P('row', 'vec')
The draws below stay inside these ranges and needn't reach their ends.
Inputs may be any that keep to these rules, and one draw needn't show every extreme that they name: `block_vector`: of one device's valid slots, at most 8 name vectors of one owner (vector // 4); in each row index one owner receives exactly 8 valid slots from every device. `block_count`: in each row index some device has all 256 slots valid.
All inputs are finite; a program needn't handle non-finite values.
Results may differ from the reference program's by a relative error of at most 0.0052.
Values may be sent and summed in bfloat16 or wider, within the bound.
A program may use at most 128 MiB of HBM per device.

```python
import jax
import jax.numpy as jnp
from jax import lax

NAO = 3072
NO = 288
NV = 2688
BLK = 128
VEC_DEV = 4
CAP = 8
VECS = 128
MAXB = 256
N_VEC = 32
N_ROW = 8


def shared_counts(key):
    key_one, key_two = jax.random.split(key)
    base_counts = jax.random.randint(key_one, (N_ROW, N_VEC), CAP, MAXB // 2 + 1)
    full_slot = jax.random.randint(key_two, (N_ROW, 1), 0, N_VEC)
    lane_index = jnp.arange(N_VEC)[None, :]
    return jnp.where(lane_index == full_slot, MAXB, base_counts).astype(jnp.int32)


def owner_slots(key, slot_count, hot_owner):
    key_one, key_two = jax.random.split(key)
    others = jax.random.permutation(key_one, MAXB - CAP) + CAP
    sequence = jnp.concatenate([jnp.arange(CAP), others])
    tokens = (sequence // CAP + hot_owner) % N_VEC
    slot_index = jnp.arange(MAXB)
    scores = jax.random.randint(key_two, (MAXB,), 0, 1 << 20) + jnp.where(slot_index < slot_count, 0, 1 << 21)
    ordering = jnp.argsort(scores * MAXB + slot_index, stable=True)
    return tokens[ordering]


def draw_block_count(key, part):
    return shared_counts(key)


def draw_block_vector(key, part):
    counts = shared_counts(key)
    key = jax.random.fold_in(key, 7)
    hot_key, slot_key, member_key = jax.random.split(key, 3)
    hot_owner = jnp.broadcast_to(jax.random.randint(hot_key, (N_ROW, 1), 0, N_VEC), (N_ROW, N_VEC))
    flat_keys = jax.random.split(slot_key, N_ROW * N_VEC)
    owners = jax.vmap(owner_slots)(flat_keys, counts.reshape(-1), hot_owner.reshape(-1))
    owners = owners.reshape(N_ROW, N_VEC * MAXB)
    within = jax.random.randint(member_key, (N_ROW, N_VEC * MAXB), 0, VEC_DEV)
    return (owners * VEC_DEV + within).astype(jnp.int32)


def set_ends(array, own_key, low, high):
    shape = array.shape
    spot = [jax.random.randint(jax.random.fold_in(own_key, axis), (), 0, shape[axis]) for axis in range(len(shape))]
    array = array.at[tuple(spot)].set(low)
    longest = shape.index(max(shape))
    spot[longest] = (spot[longest] + 1) % shape[longest]
    return array.at[tuple(spot)].set(high)


def steps_of(stream_key, extent, cuts, low, high):
    def one(position, blocks):
        draws = jax.random.uniform(jax.random.fold_in(jax.random.fold_in(stream_key, 6), position), (blocks,), jnp.float32, low / len(cuts), high / len(cuts))
        return jnp.repeat(jnp.exp(draws), extent[position] // blocks).reshape((-1,) + (1,) * (len(extent) - position - 1))

    level = one(*cuts[0])
    for cut in cuts[1:]:
        level = level * one(*cut)
    return level


def gaussian(rng, shape, spread, limit, pieces=(), held_as=jnp.bfloat16):
    array = jax.random.normal(rng, shape, jnp.float32) * spread
    if len(pieces) > 0:
        array = steps_of(rng, shape, pieces, -0.22, 0.18) * array
    return jnp.clip(array, min=-limit, max=limit).astype(held_as)


def setup_inputs(seed: int = 0) -> dict:
    splits = jax.random.split(jax.random.key(seed), 8)
    blocks = gaussian(splits[0], (N_VEC * MAXB, N_ROW * BLK, BLK), 1.0, 6.0, ((0, 32), (1, 8)))
    block_vector = draw_block_vector(jax.random.fold_in(splits[7], 71), 0)
    block_pair = set_ends(jax.random.randint(splits[2], (N_ROW, N_VEC * MAXB), 0, (NAO // BLK) * (NAO // BLK // N_ROW)), jax.random.fold_in(splits[2], 1), 0, ((NAO // BLK) * (NAO // BLK // N_ROW)) - 1).astype(jnp.int32)
    block_count = draw_block_count(jax.random.fold_in(splits[7], 71), 0)
    occ_order = jax.random.permutation(splits[4], NO).astype(jnp.int32)
    occ_coeffs = gaussian(splits[5], (NAO, NO), NAO ** -0.5, 0.109375, ((0, 8),))
    vir_coeffs = gaussian(splits[6], (NAO, NV), NAO ** -0.5, 0.109375, ((0, 8),))
    return dict(blocks=blocks, block_vector=block_vector, block_pair=block_pair, block_count=block_count, occ_order=occ_order, occ_coeffs=occ_coeffs, vir_coeffs=vir_coeffs)


def reference(blocks, block_vector, block_pair, block_count, occ_order, occ_coeffs, vir_coeffs):
    tile_rows = NAO // N_ROW // BLK
    tiles_across = NAO // BLK
    pair_total = tile_rows * tiles_across
    row_span = NAO // N_ROW
    perm_occ = occ_coeffs[:, occ_order]
    perm_wide = perm_occ.astype(jnp.float32)
    vir_wide = vir_coeffs.astype(jnp.float32)
    slot_index = jnp.arange(MAXB, dtype=jnp.int32)
    ov_total = jnp.zeros((NV, NO, VECS), jnp.float32)
    oo_total = jnp.zeros((NO, NO, VECS), jnp.float32)
    for row_group in range(N_ROW):
        tile_data = blocks[:, row_group * BLK:(row_group + 1) * BLK, :].astype(jnp.float32)
        is_valid = (slot_index[None, :] < block_count[row_group][:, None]).reshape(-1)
        target = jnp.where(is_valid, block_vector[row_group] * pair_total + block_pair[row_group], VECS * pair_total).astype(jnp.int32)
        placed = jnp.zeros((VECS * pair_total, BLK, BLK), jnp.float32).at[target].add(tile_data, mode="drop")
        matrix = placed.reshape(VECS, tile_rows, tiles_across, BLK, BLK).transpose(0, 1, 3, 2, 4).reshape(VECS, row_span, NAO)
        matrix = lax.optimization_barrier(matrix.astype(jnp.bfloat16)).astype(jnp.float32)
        half_moved = jnp.einsum("vrm,mi->vri", matrix, perm_wide)
        half_moved = lax.optimization_barrier(half_moved.astype(jnp.bfloat16)).astype(jnp.float32)
        lower = row_group * row_span
        ov_total = ov_total + jnp.einsum("ma,vmi->aiv", vir_wide[lower:lower + row_span], half_moved)
        oo_total = oo_total + jnp.einsum("mj,vmi->jiv", perm_wide[lower:lower + row_span], half_moved)
    return ov_total.astype(jnp.bfloat16), oo_total.astype(jnp.bfloat16)
```

```python
import jax
import jax.numpy as jnp
from jax import lax
from jax.experimental import pallas as pl
from jax.experimental.pallas import tpu as pltpu
from jax.sharding import PartitionSpec as P

MESH = pl.DeviceIdType.MESH
F32, BF16, I32 = jnp.float32, jnp.bfloat16, jnp.int32

N_VEC, N_ROW, N_CHIP = 32, 8, 16
CAP, SLOTS, BLK = 8, 256, 128
NAO, NO, NV, SPAN = 3072, 288, 2688, 384
VEC_DEV, PAIRS, ACROSS, TALL = 4, 72, 24, 3
NV_R, NO_R, NO_V = NV // N_ROW, NO // N_ROW, NO // N_VEC
W_R = 384
WIDE = 4 * W_R
K_HALF = NO // 2
CHUNK = 32
PARTS = 8
Q = 8
VMEM = pltpu.VMEM
ANY = pl.BlockSpec(memory_space=pl.ANY)
IN_VMEM = pl.BlockSpec(memory_space=pltpu.VMEM)
DMA = pltpu.SemaphoreType.DMA


def prepare_kernel(vec_ref, pair_ref, count_ref, order_ref, occ_ref, vir_ref, blocks_ref,
                   send_ref, code_ref, w_ref, perm_ref, pos_vmem, pos_smem, sem, pos_sem):
    core = lax.rem(lax.axis_index("vec"), 2)
    count = count_ref[0, 0]
    vectors, pairs = vec_ref[...], pair_ref[...]
    owner = vectors // VEC_DEV
    code = vectors % VEC_DEV * PAIRS + pairs + 1
    above = lax.broadcasted_iota(I32, (SLOTS, SLOTS), 0)
    across = lax.broadcasted_iota(I32, (SLOTS, SLOTS), 1)
    owner_col = jnp.sum(jnp.where(above == across, owner, 0), axis=1, keepdims=True)
    earlier = (owner_col == owner) & (above < across)
    rank = jnp.sum(jnp.where(earlier, 1, 0), axis=0, keepdims=True)
    pos_vmem[...] = owner * CAP + rank
    to_smem = pltpu.make_async_copy(pos_vmem, pos_smem, pos_sem)
    to_smem.start()
    to_smem.wait()

    def begin(slot, carry):
        pltpu.make_async_copy(blocks_ref.at[slot], send_ref.at[pos_smem[0, slot]], sem).start()
        return carry

    lax.fori_loop(0, count, begin, 0)

    valid = lax.broadcasted_iota(I32, (1, SLOTS), 1) < count
    owners = lax.broadcasted_iota(I32, (N_VEC, SLOTS), 0)
    lane = lax.broadcasted_iota(I32, (N_VEC, BLK), 1)
    mine = (owners == owner) & valid
    table = jnp.zeros((N_VEC, BLK), I32)
    for r in range(CAP):
        picked = jnp.sum(jnp.where(mine & (rank == r), code, 0), axis=1, keepdims=True)
        table = jnp.where(lane == r, picked, table)
    code_ref[...] = jnp.broadcast_to(table[:, None, :], (N_VEC, 8, BLK))

    pick = (lax.broadcasted_iota(I32, (NO, NO), 0) == order_ref[...]).astype(BF16)
    perm = jnp.dot(occ_ref[...], pick, preferred_element_type=F32)
    perm_ref[...] = perm.T.astype(BF16)
    for half in range(2):
        @pl.when(core == half)
        def _():
            for q in range(4):
                r = 4 * half + q
                w_ref[:, 256 * q:256 * q + 256] = vir_ref[:, NV_R * r:NV_R * r + 256]
                tail = vir_ref[:, NV_R * r + 256:NV_R * r + NV_R].astype(F32)
                occ = perm[:, NO_R * r:NO_R * r + NO_R]
                zero = jnp.zeros((SPAN, 12), F32)
                w_ref[:, 1024 + 128 * q:1152 + 128 * q] = jnp.concatenate([tail, occ, zero], axis=1).astype(BF16)

    def end(slot, carry):
        pltpu.make_async_copy(blocks_ref.at[0], send_ref.at[0], sem).wait()
        return carry

    lax.fori_loop(0, count, end, 0)


def prepare(vectors, pairs, count, order, occ, vir, blocks):
    return pl.pallas_call(
        prepare_kernel,
        out_shape=(
            jax.ShapeDtypeStruct((N_VEC * CAP, BLK, BLK), BF16),
            jax.ShapeDtypeStruct((N_VEC, 8, BLK), I32),
            jax.ShapeDtypeStruct((SPAN, WIDE), BF16),
            jax.ShapeDtypeStruct((NO, SPAN), BF16),
        ),
        in_specs=[IN_VMEM, IN_VMEM, pl.BlockSpec(memory_space=pltpu.SMEM), IN_VMEM, IN_VMEM, IN_VMEM, ANY],
        out_specs=(ANY, IN_VMEM, IN_VMEM, IN_VMEM),
        scratch_shapes=[VMEM((1, SLOTS), I32), pltpu.SMEM((1, SLOTS), I32), DMA, DMA],
        compiler_params=pltpu.CompilerParams(vmem_limit_bytes=40 * 2**20),
        name="prepare",
    )(vectors, pairs, count, order, occ, vir, blocks)


def exchange_kernel(send, code, w, recv, rcode, wfull, lsem, tsend, trecv, csend, crecv, us, ur, ds, dr):
    v, z = lax.axis_index("vec"), lax.axis_index("row")
    core, x, y = lax.rem(v, 2), lax.rem(v // 2, 4), v // 8
    up, down = lax.rem(z + 1, N_ROW), lax.rem(z + N_ROW - 1, N_ROW)
    barrier = pltpu.get_barrier_semaphore()

    def greet(i, carry):
        pl.semaphore_signal(barrier, inc=1, device_id=(lax.rem(v + i, N_VEC), z), device_id_type=MESH)
        return carry

    lax.fori_loop(1, N_VEC, greet, 0)
    pl.semaphore_signal(barrier, inc=1, device_id=(v, up), device_id_type=MESH)
    pl.semaphore_signal(barrier, inc=1, device_id=(v, down), device_id_type=MESH)
    pl.semaphore_wait(barrier, N_VEC + 1)

    own = [
        pltpu.make_async_copy(send.at[v], recv.at[v], lsem.at[0]),
        pltpu.make_async_copy(code.at[v], rcode.at[v], lsem.at[1]),
        pltpu.make_async_copy(w, wfull.at[z], lsem.at[2]),
    ]
    for copy in own:
        copy.start()

    def remote(src, dst, send_sem, recv_sem, device):
        return pltpu.make_async_remote_copy(
            src_ref=src, dst_ref=dst, send_sem=send_sem, recv_sem=recv_sem, device_id=device, device_id_type=MESH
        )

    rows = SPAN // Q

    def ring(step, piece, sign):
        origin = lax.rem(z - sign * step + 2 * N_ROW, N_ROW)
        part = pl.ds(piece * rows, rows)
        src = w.at[part] if step == 0 else wfull.at[origin, part]
        ssem, rsem, to = (us, ur, up) if sign > 0 else (ds, dr, down)
        return remote(src, wfull.at[origin, part], ssem.at[step * Q + piece], rsem.at[step * Q + piece], (v, to))

    def pieces(step, sign):
        if step < 3:
            return 0, Q
        return (0, Q // 2) if sign > 0 else (Q // 2, Q)

    def first(piece, carry):
        ring(0, piece, 1).start()
        ring(0, piece, -1).start()
        return carry

    lax.fori_loop(0, Q, first, 0)

    def target(j):
        return ((y + j // 8) % 4) * 8 + ((x + j // 2) % 4) * 2 + lax.rem(core + j, 2)

    def give(n, carry):
        part = n // (N_VEC - 1)
        j = 1 + lax.rem(n * 11, N_VEC - 1)
        d = target(j)
        spot = pl.ds(part * (CAP // PARTS), CAP // PARTS)
        remote(send.at[d, spot], recv.at[v, spot], tsend.at[d], trecv.at[v], (d, z)).start()
        return carry

    def give_code(j, carry):
        d = target(j)
        remote(code.at[d], rcode.at[v], csend.at[d], crecv.at[v], (d, z)).start()
        return carry

    lax.fori_loop(0, PARTS * (N_VEC - 1), give, 0)
    lax.fori_loop(1, N_VEC, give_code, 0)

    for step in range(1, 4):
        for piece in range(Q):
            for sign in (1, -1):
                low, high = pieces(step, sign)
                if low <= piece < high:
                    ring(step - 1, piece, sign).wait_recv()
                    ring(step, piece, sign).start()

    def finish(i, carry):
        d = lax.rem(v + i, N_VEC)
        pltpu.make_async_copy(send.at[d], recv.at[d], tsend.at[d]).wait()
        pltpu.make_async_copy(code.at[d], rcode.at[d], csend.at[d]).wait()
        pltpu.make_async_copy(send.at[d], recv.at[d], trecv.at[d]).wait()
        pltpu.make_async_copy(code.at[d], rcode.at[d], crecv.at[d]).wait()
        return carry

    for sign in (1, -1):
        for step in range(4):
            low, high = pieces(step, sign)
            for piece in range(low, high):
                ring(step, piece, sign).wait_send()
        for step in (2, 3):
            low, high = pieces(step, sign)
            skip = pieces(3, sign) if step == 2 else (Q, Q)
            for piece in range(low, high):
                if not skip[0] <= piece < skip[1]:
                    ring(step, piece, sign).wait_recv()
    lax.fori_loop(1, N_VEC, finish, 0)
    for copy in own:
        copy.wait()


def exchange(send, code, w):
    return pl.pallas_call(
        exchange_kernel,
        out_shape=(
            jax.ShapeDtypeStruct(send.shape, BF16),
            jax.ShapeDtypeStruct(code.shape, I32),
            jax.ShapeDtypeStruct((N_ROW,) + w.shape, BF16),
        ),
        in_specs=[ANY] * 3,
        out_specs=(ANY,) * 3,
        scratch_shapes=[DMA((3,))] + [DMA((N_VEC,))] * 4 + [DMA((4 * Q,))] * 4,
        compiler_params=pltpu.CompilerParams(collective_id=0, has_side_effects=True),
        name="exchange",
    )(send, code, w)


def half_kernel(code_ref, tiles_ref, occ_ref, out_ref, tiles, dense, occ, sems):
    group = 32
    loads = [
        pltpu.make_async_copy(
            tiles_ref.at[pl.ds(n * group, group)], tiles.at[pl.ds(n * group, group)], sems.at[n]
        )
        for n in range(SLOTS // group)
    ]
    for load in loads:
        load.start()

    def clear(n, carry):
        dense[n] = jnp.zeros((BLK, NAO), F32)
        return carry

    lax.fori_loop(0, VEC_DEV * TALL, clear, 0)
    for r in range(N_ROW):
        occ[:, SPAN * r:SPAN * r + SPAN] = occ_ref[r]

    def place(n, carry):
        code = code_ref[n] - 1

        @pl.when(code >= 0)
        def _():
            block = code // ACROSS
            column = pl.ds(pl.multiple_of(lax.rem(code, ACROSS) * BLK, BLK), BLK)
            dense[block, :, column] += tiles[n].astype(F32)

        return carry

    for n, load in enumerate(loads):
        load.wait()
        lax.fori_loop(n * group, n * group + group, place, 0)

    for pair in range(VEC_DEV * TALL // 2):
        rows = jnp.concatenate([dense[2 * pair], dense[2 * pair + 1]], axis=0).astype(BF16)
        product = lax.dot_general(
            occ[...], rows, (((1,), (1,)), ((), ())), preferred_element_type=F32
        ).astype(BF16)
        for n in range(2):
            j, block = divmod(2 * pair + n, TALL)
            out_ref[j, :, BLK * block:BLK * block + BLK] = product[:, BLK * n:BLK * n + BLK]


def half_transform(code, tiles, occ):
    return pl.pallas_call(
        half_kernel,
        out_shape=jax.ShapeDtypeStruct((VEC_DEV, NO, SPAN), BF16),
        in_specs=[pl.BlockSpec(memory_space=pltpu.SMEM), ANY, IN_VMEM],
        out_specs=IN_VMEM,
        scratch_shapes=[
            VMEM((SLOTS, BLK, BLK), BF16),
            VMEM((VEC_DEV * TALL, BLK, NAO), F32),
            VMEM((NO, NAO), BF16),
            DMA((SLOTS // 32,)),
        ],
        compiler_params=pltpu.CompilerParams(vmem_limit_bytes=56 * 2**20),
        name="half",
    )(code, tiles, occ)


def finish_kernel(half, w_hbm, out_ref, w, held, total, chunk, taken, wide, wsem, lsem, hsend, hrecv, ssend, srecv, csend, crecv):
    v, z = lax.axis_index("vec"), lax.axis_index("row")
    chip, core = v // 2, lax.rem(v, 2)
    giver = z // 4
    takes_own = giver == core
    other = 2 * chip + 1 - core

    loads = [pltpu.make_async_copy(w_hbm.at[r], w.at[r], wsem.at[r]) for r in range(N_ROW)]
    for load in loads:
        load.start()

    barrier = pltpu.get_barrier_semaphore()

    def greet(device):
        pl.semaphore_signal(barrier, inc=1, device_id=device, device_id_type=MESH)

    def greet_sources(n, carry):
        source = (2 * (n // N_ROW) + giver, lax.rem(n, N_ROW))

        @pl.when(jnp.logical_not((source[0] == v) & (source[1] == z)))
        def _():
            greet(source)

        return carry

    lax.fori_loop(0, N_CHIP * N_ROW, greet_sources, 0)

    def greet_halves(r, carry):
        @pl.when(jnp.logical_not(takes_own & (r == z)))
        def _():
            greet((2 * chip + giver, r))

        return carry

    lax.fori_loop(0, N_ROW, greet_halves, 0)
    greet((other, z))
    expected = 8 + 1 + 4 * N_VEC - 2 * takes_own.astype(I32)
    pl.semaphore_wait(barrier, expected)

    def remote(src, dst, send_sem, recv_sem, device):
        return pltpu.make_async_remote_copy(
            src_ref=src, dst_ref=dst, send_sem=send_sem, recv_sem=recv_sem, device_id=device, device_id_type=MESH
        )

    def rows(h):
        return pl.ds(pl.multiple_of(h * K_HALF, 16), K_HALF)

    def send_half(n):
        j, h = n // 2, lax.rem(n, 2)
        return remote(half.at[j, rows(h)], held.at[z, rows(h)], hsend.at[n], hrecv.at[z], (2 * chip + h, 4 * core + j))

    def to_self(n):
        return (4 * core + n // 2 == z) & (lax.rem(n, 2) == core)

    stay = pltpu.make_async_copy(half.at[lax.rem(z, 4), rows(core)], held.at[z, rows(core)], lsem.at[0])

    def start_half(n, carry):
        @pl.when(jnp.logical_not(to_self(n)))
        def _():
            send_half(n).start()

        return carry

    lax.fori_loop(0, 8, start_half, 0)

    @pl.when(takes_own)
    def _():
        stay.start()

    def swap(r):
        return remote(held.at[r, rows(core)], held.at[r, rows(core)], ssend.at[r], srecv.at[r], (other, z))

    def pass_on(i):
        r = lax.rem(z + i, N_ROW)
        if i == 0:
            @pl.when(takes_own)
            def _():
                stay.wait()

            @pl.when(jnp.logical_not(takes_own))
            def _():
                pltpu.make_async_copy(held.at[r, rows(core)], held.at[r, rows(core)], hrecv.at[r]).wait()
        else:
            pltpu.make_async_copy(held.at[r, rows(core)], held.at[r, rows(core)], hrecv.at[r]).wait()
        swap(r).start()

    def arrived(i):
        r = lax.rem(z + i, N_ROW)
        theirs = held.at[r, rows(1 - core)]
        pltpu.make_async_copy(theirs, theirs, srecv.at[r]).wait()
        return r

    sequence = (0, 1, 7, 2, 6, 3, 5, 4)
    for load in loads:
        load.wait()
    for n in range(4):
        first, second = sequence[2 * n], sequence[2 * n + 1]
        pass_on(first)
        pass_on(second)
        a, b = arrived(first), arrived(second)
        deep = jnp.concatenate([held[a], held[b]], axis=1)
        for col in range(0, WIDE, 512):
            part = pl.ds(col, 512)
            block = jnp.concatenate([w[a, :, part], w[b, :, part]], axis=0)
            product = jnp.dot(deep, block, preferred_element_type=F32)
            if n == 0:
                total[:, part] = product
            else:
                total[:, part] += product

    row = lax.broadcasted_iota(I32, (N_VEC * CHUNK, NO), 0)
    source = lax.broadcasted_iota(I32, (N_VEC * CHUNK, NO), 1)
    inside = row % CHUNK
    base = row // CHUNK * NO_V
    stacked = jnp.zeros((N_VEC * CHUNK, 4 * BLK), F32)
    for t in range(3):
        pick = ((inside // NO_V == t) & (base + inside % NO_V == source)).astype(BF16)
        if t < 2:
            columns = jnp.concatenate([total[:, 256 * q + 128 * t:256 * q + 128 * t + 128] for q in range(4)], axis=1)
        else:
            columns = total[:, 1024:1536]
        stacked = stacked + jnp.dot(pick, columns.astype(BF16), preferred_element_type=F32)
    chunk[...] = stacked.astype(BF16)

    place = chip * N_ROW + z

    def final_copy(n):
        to, q = n // 4, lax.rem(n, 4)
        src = chunk.at[pl.ds(pl.multiple_of(to * CHUNK, CHUNK), CHUNK), pl.ds(pl.multiple_of(q * BLK, BLK), BLK)]
        dst = taken.at[pl.ds(pl.multiple_of(place * CHUNK, CHUNK), CHUNK)]
        return src, dst, (to, 4 * core + q)

    def start_final(i, carry):
        n = lax.rem(i * 37 + v * 4, 4 * N_VEC)
        src, dst, device = final_copy(n)
        own = (device[0] == v) & (device[1] == z)

        @pl.when(jnp.logical_not(own))
        def _():
            remote(src, dst, csend, crecv, device).start()

        @pl.when(own)
        def _():
            pltpu.make_async_copy(src, dst, lsem.at[1]).start()

        return carry

    lax.fori_loop(0, 4 * N_VEC, start_final, 0)

    def wait_half(n, carry):
        @pl.when(jnp.logical_not(to_self(n)))
        def _():
            send_half(n).wait_send()

        return carry

    lax.fori_loop(0, 8, wait_half, 0)

    def wait_swap(r, carry):
        swap(r).wait_send()
        return carry

    lax.fori_loop(0, N_ROW, wait_swap, 0)

    def wait_chunks(count):
        part = taken.at[pl.ds(0, count * CHUNK)]
        pltpu.make_async_copy(part, part, crecv).wait()
        pltpu.make_async_copy(part, part, csend).wait()

    @pl.when(takes_own)
    def _():
        wait_chunks(4 * N_VEC - 1)
        part = taken.at[pl.ds(0, CHUNK)]
        pltpu.make_async_copy(part, part, lsem.at[1]).wait()

    @pl.when(jnp.logical_not(takes_own))
    def _():
        wait_chunks(4 * N_VEC)

    wide[...] = taken[...].astype(F32)
    for t in range(3):
        for k in range(NO_V):
            block = wide[pl.ds(NO_V * t + k, BLK, stride=CHUNK), :]
            out_ref[k, BLK * t:BLK * t + BLK, :] = block.T.astype(BF16)


def finish(half, w):
    return pl.pallas_call(
        finish_kernel,
        out_shape=jax.ShapeDtypeStruct((NO_V, W_R, BLK), BF16),
        in_specs=[IN_VMEM, ANY],
        out_specs=IN_VMEM,
        scratch_shapes=[
            VMEM((N_ROW, SPAN, WIDE), BF16),
            VMEM((N_ROW, NO, SPAN), BF16),
            VMEM((NO, WIDE), F32),
            VMEM((N_VEC * CHUNK, 4 * BLK), BF16),
            VMEM((BLK * CHUNK, BLK), BF16),
            VMEM((BLK * CHUNK, BLK), F32),
            DMA((N_ROW,)),
            DMA((2,)),
            DMA((8,)),
            DMA((N_ROW,)),
            DMA((N_ROW,)),
            DMA((N_ROW,)),
            DMA,
            DMA,
        ],
        compiler_params=pltpu.CompilerParams(
            collective_id=1, has_side_effects=True, vmem_limit_bytes=48 * 2**20
        ),
        name="finish",
    )(half, w)


def on_device(blocks, block_vector, block_pair, block_count, occ_order, occ_coeffs, vir_coeffs):
    send, code, w, perm = prepare(
        block_vector, block_pair, block_count, occ_order.reshape(1, NO), occ_coeffs, vir_coeffs, blocks
    )
    occ = lax.all_gather(perm, "row", axis=0)
    tiles, codes, w_all = exchange(send.reshape(N_VEC, CAP, BLK, BLK), code, w)
    half = half_transform(codes[:, 0, :CAP].reshape(-1), tiles.reshape(SLOTS, BLK, BLK), occ)
    result = finish(half, w_all)
    return (
        result[:, :NV_R].transpose(1, 0, 2),
        result[:, NV_R:NV_R + NO_R].transpose(1, 0, 2),
    )


def solution(mesh):
    placed = (
        P("vec", "row", None),
        P("row", "vec"),
        P("row", "vec"),
        P("row", "vec"),
        P(),
        P("row", None),
        P("row", None),
    )
    return jax.shard_map(
        on_device,
        mesh=mesh,
        in_specs=placed,
        out_specs=(P("row", "vec", None), P("row", "vec", None)),
        check_vma=False,
    )
```

```python
import jax
import jax.numpy as jnp
from jax import lax
from jax.experimental import pallas as pl
from jax.experimental.pallas import tpu as pltpu
from jax.sharding import PartitionSpec as P

MESH = pl.DeviceIdType.MESH
F32, BF16, I32 = jnp.float32, jnp.bfloat16, jnp.int32

N_VEC, N_ROW, N_CHIP = 32, 8, 16
CAP, SLOTS, BLK = 8, 256, 128
NAO, NO, NV, SPAN = 3072, 288, 2688, 384
VEC_DEV, PAIRS, ACROSS, TALL = 4, 72, 24, 3
NV_R, NO_R, NO_V = NV // N_ROW, NO // N_ROW, NO // N_VEC
W_R = 384
WIDE = 4 * W_R
K_HALF = NO // 2
CHUNK = 32
PARTS = 8
Q = 8
VMEM = pltpu.VMEM
LIMIT = 60 * 2**20
ANY = pl.BlockSpec(memory_space=pl.ANY)
IN_VMEM = pl.BlockSpec(memory_space=pltpu.VMEM)
DMA = pltpu.SemaphoreType.DMA


def prepare_kernel(vec_hbm, pair_hbm, count_ref, order_hbm, occ_hbm, vir_hbm, blocks_ref,
                   send_ref, code_hbm, w_hbm, vec_ref, pair_ref, order_ref, occ_ref, vir_ref,
                   code_ref, w_ref, pos_vmem, pos_smem, sem, pos_sem, in_sems, out_sems):
    loads = [
        pltpu.make_async_copy(src, dst, in_sems.at[n])
        for n, (src, dst) in enumerate(
            ((vec_hbm, vec_ref), (pair_hbm, pair_ref), (order_hbm, order_ref), (occ_hbm, occ_ref), (vir_hbm, vir_ref))
        )
    ]
    for load in loads:
        load.start()
    core = lax.rem(lax.axis_index("vec"), 2)
    count = count_ref[0, 0]
    loads[0].wait()
    vectors = vec_ref[...]
    owner = vectors // VEC_DEV
    above = lax.broadcasted_iota(I32, (SLOTS, SLOTS), 0)
    across = lax.broadcasted_iota(I32, (SLOTS, SLOTS), 1)
    owner_col = jnp.sum(jnp.where(above == across, owner, 0), axis=1, keepdims=True)
    earlier = (owner_col == owner) & (above < across)
    rank = jnp.sum(jnp.where(earlier, 1, 0), axis=0, keepdims=True)
    pos_vmem[...] = owner * CAP + rank
    to_smem = pltpu.make_async_copy(pos_vmem, pos_smem, pos_sem)
    to_smem.start()
    to_smem.wait()

    def begin(slot, carry):
        pltpu.make_async_copy(blocks_ref.at[slot], send_ref.at[pos_smem[0, slot]], sem).start()
        return carry

    lax.fori_loop(0, count, begin, 0)

    loads[1].wait()
    code = vectors % VEC_DEV * PAIRS + pair_ref[...] + 1
    valid = lax.broadcasted_iota(I32, (1, SLOTS), 1) < count
    owners = lax.broadcasted_iota(I32, (N_VEC, SLOTS), 0)
    lane = lax.broadcasted_iota(I32, (N_VEC, BLK), 1)
    mine = (owners == owner) & valid
    table = jnp.zeros((N_VEC, BLK), I32)
    for r in range(CAP):
        picked = jnp.sum(jnp.where(mine & (rank == r), code, 0), axis=1, keepdims=True)
        table = jnp.where(lane == r, picked, table)
    code_ref[...] = jnp.broadcast_to(table[:, None, :], (N_VEC, 8, BLK))
    code_out = pltpu.make_async_copy(code_ref, code_hbm, out_sems.at[0])
    code_out.start()

    for load in loads[2:]:
        load.wait()
    pick = (lax.broadcasted_iota(I32, (NO, NO), 0) == order_ref[...]).astype(BF16)
    perm = lax.dot_general(occ_ref[...], pick, (((0,), (0,)), ((), ())), preferred_element_type=F32)
    for half in range(2):
        @pl.when(core == half)
        def _():
            for q in range(4):
                r = 4 * half + q
                w_ref[:, 256 * q:256 * q + 256] = vir_ref[:, NV_R * r:NV_R * r + 256]
                tail = vir_ref[:, NV_R * r + 256:NV_R * r + NV_R].astype(F32)
                occ = perm[:, NO_R * r:NO_R * r + NO_R]
                zero = jnp.zeros((SPAN, 12), F32)
                w_ref[:, 1024 + 128 * q:1152 + 128 * q] = jnp.concatenate([tail, occ, zero], axis=1).astype(BF16)
    w_out = pltpu.make_async_copy(w_ref, w_hbm, out_sems.at[1])
    w_out.start()

    def end(slot, carry):
        pltpu.make_async_copy(blocks_ref.at[0], send_ref.at[0], sem).wait()
        return carry

    lax.fori_loop(0, count, end, 0)
    code_out.wait()
    w_out.wait()


def prepare(vectors, pairs, count, order, occ, vir, blocks):
    return pl.pallas_call(
        prepare_kernel,
        out_shape=(
            jax.ShapeDtypeStruct((N_VEC * CAP, BLK, BLK), BF16),
            jax.ShapeDtypeStruct((N_VEC, 8, BLK), I32),
            jax.ShapeDtypeStruct((SPAN, WIDE), BF16),
        ),
        in_specs=[ANY, ANY, pl.BlockSpec(memory_space=pltpu.SMEM), ANY, ANY, ANY, ANY],
        out_specs=(ANY, ANY, ANY),
        scratch_shapes=[
            VMEM((1, SLOTS), I32),
            VMEM((1, SLOTS), I32),
            VMEM((1, NO), I32),
            VMEM((NO, SPAN), BF16),
            VMEM((SPAN, NV), BF16),
            VMEM((N_VEC, 8, BLK), I32),
            VMEM((SPAN, WIDE), BF16),
            VMEM((1, SLOTS), I32),
            pltpu.SMEM((1, SLOTS), I32),
            DMA,
            DMA,
            DMA((5,)),
            DMA((2,)),
        ],
        compiler_params=pltpu.CompilerParams(vmem_limit_bytes=LIMIT),
        name="prepare",
    )(vectors, pairs, count, order, occ, vir, blocks)


def exchange_kernel(send, code, w, recv, rcode, wfull, theirs, lsem, tsend, trecv, csend, crecv, us, ur, ds, dr, os, orc):
    v, z = lax.axis_index("vec"), lax.axis_index("row")
    core, x, y = lax.rem(v, 2), lax.rem(v // 2, 4), v // 8
    up, down = lax.rem(z + 1, N_ROW), lax.rem(z + N_ROW - 1, N_ROW)
    barrier = pltpu.get_barrier_semaphore()

    def greet(i, carry):
        pl.semaphore_signal(barrier, inc=1, device_id=(lax.rem(v + i, N_VEC), z), device_id_type=MESH)
        return carry

    lax.fori_loop(1, N_VEC, greet, 0)
    pl.semaphore_signal(barrier, inc=1, device_id=(v, up), device_id_type=MESH)
    pl.semaphore_signal(barrier, inc=1, device_id=(v, down), device_id_type=MESH)
    pl.semaphore_wait(barrier, N_VEC + 1)

    own = [
        pltpu.make_async_copy(send.at[v], recv.at[v], lsem.at[0]),
        pltpu.make_async_copy(code.at[v], rcode.at[v], lsem.at[1]),
        pltpu.make_async_copy(w, wfull.at[z], lsem.at[2]),
    ]
    for copy in own:
        copy.start()

    def remote(src, dst, send_sem, recv_sem, device):
        return pltpu.make_async_remote_copy(
            src_ref=src, dst_ref=dst, send_sem=send_sem, recv_sem=recv_sem, device_id=device, device_id_type=MESH
        )

    def swap(origin, src):
        columns = pl.ds(1024, 512)
        return remote(src.at[:, columns], theirs.at[origin], os.at[origin], orc.at[origin], (v + 1 - 2 * core, z))

    rows = SPAN // Q

    def ring(step, piece, sign):
        origin = lax.rem(z - sign * step + 2 * N_ROW, N_ROW)
        part = pl.ds(piece * rows, rows)
        src = w.at[part] if step == 0 else wfull.at[origin, part]
        ssem, rsem, to = (us, ur, up) if sign > 0 else (ds, dr, down)
        return remote(src, wfull.at[origin, part], ssem.at[step * Q + piece], rsem.at[step * Q + piece], (v, to))

    def pieces(step, sign):
        if step < 3:
            return 0, Q
        return (0, Q // 2) if sign > 0 else (Q // 2, Q)

    def first(piece, carry):
        ring(0, piece, 1).start()
        ring(0, piece, -1).start()
        return carry

    lax.fori_loop(0, Q, first, 0)
    swap(z, w).start()

    def target(j):
        return ((y + j // 8) % 4) * 8 + ((x + j // 2) % 4) * 2 + lax.rem(core + j, 2)

    def give(n, carry):
        part = n // (N_VEC - 1)
        j = 1 + lax.rem(n * 11, N_VEC - 1)
        d = target(j)
        spot = pl.ds(part * (CAP // PARTS), CAP // PARTS)
        remote(send.at[d, spot], recv.at[v, spot], tsend.at[d], trecv.at[v], (d, z)).start()
        return carry

    def give_code(j, carry):
        d = target(j)
        remote(code.at[d], rcode.at[v], csend.at[d], crecv.at[v], (d, z)).start()
        return carry

    lax.fori_loop(0, PARTS * (N_VEC - 1), give, 0)
    lax.fori_loop(1, N_VEC, give_code, 0)

    def pass_occ(step, sign):
        origin = lax.rem(z - sign * step + N_ROW, N_ROW)
        swap(origin, wfull.at[origin]).start()

    for step in range(1, 4):
        for piece in range(Q):
            for sign in (1, -1):
                low, high = pieces(step, sign)
                if low <= piece < high:
                    ring(step - 1, piece, sign).wait_recv()
                    ring(step, piece, sign).start()
        if step < 3:
            pass_occ(step, 1)
            pass_occ(step, -1)

    def finish(i, carry):
        d = lax.rem(v + i, N_VEC)
        pltpu.make_async_copy(send.at[d], recv.at[d], tsend.at[d]).wait()
        pltpu.make_async_copy(code.at[d], rcode.at[d], csend.at[d]).wait()
        pltpu.make_async_copy(send.at[d], recv.at[d], trecv.at[d]).wait()
        pltpu.make_async_copy(code.at[d], rcode.at[d], crecv.at[d]).wait()
        return carry

    for sign in (1, -1):
        low, high = pieces(3, sign)
        for piece in range(Q):
            if not low <= piece < high:
                ring(2, piece, sign).wait_recv()
        pass_occ(3, sign)
    for sign in (1, -1):
        low, high = pieces(3, sign)
        for piece in range(low, high):
            ring(3, piece, sign).wait_recv()
    pass_occ(4, 1)
    for sign in (1, -1):
        for step in range(4):
            low, high = pieces(step, sign)
            for piece in range(low, high):
                ring(step, piece, sign).wait_send()
    for origin in range(N_ROW):
        pltpu.make_async_copy(theirs.at[origin], theirs.at[origin], os.at[origin]).wait()
        pltpu.make_async_copy(theirs.at[origin], theirs.at[origin], orc.at[origin]).wait()
    lax.fori_loop(1, N_VEC, finish, 0)
    for copy in own:
        copy.wait()


def exchange(send, code, w):
    return pl.pallas_call(
        exchange_kernel,
        out_shape=(
            jax.ShapeDtypeStruct(send.shape, BF16),
            jax.ShapeDtypeStruct(code.shape, I32),
            jax.ShapeDtypeStruct((N_ROW,) + w.shape, BF16),
            jax.ShapeDtypeStruct((N_ROW, SPAN, 512), BF16),
        ),
        in_specs=[ANY] * 3,
        out_specs=(ANY,) * 4,
        scratch_shapes=[DMA((3,))] + [DMA((N_VEC,))] * 4 + [DMA((4 * Q,))] * 4 + [DMA((N_ROW,))] * 2,
        compiler_params=pltpu.CompilerParams(collective_id=0, has_side_effects=True, vmem_limit_bytes=LIMIT),
        name="exchange",
    )(send, code, w)


def half_kernel(code_hbm, tiles_ref, w_hbm, theirs_hbm, out_ref, tiles, dense, occ, own, theirs, code_ref, sems, more):
    group = 32
    core = lax.rem(lax.axis_index("vec"), 2)
    others = [
        pltpu.make_async_copy(code_hbm, code_ref, more.at[0]),
        pltpu.make_async_copy(w_hbm.at[:, :, pl.ds(1024, 512)], own, more.at[1]),
        pltpu.make_async_copy(theirs_hbm, theirs, more.at[2]),
    ]
    for load in others:
        load.start()
    loads = [
        pltpu.make_async_copy(
            tiles_ref.at[pl.ds(n * group, group)], tiles.at[pl.ds(n * group, group)], sems.at[n]
        )
        for n in range(SLOTS // group)
    ]
    for load in loads:
        load.start()

    def clear(n, carry):
        dense[n] = jnp.zeros((BLK, NAO), F32)
        return carry

    lax.fori_loop(0, VEC_DEV * TALL, clear, 0)
    for load in others:
        load.wait()
    index = lax.broadcasted_iota(I32, (NO, 512), 0)
    column = lax.broadcasted_iota(I32, (NO, 512), 1)
    lane = column % BLK - (NV_R - 256)
    found = (lane >= 0) & (lane < NO_R)
    wanted = index - NO_R * (column // BLK) - lane
    pick_own = (found & (wanted == 4 * NO_R * core)).astype(BF16)
    pick_theirs = (found & (wanted == 4 * NO_R * (1 - core))).astype(BF16)
    across = (((1,), (1,)), ((), ()))
    for r in range(N_ROW):
        occ[:, SPAN * r:SPAN * r + SPAN] = (
            lax.dot_general(pick_own, own[r], across, preferred_element_type=F32)
            + lax.dot_general(pick_theirs, theirs[r], across, preferred_element_type=F32)
        ).astype(BF16)

    def place(n, carry):
        code = code_ref[n // CAP, 0, lax.rem(n, CAP)] - 1

        @pl.when(code >= 0)
        def _():
            block = code // ACROSS
            column = pl.ds(pl.multiple_of(lax.rem(code, ACROSS) * BLK, BLK), BLK)
            dense[block, :, column] += tiles[n].astype(F32)

        return carry

    for n, load in enumerate(loads):
        load.wait()
        lax.fori_loop(n * group, n * group + group, place, 0)

    for pair in range(VEC_DEV * TALL // 2):
        rows = jnp.concatenate([dense[2 * pair], dense[2 * pair + 1]], axis=0).astype(BF16)
        product = lax.dot_general(
            occ[...], rows, (((1,), (1,)), ((), ())), preferred_element_type=F32
        ).astype(BF16)
        for n in range(2):
            j, block = divmod(2 * pair + n, TALL)
            out_ref[j, :, BLK * block:BLK * block + BLK] = product[:, BLK * n:BLK * n + BLK]


def half_transform(code, tiles, w, theirs):
    return pl.pallas_call(
        half_kernel,
        out_shape=jax.ShapeDtypeStruct((VEC_DEV, NO, SPAN), BF16),
        in_specs=[ANY] * 4,
        out_specs=IN_VMEM,
        scratch_shapes=[
            VMEM((SLOTS, BLK, BLK), BF16),
            VMEM((VEC_DEV * TALL, BLK, NAO), F32),
            VMEM((NO, NAO), BF16),
            VMEM((N_ROW, SPAN, 512), BF16),
            VMEM((N_ROW, SPAN, 512), BF16),
            pltpu.SMEM((N_VEC, 8, BLK), I32),
            DMA((SLOTS // 32,)),
            DMA((3,)),
        ],
        compiler_params=pltpu.CompilerParams(vmem_limit_bytes=LIMIT),
        name="half",
    )(code, tiles, w, theirs)


def finish_kernel(half, w_hbm, out_ref, w, held, total, chunk, taken, wide, wsem, lsem, hsend, hrecv, ssend, srecv, csend, crecv, x_sem, y_sem):
    v, z = lax.axis_index("vec"), lax.axis_index("row")
    chip, core = v // 2, lax.rem(v, 2)
    giver = z // 4
    takes_own = giver == core
    other = 2 * chip + 1 - core

    loads = [pltpu.make_async_copy(w_hbm.at[r], w.at[r], wsem.at[r]) for r in range(N_ROW)]
    for load in loads:
        load.start()

    barrier = pltpu.get_barrier_semaphore()

    def greet(device):
        pl.semaphore_signal(barrier, inc=1, device_id=device, device_id_type=MESH)

    x, y = lax.rem(chip, 4), chip // 4

    def line(i, carry):
        greet((v, lax.rem(z + i, N_ROW)))
        return carry

    def other_line(i, carry):
        greet((other, lax.rem(z + i, N_ROW)))
        return carry

    def along_x(i):
        return (y * 8 + lax.rem(x + i, 4) * 2 + core, z)

    def along_y(i):
        return (lax.rem(y + i, 4) * 8 + x * 2 + core, z)

    lax.fori_loop(1, N_ROW, line, 0)
    lax.fori_loop(0, N_ROW, other_line, 0)
    for i in range(1, 4):
        greet(along_x(i))
        greet(along_y(i))
    pl.semaphore_wait(barrier, 7 + 8 + 6)
    for i in range(1, 4):
        pl.semaphore_signal(x_sem, inc=1, device_id=along_x(i), device_id_type=MESH)

    def remote(src, dst, send_sem, recv_sem, device):
        return pltpu.make_async_remote_copy(
            src_ref=src, dst_ref=dst, send_sem=send_sem, recv_sem=recv_sem, device_id=device, device_id_type=MESH
        )

    def rows(h):
        return pl.ds(pl.multiple_of(h * K_HALF, 16), K_HALF)

    def send_half(n):
        j, h = n // 2, lax.rem(n, 2)
        return remote(half.at[j, rows(h)], held.at[z, rows(h)], hsend.at[n], hrecv.at[z], (2 * chip + h, 4 * core + j))

    def to_self(n):
        return (4 * core + n // 2 == z) & (lax.rem(n, 2) == core)

    stay = pltpu.make_async_copy(half.at[lax.rem(z, 4), rows(core)], held.at[z, rows(core)], lsem.at[0])

    def start_half(n, carry):
        @pl.when(jnp.logical_not(to_self(n)))
        def _():
            send_half(n).start()

        return carry

    lax.fori_loop(0, 8, start_half, 0)

    @pl.when(takes_own)
    def _():
        stay.start()

    def swap(r):
        return remote(held.at[r, rows(core)], held.at[r, rows(core)], ssend.at[r], srecv.at[r], (other, z))

    def pass_on(i):
        r = lax.rem(z + i, N_ROW)
        if i == 0:
            @pl.when(takes_own)
            def _():
                stay.wait()

            @pl.when(jnp.logical_not(takes_own))
            def _():
                pltpu.make_async_copy(held.at[r, rows(core)], held.at[r, rows(core)], hrecv.at[r]).wait()
        else:
            pltpu.make_async_copy(held.at[r, rows(core)], held.at[r, rows(core)], hrecv.at[r]).wait()
        swap(r).start()

    def arrived(i):
        r = lax.rem(z + i, N_ROW)
        theirs = held.at[r, rows(1 - core)]
        pltpu.make_async_copy(theirs, theirs, srecv.at[r]).wait()
        return r

    pl.semaphore_wait(x_sem, 3)
    for i in range(1, 4):
        pl.semaphore_signal(y_sem, inc=1, device_id=along_y(i), device_id_type=MESH)

    sequence = (0, 1, 7, 2, 6, 3, 5, 4)
    for load in loads:
        load.wait()
    for n in range(4):
        first, second = sequence[2 * n], sequence[2 * n + 1]
        pass_on(first)
        pass_on(second)
        a, b = arrived(first), arrived(second)
        deep = jnp.concatenate([held[a], held[b]], axis=1)
        for col in range(0, WIDE, 512):
            part = pl.ds(col, 512)
            block = jnp.concatenate([w[a, :, part], w[b, :, part]], axis=0)
            product = jnp.dot(deep, block, preferred_element_type=F32)
            if n == 0:
                total[:, part] = product
            else:
                total[:, part] += product

    row = lax.broadcasted_iota(I32, (N_VEC * CHUNK, NO), 0)
    source = lax.broadcasted_iota(I32, (N_VEC * CHUNK, NO), 1)
    inside = row % CHUNK
    base = row // CHUNK * NO_V
    stacked = jnp.zeros((N_VEC * CHUNK, 4 * BLK), F32)
    for t in range(3):
        pick = ((inside // NO_V == t) & (base + inside % NO_V == source)).astype(BF16)
        if t < 2:
            columns = jnp.concatenate([total[:, 256 * q + 128 * t:256 * q + 128 * t + 128] for q in range(4)], axis=1)
        else:
            columns = total[:, 1024:1536]
        stacked = stacked + jnp.dot(pick, columns.astype(BF16), preferred_element_type=F32)
    for q in range(4):
        chunk[q] = stacked[:, BLK * q:BLK * q + BLK].astype(BF16)
    pl.semaphore_wait(y_sem, 3)

    place = chip * N_ROW + z

    def final_copy(n):
        to, q = n // 4, lax.rem(n, 4)
        src = chunk.at[q, pl.ds(pl.multiple_of(to * CHUNK, CHUNK), CHUNK)]
        dst = taken.at[pl.ds(pl.multiple_of(place * CHUNK, CHUNK), CHUNK)]
        return src, dst, (to, 4 * core + q)

    def start_final(i, carry):
        n = lax.rem(i * 37 + v * 4, 4 * N_VEC)
        src, dst, device = final_copy(n)
        own = (device[0] == v) & (device[1] == z)

        @pl.when(jnp.logical_not(own))
        def _():
            remote(src, dst, csend, crecv, device).start()

        @pl.when(own)
        def _():
            pltpu.make_async_copy(src, dst, lsem.at[1]).start()

        return carry

    lax.fori_loop(0, 4 * N_VEC, start_final, 0)

    def wait_half(n, carry):
        @pl.when(jnp.logical_not(to_self(n)))
        def _():
            send_half(n).wait_send()

        return carry

    lax.fori_loop(0, 8, wait_half, 0)

    def wait_swap(r, carry):
        swap(r).wait_send()
        return carry

    lax.fori_loop(0, N_ROW, wait_swap, 0)

    def wait_chunks(count):
        part = taken.at[pl.ds(0, count * CHUNK)]
        pltpu.make_async_copy(part, part, crecv).wait()
        pltpu.make_async_copy(part, part, csend).wait()

    @pl.when(takes_own)
    def _():
        wait_chunks(4 * N_VEC - 1)
        part = taken.at[pl.ds(0, CHUNK)]
        pltpu.make_async_copy(part, part, lsem.at[1]).wait()

    @pl.when(jnp.logical_not(takes_own))
    def _():
        wait_chunks(4 * N_VEC)

    wide[...] = taken[...].astype(F32)
    for t in range(3):
        for k in range(NO_V):
            block = wide[pl.ds(NO_V * t + k, BLK, stride=CHUNK), :]
            out_ref[k, BLK * t:BLK * t + BLK, :] = block.T.astype(BF16)


def finish(half, w):
    return pl.pallas_call(
        finish_kernel,
        out_shape=jax.ShapeDtypeStruct((NO_V, W_R, BLK), BF16),
        in_specs=[ANY, ANY],
        out_specs=IN_VMEM,
        scratch_shapes=[
            VMEM((N_ROW, SPAN, WIDE), BF16),
            VMEM((N_ROW, NO, SPAN), BF16),
            VMEM((NO, WIDE), F32),
            VMEM((4, N_VEC * CHUNK, BLK), BF16),
            VMEM((BLK * CHUNK, BLK), BF16),
            VMEM((BLK * CHUNK, BLK), F32),
            DMA((N_ROW,)),
            DMA((2,)),
            DMA((8,)),
            DMA((N_ROW,)),
            DMA((N_ROW,)),
            DMA((N_ROW,)),
            DMA,
            DMA,
            pltpu.SemaphoreType.REGULAR,
            pltpu.SemaphoreType.REGULAR,
        ],
        compiler_params=pltpu.CompilerParams(
            collective_id=1, has_side_effects=True, vmem_limit_bytes=LIMIT
        ),
        name="finish",
    )(half, w)


def on_device(blocks, block_vector, block_pair, block_count, occ_order, occ_coeffs, vir_coeffs):
    send, code, w = prepare(
        block_vector, block_pair, block_count, occ_order.reshape(1, NO), occ_coeffs.T, vir_coeffs, blocks
    )
    tiles, codes, w_all, theirs = exchange(send.reshape(N_VEC, CAP, BLK, BLK), code, w)
    half = half_transform(codes, tiles.reshape(SLOTS, BLK, BLK), w_all, theirs)
    result = finish(half, w_all)
    return (
        result[:, :NV_R].transpose(1, 0, 2),
        result[:, NV_R:NV_R + NO_R].transpose(1, 0, 2),
    )


def solution(mesh):
    placed = (
        P("vec", "row", None),
        P("row", "vec"),
        P("row", "vec"),
        P("row", "vec"),
        P(),
        P("row", None),
        P("row", None),
    )
    return jax.shard_map(
        on_device,
        mesh=mesh,
        in_specs=placed,
        out_specs=(P("row", "vec", None), P("row", "vec", None)),
        check_vma=False,
    )
```

```python
import jax
import jax.numpy as jnp
from jax import lax
from jax.experimental import pallas as pl
from jax.experimental.pallas import tpu as pltpu
from jax.sharding import PartitionSpec as P

MESH = pl.DeviceIdType.MESH
F32, BF16, I32 = jnp.float32, jnp.bfloat16, jnp.int32

N_VEC, N_ROW, N_CHIP = 32, 8, 16
CAP, SLOTS, BLK = 8, 256, 128
NAO, NO, NV, SPAN = 3072, 288, 2688, 384
VEC_DEV, PAIRS, ACROSS, TALL = 4, 72, 24, 3
NV_R, NO_R, NO_V = NV // N_ROW, NO // N_ROW, NO // N_VEC
W_R = 384
WIDE = 4 * W_R
K_HALF = NO // 2
CHUNK = 32
PARTS = 8
Q = 12
W_SHAPE = (Q, SPAN // 4, 512)
VMEM = pltpu.VMEM
LIMIT = 60 * 2**20
ANY = pl.BlockSpec(memory_space=pl.ANY)
IN_VMEM = pl.BlockSpec(memory_space=pltpu.VMEM)
DMA = pltpu.SemaphoreType.DMA


def prepare_kernel(vec_hbm, pair_hbm, count_ref, order_hbm, occ_hbm, vir_hbm, blocks_ref,
                   send_ref, code_hbm, w_hbm, vec_ref, pair_ref, order_ref, occ_ref, vir_ref,
                   code_ref, w_ref, tiles, pos_vmem, pos_smem, sem, pos_sem, in_sems, out_sems):
    loads = [
        pltpu.make_async_copy(src, dst, in_sems.at[n])
        for n, (src, dst) in enumerate(
            ((vec_hbm, vec_ref), (pair_hbm, pair_ref), (order_hbm, order_ref), (occ_hbm, occ_ref), (vir_hbm, vir_ref))
        )
    ]
    for load in loads:
        load.start()
    core = lax.rem(lax.axis_index("vec"), 2)
    count = count_ref[0, 0]
    loads[0].wait()
    vectors = vec_ref[...]
    owner = vectors // VEC_DEV
    above = lax.broadcasted_iota(I32, (SLOTS, SLOTS), 0)
    across = lax.broadcasted_iota(I32, (SLOTS, SLOTS), 1)
    owner_col = jnp.sum(jnp.where(above == across, owner, 0), axis=1, keepdims=True)
    earlier = (owner_col == owner) & (above < across)
    rank = jnp.sum(jnp.where(earlier, 1, 0), axis=0, keepdims=True)
    pos_vmem[...] = owner * CAP + rank
    to_smem = pltpu.make_async_copy(pos_vmem, pos_smem, pos_sem)
    to_smem.start()
    to_smem.wait()

    def begin(slot, carry):
        pltpu.make_async_copy(blocks_ref.at[slot], tiles.at[pos_smem[0, slot]], sem).start()
        return carry

    lax.fori_loop(0, count, begin, 0)

    loads[1].wait()
    code = vectors % VEC_DEV * PAIRS + pair_ref[...] + 1
    valid = lax.broadcasted_iota(I32, (1, SLOTS), 1) < count
    owners = lax.broadcasted_iota(I32, (N_VEC, SLOTS), 0)
    lane = lax.broadcasted_iota(I32, (N_VEC, BLK), 1)
    mine = (owners == owner) & valid
    table = jnp.zeros((N_VEC, BLK), I32)
    for r in range(CAP):
        picked = jnp.sum(jnp.where(mine & (rank == r), code, 0), axis=1, keepdims=True)
        table = jnp.where(lane == r, picked, table)
    code_ref[...] = jnp.broadcast_to(table[:, None, :], (N_VEC, 8, BLK))
    code_out = pltpu.make_async_copy(code_ref, code_hbm, out_sems.at[0])
    code_out.start()

    for load in loads[2:]:
        load.wait()
    pick = (lax.broadcasted_iota(I32, (NO, NO), 0) == order_ref[...]).astype(BF16)
    perm = lax.dot_general(occ_ref[...], pick, (((0,), (0,)), ((), ())), preferred_element_type=F32)
    for half in range(2):
        @pl.when(core == half)
        def _():
            for q in range(4):
                r = 4 * half + q
                head = vir_ref[:, NV_R * r:NV_R * r + 256]
                tail = vir_ref[:, NV_R * r + 256:NV_R * r + NV_R].astype(F32)
                occ = perm[:, NO_R * r:NO_R * r + NO_R]
                zero = jnp.zeros((SPAN, 12), F32)
                last = jnp.concatenate([tail, occ, zero], axis=1).astype(BF16)
                for b in range(4):
                    rows = slice(96 * b, 96 * b + 96)
                    w_ref[4 * (q // 2) + b, :, 256 * (q % 2):256 * (q % 2) + 256] = head[rows]
                    w_ref[8 + b, :, BLK * q:BLK * q + BLK] = last[rows]
    w_out = pltpu.make_async_copy(w_ref, w_hbm, out_sems.at[1])
    w_out.start()

    def end(slot, carry):
        pltpu.make_async_copy(blocks_ref.at[0], tiles.at[0], sem).wait()
        return carry

    lax.fori_loop(0, count, end, 0)
    tiles_out = pltpu.make_async_copy(tiles, send_ref, sem)
    tiles_out.start()
    tiles_out.wait()
    code_out.wait()
    w_out.wait()


def prepare(vectors, pairs, count, order, occ, vir, blocks):
    return pl.pallas_call(
        prepare_kernel,
        out_shape=(
            jax.ShapeDtypeStruct((N_VEC * CAP, BLK, BLK), BF16),
            jax.ShapeDtypeStruct((N_VEC, 8, BLK), I32),
            jax.ShapeDtypeStruct(W_SHAPE, BF16),
        ),
        in_specs=[ANY, ANY, pl.BlockSpec(memory_space=pltpu.SMEM), ANY, ANY, ANY, ANY],
        out_specs=(ANY, ANY, ANY),
        scratch_shapes=[
            VMEM((1, SLOTS), I32),
            VMEM((1, SLOTS), I32),
            VMEM((1, NO), I32),
            VMEM((NO, SPAN), BF16),
            VMEM((SPAN, NV), BF16),
            VMEM((N_VEC, 8, BLK), I32),
            VMEM(W_SHAPE, BF16),
            VMEM((N_VEC * CAP, BLK, BLK), BF16),
            VMEM((1, SLOTS), I32),
            pltpu.SMEM((1, SLOTS), I32),
            DMA,
            DMA,
            DMA((5,)),
            DMA((2,)),
        ],
        compiler_params=pltpu.CompilerParams(vmem_limit_bytes=LIMIT),
        name="prepare",
    )(vectors, pairs, count, order, occ, vir, blocks)


def exchange_kernel(send, code, w, recv, rcode, wfull, occ_hbm, tile_bounce, code_bounce, w_bounce, mine, theirs, occ,
                    lsem, tsend, trecv, csend, crecv, us, ur, ds, dr, os, orc, ol):
    v, z = lax.axis_index("vec"), lax.axis_index("row")
    core, x, y = lax.rem(v, 2), lax.rem(v // 2, 4), v // 8
    up, down = lax.rem(z + 1, N_ROW), lax.rem(z + N_ROW - 1, N_ROW)
    barrier = pltpu.get_barrier_semaphore()

    def greet(i, carry):
        pl.semaphore_signal(barrier, inc=1, device_id=(lax.rem(v + i, N_VEC), z), device_id_type=MESH)
        return carry

    lax.fori_loop(1, N_VEC, greet, 0)
    pl.semaphore_signal(barrier, inc=1, device_id=(v, up), device_id_type=MESH)
    pl.semaphore_signal(barrier, inc=1, device_id=(v, down), device_id_type=MESH)
    pl.semaphore_wait(barrier, N_VEC + 1)

    own = [(send.at[v], tile_bounce, recv.at[v]), (code.at[v], code_bounce, rcode.at[v]), (w, w_bounce, wfull.at[z])]
    own_in = [pltpu.make_async_copy(a, b, lsem.at[n]) for n, (a, b, c) in enumerate(own)]
    own_out = [pltpu.make_async_copy(b, c, lsem.at[n]) for n, (a, b, c) in enumerate(own)]
    for copy in own_in:
        copy.start()

    def remote(src, dst, send_sem, recv_sem, device):
        return pltpu.make_async_remote_copy(
            src_ref=src, dst_ref=dst, send_sem=send_sem, recv_sem=recv_sem, device_id=device, device_id_type=MESH
        )

    last = pl.ds(8, 4)

    def swap(origin, src):
        return remote(src.at[last], theirs.at[origin], os.at[origin], orc.at[origin], (v + 1 - 2 * core, z))

    def fetch(origin, src):
        return pltpu.make_async_copy(src.at[last], mine.at[origin], ol.at[origin])

    index = lax.broadcasted_iota(I32, (NO, 512), 0)
    column = lax.broadcasted_iota(I32, (NO, 512), 1)
    lane = column % BLK - (NV_R - 256)
    found = (lane >= 0) & (lane < NO_R)
    wanted = index - NO_R * (column // BLK) - lane
    pick_mine = (found & (wanted == 4 * NO_R * core)).astype(BF16)
    pick_theirs = (found & (wanted == 4 * NO_R * (1 - core))).astype(BF16)
    across = (((1,), (1,)), ((), ()))

    def pick_occ(origin):
        fetch(origin, w).wait()
        swap(origin, w).wait_recv()
        part = lax.dot_general(
            pick_mine, mine[origin].reshape(SPAN, 512), across, preferred_element_type=F32
        ) + lax.dot_general(pick_theirs, theirs[origin].reshape(SPAN, 512), across, preferred_element_type=F32)
        occ[:, pl.ds(pl.multiple_of(origin * SPAN, SPAN), SPAN)] = part.astype(BF16)

    def ring(step, piece, sign):
        origin = lax.rem(z - sign * step + 2 * N_ROW, N_ROW)
        src = w.at[piece] if step == 0 else wfull.at[origin, piece]
        ssem, rsem, to = (us, ur, up) if sign > 0 else (ds, dr, down)
        return remote(src, wfull.at[origin, piece], ssem.at[step * Q + piece], rsem.at[step * Q + piece], (v, to))

    def pieces(step, sign):
        if step < 3:
            return 0, Q
        return (0, Q // 2) if sign > 0 else (Q // 2, Q)

    def first(piece, carry):
        ring(0, piece, 1).start()
        ring(0, piece, -1).start()
        return carry

    lax.fori_loop(0, Q, first, 0)
    swap(z, w).start()
    fetch(z, w).start()

    def target(j):
        return ((y + j // 8) % 4) * 8 + ((x + j // 2) % 4) * 2 + lax.rem(core + j, 2)

    def give(n, carry):
        part = n // (N_VEC - 1)
        j = 1 + lax.rem(n * 11, N_VEC - 1)
        d = target(j)
        spot = pl.ds(part * (CAP // PARTS), CAP // PARTS)
        remote(send.at[d, spot], recv.at[v, spot], tsend.at[d], trecv.at[v], (d, z)).start()
        return carry

    def give_code(j, carry):
        d = target(j)
        remote(code.at[d], rcode.at[v], csend.at[d], crecv.at[v], (d, z)).start()
        return carry

    lax.fori_loop(0, PARTS * (N_VEC - 1), give, 0)
    lax.fori_loop(1, N_VEC, give_code, 0)

    for n in range(3):
        own_in[n].wait()
        own_out[n].start()

    def origin_of(step, sign):
        return lax.rem(z - sign * step + N_ROW, N_ROW)

    def pass_occ(step, sign):
        origin = origin_of(step, sign)
        swap(origin, wfull.at[origin]).start()
        fetch(origin, wfull.at[origin]).start()

    for step in range(1, 4):
        for piece in range(Q):
            for sign in (1, -1):
                low, high = pieces(step, sign)
                if low <= piece < high:
                    ring(step - 1, piece, sign).wait_recv()
                    ring(step, piece, sign).start()
        if step < 3:
            pass_occ(step, 1)
            pass_occ(step, -1)
        if step == 2:
            pick_occ(z)
        if step == 3:
            for sign in (1, -1):
                pick_occ(origin_of(1, sign))
                pick_occ(origin_of(2, sign))

    def finish(i, carry):
        d = lax.rem(v + i, N_VEC)
        pltpu.make_async_copy(send.at[d], recv.at[d], tsend.at[d]).wait()
        pltpu.make_async_copy(code.at[d], rcode.at[d], csend.at[d]).wait()
        pltpu.make_async_copy(send.at[d], recv.at[d], trecv.at[d]).wait()
        pltpu.make_async_copy(code.at[d], rcode.at[d], crecv.at[d]).wait()
        return carry

    for sign in (1, -1):
        low, high = pieces(3, sign)
        for piece in range(Q):
            if not low <= piece < high:
                ring(2, piece, sign).wait_recv()
        pass_occ(3, sign)
    for sign in (1, -1):
        low, high = pieces(3, sign)
        for piece in range(low, high):
            ring(3, piece, sign).wait_recv()
    pass_occ(4, 1)
    pick_occ(origin_of(3, 1))
    pick_occ(origin_of(3, -1))
    pick_occ(origin_of(4, 1))
    occ_out = pltpu.make_async_copy(occ, occ_hbm, lsem.at[3])
    occ_out.start()
    for sign in (1, -1):
        for step in range(4):
            low, high = pieces(step, sign)
            for piece in range(low, high):
                ring(step, piece, sign).wait_send()
    for origin in range(N_ROW):
        swap(origin, w).wait_send()
    lax.fori_loop(1, N_VEC, finish, 0)
    for copy in own_out:
        copy.wait()
    occ_out.wait()


def exchange(send, code, w):
    return pl.pallas_call(
        exchange_kernel,
        out_shape=(
            jax.ShapeDtypeStruct(send.shape, BF16),
            jax.ShapeDtypeStruct(code.shape, I32),
            jax.ShapeDtypeStruct((N_ROW,) + w.shape, BF16),
            jax.ShapeDtypeStruct((NO, NAO), BF16),
        ),
        in_specs=[ANY] * 3,
        out_specs=(ANY,) * 4,
        scratch_shapes=[
            VMEM((CAP, BLK, BLK), BF16),
            VMEM((8, BLK), I32),
            VMEM(W_SHAPE, BF16),
            VMEM((N_ROW, 4) + W_SHAPE[1:], BF16),
            VMEM((N_ROW, 4) + W_SHAPE[1:], BF16),
            VMEM((NO, NAO), BF16),
            DMA((4,)),
        ]
        + [DMA((N_VEC,))] * 4
        + [DMA((4 * Q,))] * 4
        + [DMA((N_ROW,))] * 3,
        compiler_params=pltpu.CompilerParams(collective_id=0, has_side_effects=True, vmem_limit_bytes=LIMIT),
        name="exchange",
    )(send, code, w)


def half_kernel(code_hbm, tiles_ref, occ_hbm, out_ref, tiles, dense, occ, code_ref, sems, more):
    group = 32
    others = [
        pltpu.make_async_copy(code_hbm, code_ref, more.at[0]),
        pltpu.make_async_copy(occ_hbm, occ, more.at[1]),
    ]
    for load in others:
        load.start()
    loads = [
        pltpu.make_async_copy(
            tiles_ref.at[pl.ds(n * group, group)], tiles.at[pl.ds(n * group, group)], sems.at[n]
        )
        for n in range(SLOTS // group)
    ]
    for load in loads:
        load.start()

    def clear(n, carry):
        dense[n] = jnp.zeros((BLK, NAO), F32)
        return carry

    lax.fori_loop(0, VEC_DEV * TALL, clear, 0)
    for load in others:
        load.wait()

    def place(n, carry):
        code = code_ref[n // CAP, 0, lax.rem(n, CAP)] - 1

        @pl.when(code >= 0)
        def _():
            block = code // ACROSS
            column = pl.ds(pl.multiple_of(lax.rem(code, ACROSS) * BLK, BLK), BLK)
            dense[block, :, column] += tiles[n].astype(F32)

        return carry

    for n, load in enumerate(loads):
        load.wait()
        lax.fori_loop(n * group, n * group + group, place, 0)

    for pair in range(VEC_DEV * TALL // 2):
        rows = jnp.concatenate([dense[2 * pair], dense[2 * pair + 1]], axis=0).astype(BF16)
        product = lax.dot_general(
            occ[...], rows, (((1,), (1,)), ((), ())), preferred_element_type=F32
        ).astype(BF16)
        for n in range(2):
            j, block = divmod(2 * pair + n, TALL)
            out_ref[j, :, BLK * block:BLK * block + BLK] = product[:, BLK * n:BLK * n + BLK]


def half_transform(code, tiles, occ):
    return pl.pallas_call(
        half_kernel,
        out_shape=jax.ShapeDtypeStruct((VEC_DEV, NO, SPAN), BF16),
        in_specs=[ANY] * 3,
        out_specs=IN_VMEM,
        scratch_shapes=[
            VMEM((SLOTS, BLK, BLK), BF16),
            VMEM((VEC_DEV * TALL, BLK, NAO), F32),
            VMEM((NO, NAO), BF16),
            pltpu.SMEM((N_VEC, 8, BLK), I32),
            DMA((SLOTS // 32,)),
            DMA((2,)),
        ],
        compiler_params=pltpu.CompilerParams(vmem_limit_bytes=LIMIT),
        name="half",
    )(code, tiles, occ)


def finish_kernel(half, w_hbm, out_ref, w, held, total, picks, chunk, taken, wide, wsem, lsem, hsend, hrecv, ssend, srecv, csend, crecv, x_sem, y_sem):
    v, z = lax.axis_index("vec"), lax.axis_index("row")
    chip, core = v // 2, lax.rem(v, 2)
    giver = z // 4
    takes_own = giver == core
    other = 2 * chip + 1 - core

    loads = [pltpu.make_async_copy(w_hbm.at[r], w.at[r], wsem.at[r]) for r in range(N_ROW)]
    for load in loads:
        load.start()

    barrier = pltpu.get_barrier_semaphore()

    def greet(device):
        pl.semaphore_signal(barrier, inc=1, device_id=device, device_id_type=MESH)

    x, y = lax.rem(chip, 4), chip // 4

    def line(i, carry):
        greet((v, lax.rem(z + i, N_ROW)))
        return carry

    def other_line(i, carry):
        greet((other, lax.rem(z + i, N_ROW)))
        return carry

    def along_x(i):
        return (y * 8 + lax.rem(x + i, 4) * 2 + core, z)

    def along_y(i):
        return (lax.rem(y + i, 4) * 8 + x * 2 + core, z)

    lax.fori_loop(1, N_ROW, line, 0)
    lax.fori_loop(0, N_ROW, other_line, 0)
    for i in range(1, 4):
        greet(along_x(i))
        greet(along_y(i))
    pl.semaphore_wait(barrier, 7 + 8 + 6)
    for i in range(1, 4):
        pl.semaphore_signal(x_sem, inc=1, device_id=along_x(i), device_id_type=MESH)

    def remote(src, dst, send_sem, recv_sem, device):
        return pltpu.make_async_remote_copy(
            src_ref=src, dst_ref=dst, send_sem=send_sem, recv_sem=recv_sem, device_id=device, device_id_type=MESH
        )

    def rows(h):
        return pl.ds(pl.multiple_of(h * K_HALF, 16), K_HALF)

    def send_half(n):
        j, h = n // 2, lax.rem(n, 2)
        return remote(half.at[j, rows(h)], held.at[z, rows(h)], hsend.at[n], hrecv.at[z], (2 * chip + h, 4 * core + j))

    def to_self(n):
        return (4 * core + n // 2 == z) & (lax.rem(n, 2) == core)

    stay = pltpu.make_async_copy(half.at[lax.rem(z, 4), rows(core)], held.at[z, rows(core)], lsem.at[0])

    def start_half(n, carry):
        @pl.when(jnp.logical_not(to_self(n)))
        def _():
            send_half(n).start()

        return carry

    lax.fori_loop(0, 8, start_half, 0)

    @pl.when(takes_own)
    def _():
        stay.start()

    def swap(r):
        return remote(held.at[r, rows(core)], held.at[r, rows(core)], ssend.at[r], srecv.at[r], (other, z))

    def pass_on(i):
        r = lax.rem(z + i, N_ROW)
        if i == 0:
            @pl.when(takes_own)
            def _():
                stay.wait()

            @pl.when(jnp.logical_not(takes_own))
            def _():
                pltpu.make_async_copy(held.at[r, rows(core)], held.at[r, rows(core)], hrecv.at[r]).wait()
        else:
            pltpu.make_async_copy(held.at[r, rows(core)], held.at[r, rows(core)], hrecv.at[r]).wait()
        swap(r).start()

    def arrived(i):
        r = lax.rem(z + i, N_ROW)
        theirs = held.at[r, rows(1 - core)]
        pltpu.make_async_copy(theirs, theirs, srecv.at[r]).wait()
        return r

    pl.semaphore_wait(x_sem, 3)
    for i in range(1, 4):
        pl.semaphore_signal(y_sem, inc=1, device_id=along_y(i), device_id_type=MESH)

    row = lax.broadcasted_iota(I32, (N_VEC * CHUNK, NO), 0)
    source = lax.broadcasted_iota(I32, (N_VEC * CHUNK, NO), 1)
    inside = row % CHUNK
    base = row // CHUNK * NO_V
    for t in range(3):
        picks[t] = ((inside // NO_V == t) & (base + inside % NO_V == source)).astype(BF16)

    place = chip * N_ROW + z

    def start_final(u):
        def body(i, carry):
            n = lax.rem(i * 37 + v * 2, 2 * N_VEC)
            to, q = n // 2, 2 * u + lax.rem(n, 2)
            src = chunk.at[q, pl.ds(pl.multiple_of(to * CHUNK, CHUNK), CHUNK)]
            dst = taken.at[pl.ds(pl.multiple_of(place * CHUNK, CHUNK), CHUNK)]
            device = (to, 4 * core + q)
            own = (to == v) & (device[1] == z)

            @pl.when(jnp.logical_not(own))
            def _():
                remote(src, dst, csend, crecv, device).start()

            @pl.when(own)
            def _():
                pltpu.make_async_copy(src, dst, lsem.at[1]).start()

            return carry

        lax.fori_loop(0, 2 * N_VEC, body, 0)

    sequence = (0, 1, 7, 2, 6, 3, 5, 4)
    for load in loads:
        load.wait()

    def columns(g, width=512):
        return pl.ds(pl.multiple_of(g * width, width), width)

    for n in range(4):
        first, second = sequence[2 * n], sequence[2 * n + 1]
        pass_on(first)
        pass_on(second)
        a, b = arrived(first), arrived(second)
        deep = jnp.concatenate([held[a], held[b]], axis=1)

        def add(g):
            four = pl.ds(4 * g, 4)
            block = jnp.concatenate([w[a, four].reshape(SPAN, 512), w[b, four].reshape(SPAN, 512)], axis=0)
            product = jnp.dot(deep, block, preferred_element_type=F32)
            if n == 0:
                total[:, columns(g)] = product
            else:
                total[:, columns(g)] += product

        add(2)
        if n < 3:
            add(0)
            add(1)
            continue
        for turn in range(2):
            u = lax.rem(z + turn, 2)
            add(u)
            stacked = jnp.zeros((N_VEC * CHUNK, 2 * BLK), F32)
            for t in range(3):
                if t < 2:
                    taken_columns = [total[:, columns(4 * u + 2 * q + t, BLK)] for q in range(2)]
                else:
                    taken_columns = [total[:, columns(8 + 2 * u + q, BLK)] for q in range(2)]
                addend = jnp.concatenate(taken_columns, axis=1).astype(BF16)
                stacked = stacked + jnp.dot(picks[t], addend, preferred_element_type=F32)
            for q in range(2):
                chunk[2 * u + q] = stacked[:, BLK * q:BLK * q + BLK].astype(BF16)
            if turn == 0:
                pl.semaphore_wait(y_sem, 3)
            start_final(u)

    def wait_half(n, carry):
        @pl.when(jnp.logical_not(to_self(n)))
        def _():
            send_half(n).wait_send()

        return carry

    lax.fori_loop(0, 8, wait_half, 0)

    def wait_swap(r, carry):
        swap(r).wait_send()
        return carry

    lax.fori_loop(0, N_ROW, wait_swap, 0)

    def wait_chunks(count):
        part = taken.at[pl.ds(0, count * CHUNK)]
        pltpu.make_async_copy(part, part, crecv).wait()
        pltpu.make_async_copy(part, part, csend).wait()

    @pl.when(takes_own)
    def _():
        wait_chunks(4 * N_VEC - 1)
        part = taken.at[pl.ds(0, CHUNK)]
        pltpu.make_async_copy(part, part, lsem.at[1]).wait()

    @pl.when(jnp.logical_not(takes_own))
    def _():
        wait_chunks(4 * N_VEC)

    wide[...] = taken[...].astype(F32)
    for t in range(3):
        for k in range(NO_V):
            block = wide[pl.ds(NO_V * t + k, BLK, stride=CHUNK), :]
            out_ref[k, BLK * t:BLK * t + BLK, :] = block.T.astype(BF16)


def finish(half, w):
    return pl.pallas_call(
        finish_kernel,
        out_shape=jax.ShapeDtypeStruct((NO_V, W_R, BLK), BF16),
        in_specs=[ANY, ANY],
        out_specs=IN_VMEM,
        scratch_shapes=[
            VMEM((N_ROW,) + W_SHAPE, BF16),
            VMEM((N_ROW, NO, SPAN), BF16),
            VMEM((NO, WIDE), F32),
            VMEM((3, N_VEC * CHUNK, NO), BF16),
            VMEM((4, N_VEC * CHUNK, BLK), BF16),
            VMEM((BLK * CHUNK, BLK), BF16),
            VMEM((BLK * CHUNK, BLK), F32),
            DMA((N_ROW,)),
            DMA((2,)),
            DMA((8,)),
            DMA((N_ROW,)),
            DMA((N_ROW,)),
            DMA((N_ROW,)),
            DMA,
            DMA,
            pltpu.SemaphoreType.REGULAR,
            pltpu.SemaphoreType.REGULAR,
        ],
        compiler_params=pltpu.CompilerParams(
            collective_id=1, has_side_effects=True, vmem_limit_bytes=LIMIT
        ),
        name="finish",
    )(half, w)


def on_device(blocks, block_vector, block_pair, block_count, occ_order, occ_coeffs, vir_coeffs):
    send, code, w = prepare(
        block_vector, block_pair, block_count, occ_order.reshape(1, NO), occ_coeffs.T, vir_coeffs, blocks
    )
    tiles, codes, w_all, occ = exchange(send.reshape(N_VEC, CAP, BLK, BLK), code, w)
    half = half_transform(codes, tiles.reshape(SLOTS, BLK, BLK), occ)
    result = finish(half, w_all)
    return (
        result[:, :NV_R].transpose(1, 0, 2),
        result[:, NV_R:NV_R + NO_R].transpose(1, 0, 2),
    )


def solution(mesh):
    placed = (
        P("vec", "row", None),
        P("row", "vec"),
        P("row", "vec"),
        P("row", "vec"),
        P(),
        P("row", None),
        P("row", None),
    )
    return jax.shard_map(
        on_device,
        mesh=mesh,
        in_specs=placed,
        out_specs=(P("row", "vec", None), P("row", "vec", None)),
        check_vma=False,
    )
```

```python
import jax
import jax.numpy as jnp
from jax import lax
from jax.experimental import pallas as pl
from jax.experimental.pallas import tpu as pltpu
from jax.sharding import PartitionSpec as P

MESH = pl.DeviceIdType.MESH
F32, BF16, I32 = jnp.float32, jnp.bfloat16, jnp.int32

N_VEC, N_ROW, N_CHIP = 32, 8, 16
CAP, SLOTS, BLK = 8, 256, 128
NAO, NO, NV, SPAN = 3072, 288, 2688, 384
VEC_DEV, PAIRS, ACROSS, TALL = 4, 72, 24, 3
NV_R, NO_R, NO_V = NV // N_ROW, NO // N_ROW, NO // N_VEC
W_R = 384
WIDE = 4 * W_R
K_HALF = NO // 2
CHUNK = 32
PARTS = 8
Q = 12
W_SHAPE = (Q, SPAN // 4, 512)
VMEM = pltpu.VMEM
LIMIT = 60 * 2**20
ANY = pl.BlockSpec(memory_space=pl.ANY)
IN_VMEM = pl.BlockSpec(memory_space=pltpu.VMEM)
DMA = pltpu.SemaphoreType.DMA


def prepare_kernel(vec_hbm, pair_hbm, count_ref, order_hbm, occ_hbm, vir_hbm, blocks_ref,
                   send_ref, code_hbm, w_hbm, vec_ref, pair_ref, order_ref, occ_ref, vir_ref,
                   code_ref, w_ref, tiles, pos_vmem, pos_smem, sem, pos_sem, in_sems, out_sems):
    loads = [
        pltpu.make_async_copy(src, dst, in_sems.at[n])
        for n, (src, dst) in enumerate(
            ((vec_hbm, vec_ref), (pair_hbm, pair_ref), (order_hbm, order_ref), (occ_hbm, occ_ref), (vir_hbm, vir_ref))
        )
    ]
    for load in loads:
        load.start()
    core = lax.rem(lax.axis_index("vec"), 2)
    count = count_ref[0, 0]
    loads[0].wait()
    vectors = vec_ref[...]
    owner = vectors // VEC_DEV
    above = lax.broadcasted_iota(I32, (SLOTS, SLOTS), 0)
    across = lax.broadcasted_iota(I32, (SLOTS, SLOTS), 1)
    owner_col = jnp.sum(jnp.where(above == across, owner, 0), axis=1, keepdims=True)
    earlier = (owner_col == owner) & (above < across)
    rank = jnp.sum(jnp.where(earlier, 1, 0), axis=0, keepdims=True)
    pos_vmem[...] = owner * CAP + rank
    to_smem = pltpu.make_async_copy(pos_vmem, pos_smem, pos_sem)
    to_smem.start()
    to_smem.wait()

    def begin(slot, carry):
        pltpu.make_async_copy(blocks_ref.at[slot], tiles.at[pos_smem[0, slot]], sem).start()
        return carry

    lax.fori_loop(0, count, begin, 0)

    loads[1].wait()
    pairs = pair_ref[...]
    code = (vectors % VEC_DEV * TALL + pairs // ACROSS) * 32 + pairs % ACROSS + 1
    valid = lax.broadcasted_iota(I32, (1, SLOTS), 1) < count
    owners = lax.broadcasted_iota(I32, (N_VEC, SLOTS), 0)
    lane = lax.broadcasted_iota(I32, (N_VEC, BLK), 1)
    mine = (owners == owner) & valid
    table = jnp.zeros((N_VEC, BLK), I32)
    for r in range(CAP):
        picked = jnp.sum(jnp.where(mine & (rank == r), code, 0), axis=1, keepdims=True)
        table = jnp.where(lane == r, picked, table)
    code_ref[...] = jnp.broadcast_to(table[:, None, :], (N_VEC, 8, BLK))
    code_out = pltpu.make_async_copy(code_ref, code_hbm, out_sems.at[0])
    code_out.start()

    for load in loads[2:]:
        load.wait()
    pick = (lax.broadcasted_iota(I32, (NO, NO), 0) == order_ref[...].reshape(1, NO)).astype(BF16)
    perm = lax.dot_general(occ_ref[...], pick, (((0,), (0,)), ((), ())), preferred_element_type=F32)
    for half in range(2):
        @pl.when(core == half)
        def _():
            for q in range(4):
                r = 4 * half + q
                head = vir_ref[:, NV_R * r:NV_R * r + 256]
                tail = vir_ref[:, NV_R * r + 256:NV_R * r + NV_R].astype(F32)
                occ = perm[:, NO_R * r:NO_R * r + NO_R]
                zero = jnp.zeros((SPAN, 12), F32)
                last = jnp.concatenate([tail, occ, zero], axis=1).astype(BF16)
                for b in range(4):
                    rows = slice(96 * b, 96 * b + 96)
                    w_ref[4 * (q // 2) + b, :, 256 * (q % 2):256 * (q % 2) + 256] = head[rows]
                    w_ref[8 + b, :, BLK * q:BLK * q + BLK] = last[rows]
    w_out = pltpu.make_async_copy(w_ref, w_hbm, out_sems.at[1])
    w_out.start()

    def end(slot, carry):
        pltpu.make_async_copy(blocks_ref.at[0], tiles.at[0], sem).wait()
        return carry

    lax.fori_loop(0, count, end, 0)
    tiles_out = pltpu.make_async_copy(tiles, send_ref, sem)
    tiles_out.start()
    tiles_out.wait()
    code_out.wait()
    w_out.wait()


def prepare(vectors, pairs, count, order, occ, vir, blocks):
    return pl.pallas_call(
        prepare_kernel,
        out_shape=(
            jax.ShapeDtypeStruct((N_VEC * CAP, BLK, BLK), BF16),
            jax.ShapeDtypeStruct((N_VEC, 8, BLK), I32),
            jax.ShapeDtypeStruct(W_SHAPE, BF16),
        ),
        in_specs=[ANY, ANY, pl.BlockSpec(memory_space=pltpu.SMEM), ANY, ANY, ANY, ANY],
        out_specs=(ANY, ANY, ANY),
        scratch_shapes=[
            VMEM((1, SLOTS), I32),
            VMEM((1, SLOTS), I32),
            VMEM((NO,), I32),
            VMEM((NO, SPAN), BF16),
            VMEM((SPAN, NV), BF16),
            VMEM((N_VEC, 8, BLK), I32),
            VMEM(W_SHAPE, BF16),
            VMEM((N_VEC * CAP, BLK, BLK), BF16),
            VMEM((1, SLOTS), I32),
            pltpu.SMEM((1, SLOTS), I32),
            DMA,
            DMA,
            DMA((5,)),
            DMA((2,)),
        ],
        compiler_params=pltpu.CompilerParams(vmem_limit_bytes=LIMIT),
        name="prepare",
    )(vectors, pairs, count, order, occ, vir, blocks)


def exchange_kernel(send, code, w, recv, code_out, wfull, occ_hbm, tile_bounce, rcode, codes, w_bounce, mine, theirs, occ,
                    lsem, tsend, trecv, csend, crecv, us, ur, ds, dr, os, orc, ol):
    v, z = lax.axis_index("vec"), lax.axis_index("row")
    core, x, y = lax.rem(v, 2), lax.rem(v // 2, 4), v // 8
    up, down = lax.rem(z + 1, N_ROW), lax.rem(z + N_ROW - 1, N_ROW)
    barrier = pltpu.get_barrier_semaphore()

    def greet(i, carry):
        pl.semaphore_signal(barrier, inc=1, device_id=(lax.rem(v + i, N_VEC), z), device_id_type=MESH)
        return carry

    lax.fori_loop(1, N_VEC, greet, 0)
    pl.semaphore_signal(barrier, inc=1, device_id=(v, up), device_id_type=MESH)
    pl.semaphore_signal(barrier, inc=1, device_id=(v, down), device_id_type=MESH)
    pl.semaphore_wait(barrier, N_VEC + 1)

    own = [(send.at[v], tile_bounce, recv.at[v]), (w, w_bounce, wfull.at[z])]
    own_in = [pltpu.make_async_copy(a, b, lsem.at[n]) for n, (a, b, c) in enumerate(own)]
    own_out = [pltpu.make_async_copy(b, c, lsem.at[n]) for n, (a, b, c) in enumerate(own)]
    own_code = pltpu.make_async_copy(code.at[v], rcode.at[v], lsem.at[2])
    own_code.start()
    for copy in own_in:
        copy.start()

    def remote(src, dst, send_sem, recv_sem, device):
        return pltpu.make_async_remote_copy(
            src_ref=src, dst_ref=dst, send_sem=send_sem, recv_sem=recv_sem, device_id=device, device_id_type=MESH
        )

    last = pl.ds(8, 4)

    def swap(origin, src):
        return remote(src.at[last], theirs.at[origin], os.at[origin], orc.at[origin], (v + 1 - 2 * core, z))

    def fetch(origin, src):
        return pltpu.make_async_copy(src.at[last], mine.at[origin], ol.at[origin])

    index = lax.broadcasted_iota(I32, (NO, 512), 0)
    column = lax.broadcasted_iota(I32, (NO, 512), 1)
    lane = column % BLK - (NV_R - 256)
    found = (lane >= 0) & (lane < NO_R)
    wanted = index - NO_R * (column // BLK) - lane
    pick_mine = (found & (wanted == 4 * NO_R * core)).astype(BF16)
    pick_theirs = (found & (wanted == 4 * NO_R * (1 - core))).astype(BF16)
    across = (((1,), (1,)), ((), ()))

    def pick_occ(origin):
        fetch(origin, w).wait()
        swap(origin, w).wait_recv()
        part = lax.dot_general(
            pick_mine, mine[origin].reshape(SPAN, 512), across, preferred_element_type=F32
        ) + lax.dot_general(pick_theirs, theirs[origin].reshape(SPAN, 512), across, preferred_element_type=F32)
        occ[:, pl.ds(pl.multiple_of(origin * SPAN, SPAN), SPAN)] = part.astype(BF16)

    def ring(step, piece, sign):
        origin = lax.rem(z - sign * step + 2 * N_ROW, N_ROW)
        src = w.at[piece] if step == 0 else wfull.at[origin, piece]
        ssem, rsem, to = (us, ur, up) if sign > 0 else (ds, dr, down)
        return remote(src, wfull.at[origin, piece], ssem.at[step * Q + piece], rsem.at[step * Q + piece], (v, to))

    def pieces(step, sign):
        if step < 3:
            return 0, Q
        return (0, Q // 2) if sign > 0 else (Q // 2, Q)

    def first(piece, carry):
        ring(0, piece, 1).start()
        ring(0, piece, -1).start()
        return carry

    lax.fori_loop(0, Q, first, 0)
    swap(z, w).start()
    fetch(z, w).start()

    def target(j):
        return ((y + j // 8) % 4) * 8 + ((x + j // 2) % 4) * 2 + lax.rem(core + j, 2)

    def give(n, carry):
        part = n // (N_VEC - 1)
        j = 1 + lax.rem(n * 11, N_VEC - 1)
        d = target(j)
        spot = pl.ds(part * (CAP // PARTS), CAP // PARTS)
        remote(send.at[d, spot], recv.at[v, spot], tsend.at[d], trecv.at[v], (d, z)).start()
        return carry

    def give_code(j, carry):
        d = target(j)
        remote(code.at[d], rcode.at[v], csend.at[d], crecv.at[v], (d, z)).start()
        return carry

    lax.fori_loop(0, PARTS * (N_VEC - 1), give, 0)
    lax.fori_loop(1, N_VEC, give_code, 0)

    for n in range(2):
        own_in[n].wait()
        own_out[n].start()

    def origin_of(step, sign):
        return lax.rem(z - sign * step + N_ROW, N_ROW)

    def pass_occ(step, sign):
        origin = origin_of(step, sign)
        swap(origin, wfull.at[origin]).start()
        fetch(origin, wfull.at[origin]).start()

    for step in range(1, 4):
        for piece in range(Q):
            for sign in (1, -1):
                low, high = pieces(step, sign)
                if low <= piece < high:
                    ring(step - 1, piece, sign).wait_recv()
                    ring(step, piece, sign).start()
        if step < 3:
            pass_occ(step, 1)
            pass_occ(step, -1)
        if step == 2:
            pick_occ(z)
        if step == 3:
            for sign in (1, -1):
                pick_occ(origin_of(1, sign))
                pick_occ(origin_of(2, sign))

    def finish(i, carry):
        d = lax.rem(v + i, N_VEC)
        pltpu.make_async_copy(send.at[d], recv.at[d], tsend.at[d]).wait()
        pltpu.make_async_copy(code.at[d], rcode.at[d], csend.at[d]).wait()
        pltpu.make_async_copy(send.at[d], recv.at[d], trecv.at[d]).wait()
        pltpu.make_async_copy(code.at[d], rcode.at[d], crecv.at[d]).wait()
        return carry

    for sign in (1, -1):
        low, high = pieces(3, sign)
        for piece in range(Q):
            if not low <= piece < high:
                ring(2, piece, sign).wait_recv()
        pass_occ(3, sign)
    for sign in (1, -1):
        low, high = pieces(3, sign)
        for piece in range(low, high):
            ring(3, piece, sign).wait_recv()
    pass_occ(4, 1)
    pick_occ(origin_of(3, 1))
    pick_occ(origin_of(3, -1))
    pick_occ(origin_of(4, 1))
    occ_out = pltpu.make_async_copy(occ, occ_hbm, lsem.at[3])
    occ_out.start()
    for sign in (1, -1):
        for step in range(4):
            low, high = pieces(step, sign)
            for piece in range(low, high):
                ring(step, piece, sign).wait_send()
    for origin in range(N_ROW):
        swap(origin, w).wait_send()
    lax.fori_loop(1, N_VEC, finish, 0)
    own_code.wait()
    codes[...] = rcode[:, 0, :]
    codes_out = pltpu.make_async_copy(codes, code_out, lsem.at[2])
    codes_out.start()
    for copy in own_out:
        copy.wait()
    occ_out.wait()
    codes_out.wait()


def exchange(send, code, w):
    return pl.pallas_call(
        exchange_kernel,
        out_shape=(
            jax.ShapeDtypeStruct(send.shape, BF16),
            jax.ShapeDtypeStruct((N_VEC, BLK), I32),
            jax.ShapeDtypeStruct((N_ROW,) + w.shape, BF16),
            jax.ShapeDtypeStruct((NO, NAO), BF16),
        ),
        in_specs=[ANY] * 3,
        out_specs=(ANY,) * 4,
        scratch_shapes=[
            VMEM((CAP, BLK, BLK), BF16),
            VMEM((N_VEC, 8, BLK), I32),
            VMEM((N_VEC, BLK), I32),
            VMEM(W_SHAPE, BF16),
            VMEM((N_ROW, 4) + W_SHAPE[1:], BF16),
            VMEM((N_ROW, 4) + W_SHAPE[1:], BF16),
            VMEM((NO, NAO), BF16),
            DMA((4,)),
        ]
        + [DMA((N_VEC,))] * 4
        + [DMA((4 * Q,))] * 4
        + [DMA((N_ROW,))] * 3,
        compiler_params=pltpu.CompilerParams(collective_id=0, has_side_effects=True, vmem_limit_bytes=LIMIT),
        name="exchange",
    )(send, code, w)


def half_kernel(code_hbm, tiles_ref, occ_hbm, out_ref, tiles, dense, occ, code_ref, sems, more):
    group = 32
    others = [
        pltpu.make_async_copy(code_hbm, code_ref, more.at[0]),
        pltpu.make_async_copy(occ_hbm, occ, more.at[1]),
    ]
    for load in others:
        load.start()
    loads = [
        pltpu.make_async_copy(
            tiles_ref.at[pl.ds(n * group, group)], tiles.at[pl.ds(n * group, group)], sems.at[n]
        )
        for n in range(SLOTS // group)
    ]
    for load in loads:
        load.start()

    def clear(n, carry):
        dense[n] = jnp.zeros((BLK, NAO), F32)
        return carry

    lax.fori_loop(0, VEC_DEV * TALL, clear, 0)
    for load in others:
        load.wait()

    def place(n, carry):
        for r in range(CAP):
            code = code_ref[n, r] - 1

            @pl.when(code >= 0)
            def _():
                block = lax.shift_right_logical(code, 5)
                column = pl.ds(pl.multiple_of((code & 31) * BLK, BLK), BLK)
                dense[block, :, column] += tiles[n * CAP + r].astype(F32)

        return carry

    for n, load in enumerate(loads):
        load.wait()
        lax.fori_loop(n * group // CAP, (n + 1) * group // CAP, place, 0)

    for pair in range(VEC_DEV * TALL // 2):
        rows = jnp.concatenate([dense[2 * pair], dense[2 * pair + 1]], axis=0).astype(BF16)
        product = lax.dot_general(
            occ[...], rows, (((1,), (1,)), ((), ())), preferred_element_type=F32
        ).astype(BF16)
        for n in range(2):
            j, block = divmod(2 * pair + n, TALL)
            out_ref[j, :, BLK * block:BLK * block + BLK] = product[:, BLK * n:BLK * n + BLK]


def half_transform(code, tiles, occ):
    return pl.pallas_call(
        half_kernel,
        out_shape=jax.ShapeDtypeStruct((VEC_DEV, NO, SPAN), BF16),
        in_specs=[ANY] * 3,
        out_specs=IN_VMEM,
        scratch_shapes=[
            VMEM((SLOTS, BLK, BLK), BF16),
            VMEM((VEC_DEV * TALL, BLK, NAO), F32),
            VMEM((NO, NAO), BF16),
            pltpu.SMEM((N_VEC, BLK), I32),
            DMA((SLOTS // 32,)),
            DMA((2,)),
        ],
        compiler_params=pltpu.CompilerParams(vmem_limit_bytes=LIMIT),
        name="half",
    )(code, tiles, occ)


def finish_kernel(half, w_hbm, taken, w, held, total, picks, chunk, wsem, lsem, hsend, hrecv, ssend, srecv, csend, crecv, x_sem, y_sem):
    v, z = lax.axis_index("vec"), lax.axis_index("row")
    chip, core = v // 2, lax.rem(v, 2)
    giver = z // 4
    takes_own = giver == core
    other = 2 * chip + 1 - core

    loads = [pltpu.make_async_copy(w_hbm.at[r], w.at[r], wsem.at[r]) for r in range(N_ROW)]
    for load in loads:
        load.start()

    barrier = pltpu.get_barrier_semaphore()

    def greet(device):
        pl.semaphore_signal(barrier, inc=1, device_id=device, device_id_type=MESH)

    x, y = lax.rem(chip, 4), chip // 4

    def line(i, carry):
        greet((v, lax.rem(z + i, N_ROW)))
        return carry

    def other_line(i, carry):
        greet((other, lax.rem(z + i, N_ROW)))
        return carry

    def along_x(i):
        return (y * 8 + lax.rem(x + i, 4) * 2 + core, z)

    def along_y(i):
        return (lax.rem(y + i, 4) * 8 + x * 2 + core, z)

    lax.fori_loop(1, N_ROW, line, 0)
    lax.fori_loop(0, N_ROW, other_line, 0)
    for i in range(1, 4):
        greet(along_x(i))
        greet(along_y(i))
    pl.semaphore_wait(barrier, 7 + 8 + 6)
    for i in range(1, 4):
        pl.semaphore_signal(x_sem, inc=1, device_id=along_x(i), device_id_type=MESH)

    def remote(src, dst, send_sem, recv_sem, device):
        return pltpu.make_async_remote_copy(
            src_ref=src, dst_ref=dst, send_sem=send_sem, recv_sem=recv_sem, device_id=device, device_id_type=MESH
        )

    def rows(phase, h):
        return pl.ds(K_HALF * phase + 80 * h, 80 - 16 * h)

    def on_core(h, condition=True):
        return pl.when((core == h) & condition)

    def send_half(phase, j, h):
        return remote(
            half.at[j, rows(phase, h)], held.at[z, rows(phase, h)],
            hsend.at[8 * phase + 2 * j + h], hrecv.at[N_ROW * phase + z], (2 * chip + h, 4 * core + j),
        )

    def not_to_self(j, h):
        return pl.when(jnp.logical_not((4 * core + j == z) & (core == h)))

    def stay(phase, h):
        part = rows(phase, h)
        return pltpu.make_async_copy(half.at[lax.rem(z, 4), part], held.at[z, part], lsem.at[phase])

    for phase in range(2):
        for j in range(4):
            for h in range(2):
                @not_to_self(j, h)
                def _():
                    send_half(phase, j, h).start()

        for h in range(2):
            @on_core(h, takes_own)
            def _():
                stay(phase, h).start()

    def swap(phase, r, h):
        part = rows(phase, h)
        n = N_ROW * phase + r
        return remote(held.at[r, part], held.at[r, part], ssend.at[n], srecv.at[n], (other, z))

    def await_part(part, semaphore):
        pltpu.make_async_copy(part, part, semaphore).wait()

    def pass_on(phase, i):
        r = lax.rem(z + i, N_ROW)
        for h in range(2):
            def arrived_here(phase=phase, h=h):
                await_part(held.at[r, rows(phase, h)], hrecv.at[N_ROW * phase + r])

            if i == 0:
                @on_core(h, takes_own)
                def _():
                    stay(phase, h).wait()

                on_core(h, jnp.logical_not(takes_own))(arrived_here)
            else:
                on_core(h)(arrived_here)

            @on_core(h)
            def _():
                swap(phase, r, h).start()

    def arrived(phase, i):
        r = lax.rem(z + i, N_ROW)
        for h in range(2):
            @on_core(h)
            def _():
                await_part(held.at[r, rows(phase, 1 - h)], srecv.at[N_ROW * phase + r])
        return r

    pl.semaphore_wait(x_sem, 3)
    for i in range(1, 4):
        pl.semaphore_signal(y_sem, inc=1, device_id=along_y(i), device_id_type=MESH)

    height = N_VEC * CHUNK // 2
    row = lax.broadcasted_iota(I32, (height, K_HALF), 0)
    source = lax.broadcasted_iota(I32, (height, K_HALF), 1)
    inside = row % CHUNK
    base = row // CHUNK * NO_V
    for t in range(3):
        picks[t] = ((inside // NO_V == t) & (base + inside % NO_V == source)).astype(BF16)

    place = chip * N_ROW + z

    def start_final(phase):
        def body(i, carry):
            n = lax.rem(i * 37 + v * 4, 2 * N_VEC)
            to, q = n // 4 + N_VEC // 2 * phase, lax.rem(n, 4)
            src = chunk.at[q, pl.ds(pl.multiple_of(to * CHUNK, CHUNK), CHUNK)]
            dst = taken.at[pl.ds(pl.multiple_of(place * CHUNK, CHUNK), CHUNK)]
            device = (to, 4 * core + q)
            own = (to == v) & (device[1] == z)

            @pl.when(jnp.logical_not(own))
            def _():
                remote(src, dst, csend, crecv, device).start()

            @pl.when(own)
            def _():
                pltpu.make_async_copy(src, dst, lsem.at[2]).start()

            return carry

        lax.fori_loop(0, 2 * N_VEC, body, 0)

    sequence = (0, 1, 7, 2, 6, 3, 5, 4)
    for load in loads:
        load.wait()
    for phase in range(2):
        here = slice(K_HALF * phase, K_HALF * phase + K_HALF)
        for n in range(4):
            first, second = sequence[2 * n], sequence[2 * n + 1]
            pass_on(phase, first)
            pass_on(phase, second)
            a, b = arrived(phase, first), arrived(phase, second)
            deep = jnp.concatenate([held[a, here], held[b, here]], axis=1)
            for g in range(3):
                four, cols = slice(4 * g, 4 * g + 4), slice(512 * g, 512 * g + 512)
                block = jnp.concatenate([w[a, four].reshape(SPAN, 512), w[b, four].reshape(SPAN, 512)], axis=0)
                product = jnp.dot(deep, block, preferred_element_type=F32)
                if n == 0:
                    total[:, cols] = product
                else:
                    total[:, cols] += product
        stacked = jnp.zeros((height, 4 * BLK), F32)
        for t in range(3):
            if t < 2:
                addend = jnp.concatenate([total[:, 256 * q + BLK * t:256 * q + BLK * t + BLK] for q in range(4)], axis=1)
            else:
                addend = total[:, 1024:1536]
            stacked = stacked + jnp.dot(picks[t], addend.astype(BF16), preferred_element_type=F32)
        for q in range(4):
            chunk[q, height * phase:height * phase + height] = stacked[:, BLK * q:BLK * q + BLK].astype(BF16)
        if phase == 0:
            pl.semaphore_wait(y_sem, 3)
        start_final(phase)

    for phase in range(2):
        for j in range(4):
            for h in range(2):
                @not_to_self(j, h)
                def _():
                    send_half(phase, j, h).wait_send()

        for h in range(2):
            @on_core(h)
            def _():
                def wait_swap(r, carry):
                    swap(phase, r, h).wait_send()
                    return carry

                lax.fori_loop(0, N_ROW, wait_swap, 0)

    def wait_chunks(count):
        part = taken.at[pl.ds(0, count * CHUNK)]
        pltpu.make_async_copy(part, part, crecv).wait()
        pltpu.make_async_copy(part, part, csend).wait()

    @pl.when(takes_own)
    def _():
        wait_chunks(4 * N_VEC - 1)
        part = taken.at[pl.ds(0, CHUNK)]
        pltpu.make_async_copy(part, part, lsem.at[2]).wait()

    @pl.when(jnp.logical_not(takes_own))
    def _():
        wait_chunks(4 * N_VEC)


def finish(half, w):
    return pl.pallas_call(
        finish_kernel,
        out_shape=jax.ShapeDtypeStruct((BLK * CHUNK, BLK), BF16),
        in_specs=[ANY, ANY],
        out_specs=ANY,
        scratch_shapes=[
            VMEM((N_ROW,) + W_SHAPE, BF16),
            VMEM((N_ROW, NO, SPAN), BF16),
            VMEM((K_HALF, WIDE), F32),
            VMEM((3, N_VEC * CHUNK // 2, K_HALF), BF16),
            VMEM((4, N_VEC * CHUNK, BLK), BF16),
            DMA((N_ROW,)),
            DMA((3,)),
            DMA((2 * 8,)),
            DMA((2 * N_ROW,)),
            DMA((2 * N_ROW,)),
            DMA((2 * N_ROW,)),
            DMA,
            DMA,
            pltpu.SemaphoreType.REGULAR,
            pltpu.SemaphoreType.REGULAR,
        ],
        compiler_params=pltpu.CompilerParams(
            collective_id=1, has_side_effects=True, vmem_limit_bytes=LIMIT
        ),
        name="finish",
    )(half, w)


def arrange_kernel(taken, ov_ref, oo_ref, wide):
    wide[...] = taken[...].astype(F32)
    for t in range(3):
        for k in range(NO_V):
            block = wide[pl.ds(NO_V * t + k, BLK, stride=CHUNK), :].T.astype(BF16)
            if t < 2:
                ov_ref[k, BLK * t:BLK * t + BLK, :] = block
            else:
                ov_ref[k, 256:NV_R, :] = block[:NV_R - 256]
                oo_ref[k] = block[NV_R - 256:W_R - 256 - 12]


def arrange(taken):
    return pl.pallas_call(
        arrange_kernel,
        out_shape=(
            jax.ShapeDtypeStruct((NO_V, NV_R, BLK), BF16),
            jax.ShapeDtypeStruct((NO_V, NO_R, BLK), BF16),
        ),
        in_specs=[IN_VMEM],
        out_specs=(IN_VMEM, IN_VMEM),
        scratch_shapes=[VMEM((BLK * CHUNK, BLK), F32)],
        compiler_params=pltpu.CompilerParams(vmem_limit_bytes=LIMIT),
        name="arrange",
    )(taken)


def on_device(blocks, block_vector, block_pair, block_count, occ_order, occ_coeffs, vir_coeffs):
    send, code, w = prepare(
        block_vector, block_pair, block_count, occ_order, occ_coeffs.T, vir_coeffs, blocks
    )
    tiles, codes, w_all, occ = exchange(send.reshape(N_VEC, CAP, BLK, BLK), code, w)
    half = half_transform(codes, tiles.reshape(SLOTS, BLK, BLK), occ)
    ov, oo = arrange(finish(half, w_all))
    return ov.transpose(1, 0, 2), oo.transpose(1, 0, 2)


def solution(mesh):
    placed = (
        P("vec", "row", None),
        P("row", "vec"),
        P("row", "vec"),
        P("row", "vec"),
        P(),
        P("row", None),
        P("row", None),
    )
    return jax.shard_map(
        on_device,
        mesh=mesh,
        in_specs=placed,
        out_specs=(P("row", "vec", None), P("row", "vec", None)),
        check_vma=False,
    )
```

```python
import jax
import jax.numpy as jnp
from jax import lax
from jax.experimental import pallas as pl
from jax.experimental.pallas import tpu as pltpu
from jax.sharding import PartitionSpec as P

MESH = pl.DeviceIdType.MESH
F32, BF16, I32 = jnp.float32, jnp.bfloat16, jnp.int32

N_VEC, N_ROW, N_CHIP = 32, 8, 16
CAP, SLOTS, BLK = 8, 256, 128
GROUP = 32
NAO, NO, NV, SPAN = 3072, 288, 2688, 384
VEC_DEV, PAIRS, ACROSS, TALL = 4, 72, 24, 3
NV_R, NO_R, NO_V = NV // N_ROW, NO // N_ROW, NO // N_VEC
W_R = 384
WIDE = 4 * W_R
K_HALF = NO // 2
CHUNK = 32
PARTS = 8
Q = 12
W_SHAPE = (Q, SPAN // 4, 512)
VMEM = pltpu.VMEM
LIMIT = 60 * 2**20
ANY = pl.BlockSpec(memory_space=pl.ANY)
IN_VMEM = pl.BlockSpec(memory_space=pltpu.VMEM)
DMA = pltpu.SemaphoreType.DMA


def prepare_kernel(vec_hbm, pair_hbm, count_ref, order_hbm, occ_hbm, vir_hbm, blocks_ref,
                   send_ref, code_hbm, w_hbm, vec_ref, pair_ref, order_ref, occ_ref, vir_ref,
                   code_ref, w_ref, tiles, pos_vmem, pos_smem, sem, pos_sem, in_sems, out_sems):
    loads = [
        pltpu.make_async_copy(src, dst, in_sems.at[n])
        for n, (src, dst) in enumerate(
            ((vec_hbm, vec_ref), (pair_hbm, pair_ref), (order_hbm, order_ref), (occ_hbm, occ_ref), (vir_hbm, vir_ref))
        )
    ]
    for load in loads:
        load.start()
    core = lax.rem(lax.axis_index("vec"), 2)
    count = count_ref[0, 0]
    loads[0].wait()
    vectors = vec_ref[...]
    owner = vectors // VEC_DEV
    above = lax.broadcasted_iota(I32, (SLOTS, SLOTS), 0)
    across = lax.broadcasted_iota(I32, (SLOTS, SLOTS), 1)
    owner_col = jnp.sum(jnp.where(above == across, owner, 0), axis=1, keepdims=True)
    earlier = (owner_col == owner) & (above < across)
    rank = jnp.sum(jnp.where(earlier, 1, 0), axis=0, keepdims=True)
    place = jnp.where(across[:1] < count, owner * CAP + rank, SLOTS)
    place_col = jnp.sum(jnp.where(above == across, place, 0), axis=1, keepdims=True)
    pos_vmem[...] = jnp.sum(jnp.where(place_col == across, above + 1, 0), axis=0, keepdims=True)
    to_smem = pltpu.make_async_copy(pos_vmem, pos_smem, pos_sem)
    to_smem.start()
    to_smem.wait()

    def load_group(group):
        def begin(i, total):
            target = group * GROUP + i
            slot = pos_smem[0, target]

            @pl.when(slot > 0)
            def _():
                pltpu.make_async_copy(blocks_ref.at[slot - 1], tiles.at[target], sem.at[group]).start()

            return total + jnp.where(slot > 0, 1, 0)

        return lax.fori_loop(0, GROUP, begin, 0)

    def write_group(group):
        part = pl.ds(group * GROUP, GROUP)
        return pltpu.make_async_copy(tiles.at[part], send_ref.at[part], sem.at[group])

    def pass_group(group, loaded):
        def end(i, carry):
            pltpu.make_async_copy(blocks_ref.at[0], tiles.at[0], sem.at[group]).wait()
            return carry

        lax.fori_loop(0, loaded, end, 0)
        write_group(group).start()

    groups = SLOTS // GROUP
    loaded = []
    for group in range(groups):
        loaded.append(load_group(group))
        if group >= 2:
            pass_group(group - 2, loaded[group - 2])

    loads[1].wait()
    pairs = pair_ref[...]
    code = (vectors % VEC_DEV * TALL + pairs // ACROSS) * 32 + pairs % ACROSS + 1
    valid = lax.broadcasted_iota(I32, (1, SLOTS), 1) < count
    owners = lax.broadcasted_iota(I32, (N_VEC, SLOTS), 0)
    lane = lax.broadcasted_iota(I32, (N_VEC, BLK), 1)
    mine = (owners == owner) & valid
    table = jnp.zeros((N_VEC, BLK), I32)
    for r in range(CAP):
        picked = jnp.sum(jnp.where(mine & (rank == r), code, 0), axis=1, keepdims=True)
        table = jnp.where(lane == r, picked, table)
    code_ref[...] = jnp.broadcast_to(table[:, None, :], (N_VEC, 8, BLK))
    code_out = pltpu.make_async_copy(code_ref, code_hbm, out_sems.at[0])
    code_out.start()

    for load in loads[2:]:
        load.wait()
    pick = (lax.broadcasted_iota(I32, (NO, NO), 0) == order_ref[...].reshape(1, NO)).astype(BF16)
    perm = lax.dot_general(occ_ref[...], pick, (((0,), (0,)), ((), ())), preferred_element_type=F32)
    for half in range(2):
        @pl.when(core == half)
        def _():
            for q in range(4):
                r = 4 * half + q
                head = vir_ref[:, NV_R * r:NV_R * r + 256]
                tail = vir_ref[:, NV_R * r + 256:NV_R * r + NV_R].astype(F32)
                occ = perm[:, NO_R * r:NO_R * r + NO_R]
                zero = jnp.zeros((SPAN, 12), F32)
                last = jnp.concatenate([tail, occ, zero], axis=1).astype(BF16)
                for b in range(4):
                    rows = slice(96 * b, 96 * b + 96)
                    w_ref[4 + 4 * (q // 2) + b, :, 256 * (q % 2):256 * (q % 2) + 256] = head[rows]
                    w_ref[b, :, BLK * q:BLK * q + BLK] = last[rows]
    w_out = pltpu.make_async_copy(w_ref, w_hbm, out_sems.at[1])
    w_out.start()

    for group in (groups - 2, groups - 1):
        pass_group(group, loaded[group])
    for group in range(groups):
        write_group(group).wait()
    code_out.wait()
    w_out.wait()


def prepare(vectors, pairs, count, order, occ, vir, blocks):
    return pl.pallas_call(
        prepare_kernel,
        out_shape=(
            jax.ShapeDtypeStruct((N_VEC * CAP, BLK, BLK), BF16),
            jax.ShapeDtypeStruct((N_VEC, 8, BLK), I32),
            jax.ShapeDtypeStruct(W_SHAPE, BF16),
        ),
        in_specs=[ANY, ANY, pl.BlockSpec(memory_space=pltpu.SMEM), ANY, ANY, ANY, ANY],
        out_specs=(ANY, ANY, ANY),
        scratch_shapes=[
            VMEM((1, SLOTS), I32),
            VMEM((1, SLOTS), I32),
            VMEM((NO,), I32),
            VMEM((NO, SPAN), BF16),
            VMEM((SPAN, NV), BF16),
            VMEM((N_VEC, 8, BLK), I32),
            VMEM(W_SHAPE, BF16),
            VMEM((N_VEC * CAP, BLK, BLK), BF16),
            VMEM((1, SLOTS), I32),
            pltpu.SMEM((1, SLOTS), I32),
            DMA((SLOTS // GROUP,)),
            DMA,
            DMA((5,)),
            DMA((2,)),
        ],
        compiler_params=pltpu.CompilerParams(vmem_limit_bytes=LIMIT),
        name="prepare",
    )(vectors, pairs, count, order, occ, vir, blocks)


def exchange_kernel(send, code, w, recv, code_out, wfull, occ_hbm, tile_bounce, rcode, codes, w_bounce, mine, theirs, occ,
                    lsem, tsend, trecv, csend, crecv, us, ur, ds, dr, os, orc, ol):
    v, z = lax.axis_index("vec"), lax.axis_index("row")
    core, x, y = lax.rem(v, 2), lax.rem(v // 2, 4), v // 8
    up, down = lax.rem(z + 1, N_ROW), lax.rem(z + N_ROW - 1, N_ROW)
    barrier = pltpu.get_barrier_semaphore()

    def greet(i, carry):
        pl.semaphore_signal(barrier, inc=1, device_id=(lax.rem(v + i, N_VEC), z), device_id_type=MESH)
        return carry

    lax.fori_loop(1, N_VEC, greet, 0)
    pl.semaphore_signal(barrier, inc=1, device_id=(v, up), device_id_type=MESH)
    pl.semaphore_signal(barrier, inc=1, device_id=(v, down), device_id_type=MESH)
    pl.semaphore_wait(barrier, N_VEC + 1)

    own = [(send.at[v], tile_bounce, recv.at[v]), (w, w_bounce, wfull.at[z])]
    own_in = [pltpu.make_async_copy(a, b, lsem.at[n]) for n, (a, b, c) in enumerate(own)]
    own_out = [pltpu.make_async_copy(b, c, lsem.at[n]) for n, (a, b, c) in enumerate(own)]
    own_code = pltpu.make_async_copy(code.at[v], rcode.at[v], lsem.at[2])
    own_code.start()
    for copy in own_in:
        copy.start()

    def remote(src, dst, send_sem, recv_sem, device):
        return pltpu.make_async_remote_copy(
            src_ref=src, dst_ref=dst, send_sem=send_sem, recv_sem=recv_sem, device_id=device, device_id_type=MESH
        )

    last = pl.ds(0, 4)

    def swap(origin, src):
        return remote(src.at[last], theirs.at[origin], os.at[origin], orc.at[origin], (v + 1 - 2 * core, z))

    def fetch(origin, src):
        return pltpu.make_async_copy(src.at[last], mine.at[origin], ol.at[origin])

    index = lax.broadcasted_iota(I32, (NO, 512), 0)
    column = lax.broadcasted_iota(I32, (NO, 512), 1)
    lane = column % BLK - (NV_R - 256)
    found = (lane >= 0) & (lane < NO_R)
    wanted = index - NO_R * (column // BLK) - lane
    pick_mine = (found & (wanted == 4 * NO_R * core)).astype(BF16)
    pick_theirs = (found & (wanted == 4 * NO_R * (1 - core))).astype(BF16)
    across = (((1,), (1,)), ((), ()))

    def pick_occ(origin):
        fetch(origin, w).wait()
        swap(origin, w).wait_recv()
        part = lax.dot_general(
            pick_mine, mine[origin].reshape(SPAN, 512), across, preferred_element_type=F32
        ) + lax.dot_general(pick_theirs, theirs[origin].reshape(SPAN, 512), across, preferred_element_type=F32)
        occ[:, pl.ds(pl.multiple_of(origin * SPAN, SPAN), SPAN)] = part.astype(BF16)

    def ring(step, piece, sign):
        origin = lax.rem(z - sign * step + 2 * N_ROW, N_ROW)
        src = w.at[piece] if step == 0 else wfull.at[origin, piece]
        ssem, rsem, to = (us, ur, up) if sign > 0 else (ds, dr, down)
        return remote(src, wfull.at[origin, piece], ssem.at[step * Q + piece], rsem.at[step * Q + piece], (v, to))

    def pieces(step, sign):
        if step < 3:
            return 0, Q
        return (0, Q // 2) if sign > 0 else (Q // 2, Q)

    def first(piece, carry):
        ring(0, piece, 1).start()
        ring(0, piece, -1).start()
        return carry

    lax.fori_loop(0, Q, first, 0)
    swap(z, w).start()
    fetch(z, w).start()

    def target(j):
        return ((y + j // 8) % 4) * 8 + ((x + j // 2) % 4) * 2 + lax.rem(core + j, 2)

    def give(n, carry):
        part = n // (N_VEC - 1)
        j = 1 + lax.rem(n * 11, N_VEC - 1)
        d = target(j)
        spot = pl.ds(part * (CAP // PARTS), CAP // PARTS)
        remote(send.at[d, spot], recv.at[v, spot], tsend, trecv, (d, z)).start()
        return carry

    def give_code(j, carry):
        d = target(j)
        remote(code.at[d], rcode.at[v], csend, crecv, (d, z)).start()
        return carry

    lax.fori_loop(0, PARTS * (N_VEC - 1), give, 0)
    lax.fori_loop(1, N_VEC, give_code, 0)

    for n in range(2):
        own_in[n].wait()
        own_out[n].start()

    def origin_of(step, sign):
        return lax.rem(z - sign * step + N_ROW, N_ROW)

    def pass_occ(step, sign):
        origin = origin_of(step, sign)
        swap(origin, wfull.at[origin]).start()
        fetch(origin, wfull.at[origin]).start()

    for step in range(1, 4):
        for piece in range(Q):
            for sign in (1, -1):
                low, high = pieces(step, sign)
                ring(step - 1, piece, sign).wait_recv()
                if low <= piece < high:
                    ring(step, piece, sign).start()
                if piece == 3:
                    pass_occ(step, sign)
        if step == 2:
            pick_occ(z)
            pick_occ(origin_of(1, 1))
            pick_occ(origin_of(1, -1))
    for piece in range(4):
        ring(3, piece, 1).wait_recv()
    pass_occ(4, 1)
    for step in (2, 3):
        for sign in (1, -1):
            pick_occ(origin_of(step, sign))
    pick_occ(origin_of(4, 1))
    occ_out = pltpu.make_async_copy(occ, occ_hbm, lsem.at[3])
    occ_out.start()
    for sign in (1, -1):
        low, high = pieces(3, sign)
        for piece in range(max(low, 4), high):
            ring(3, piece, sign).wait_recv()
    for sign in (1, -1):
        for step in range(4):
            low, high = pieces(step, sign)
            for piece in range(low, high):
                ring(step, piece, sign).wait_send()
    for origin in range(N_ROW):
        swap(origin, w).wait_send()
    tile_part, code_part = recv.at[pl.ds(0, N_VEC - 1)], rcode.at[pl.ds(0, N_VEC - 1)]
    for part, semaphore in ((tile_part, tsend), (code_part, csend), (tile_part, trecv), (code_part, crecv)):
        pltpu.make_async_copy(part, part, semaphore).wait()
    own_code.wait()
    codes[...] = rcode[:, 0, :]
    codes_out = pltpu.make_async_copy(codes, code_out, lsem.at[2])
    codes_out.start()
    for copy in own_out:
        copy.wait()
    occ_out.wait()
    codes_out.wait()


def exchange(send, code, w):
    return pl.pallas_call(
        exchange_kernel,
        out_shape=(
            jax.ShapeDtypeStruct(send.shape, BF16),
            jax.ShapeDtypeStruct((N_VEC, BLK), I32),
            jax.ShapeDtypeStruct((N_ROW,) + w.shape, BF16),
            jax.ShapeDtypeStruct((NO, NAO), BF16),
        ),
        in_specs=[ANY] * 3,
        out_specs=(ANY,) * 4,
        scratch_shapes=[
            VMEM((CAP, BLK, BLK), BF16),
            VMEM((N_VEC, 8, BLK), I32),
            VMEM((N_VEC, BLK), I32),
            VMEM(W_SHAPE, BF16),
            VMEM((N_ROW, 4) + W_SHAPE[1:], BF16),
            VMEM((N_ROW, 4) + W_SHAPE[1:], BF16),
            VMEM((NO, NAO), BF16),
            DMA((4,)),
        ]
        + [DMA] * 4
        + [DMA((4 * Q,))] * 4
        + [DMA((N_ROW,))] * 3,
        compiler_params=pltpu.CompilerParams(collective_id=0, has_side_effects=True, vmem_limit_bytes=LIMIT),
        name="exchange",
    )(send, code, w)


def half_kernel(code_hbm, tiles_ref, occ_hbm, out_ref, tiles, dense, occ, code_ref, sems, more):
    group = 32
    others = [
        pltpu.make_async_copy(code_hbm, code_ref, more.at[0]),
        pltpu.make_async_copy(occ_hbm, occ, more.at[1]),
    ]
    for load in others:
        load.start()
    loads = [
        pltpu.make_async_copy(
            tiles_ref.at[pl.ds(n * group, group)], tiles.at[pl.ds(n * group, group)], sems.at[n]
        )
        for n in range(SLOTS // group)
    ]
    for load in loads:
        load.start()

    def clear(n, carry):
        dense[n] = jnp.zeros((BLK, NAO), F32)
        return carry

    lax.fori_loop(0, VEC_DEV * TALL, clear, 0)
    for load in others:
        load.wait()

    def place(n, carry):
        for r in range(CAP):
            code = code_ref[n, r] - 1

            @pl.when(code >= 0)
            def _():
                block = lax.shift_right_logical(code, 5)
                column = pl.ds(pl.multiple_of((code & 31) * BLK, BLK), BLK)
                dense[block, :, column] += tiles[n * CAP + r].astype(F32)

        return carry

    for n, load in enumerate(loads):
        load.wait()
        lax.fori_loop(n * group // CAP, (n + 1) * group // CAP, place, 0)

    for pair in range(VEC_DEV * TALL // 2):
        rows = jnp.concatenate([dense[2 * pair], dense[2 * pair + 1]], axis=0).astype(BF16)
        product = lax.dot_general(
            occ[...], rows, (((1,), (1,)), ((), ())), preferred_element_type=F32
        ).astype(BF16)
        for n in range(2):
            j, block = divmod(2 * pair + n, TALL)
            out_ref[j, :, BLK * block:BLK * block + BLK] = product[:, BLK * n:BLK * n + BLK]


def half_transform(code, tiles, occ):
    return pl.pallas_call(
        half_kernel,
        out_shape=jax.ShapeDtypeStruct((VEC_DEV, NO, SPAN), BF16),
        in_specs=[ANY] * 3,
        out_specs=IN_VMEM,
        scratch_shapes=[
            VMEM((SLOTS, BLK, BLK), BF16),
            VMEM((VEC_DEV * TALL, BLK, NAO), F32),
            VMEM((NO, NAO), BF16),
            pltpu.SMEM((N_VEC, BLK), I32),
            DMA((SLOTS // 32,)),
            DMA((2,)),
        ],
        compiler_params=pltpu.CompilerParams(vmem_limit_bytes=LIMIT),
        name="half",
    )(code, tiles, occ)


def finish_kernel(half, w_hbm, taken, w, held, total, picks, chunk, wsem, lsem, hsend, hrecv, ssend, srecv, csend, crecv, x_sem, y_sem):
    v, z = lax.axis_index("vec"), lax.axis_index("row")
    chip, core = v // 2, lax.rem(v, 2)
    giver = z // 4
    takes_own = giver == core
    other = 2 * chip + 1 - core

    loads = [pltpu.make_async_copy(w_hbm.at[r], w.at[r], wsem.at[r]) for r in range(N_ROW)]
    for load in loads:
        load.start()

    barrier = pltpu.get_barrier_semaphore()

    def greet(device):
        pl.semaphore_signal(barrier, inc=1, device_id=device, device_id_type=MESH)

    x, y = lax.rem(chip, 4), chip // 4

    def line(i, carry):
        greet((v, lax.rem(z + i, N_ROW)))
        return carry

    def other_line(i, carry):
        greet((other, lax.rem(z + i, N_ROW)))
        return carry

    def along_x(i):
        return (y * 8 + lax.rem(x + i, 4) * 2 + core, z)

    def along_y(i):
        return (lax.rem(y + i, 4) * 8 + x * 2 + core, z)

    lax.fori_loop(1, N_ROW, line, 0)
    lax.fori_loop(0, N_ROW, other_line, 0)
    for i in range(1, 4):
        greet(along_x(i))
        greet(along_y(i))
    pl.semaphore_wait(barrier, 7 + 8 + 6)
    for i in range(1, 4):
        pl.semaphore_signal(x_sem, inc=1, device_id=along_x(i), device_id_type=MESH)

    def remote(src, dst, send_sem, recv_sem, device):
        return pltpu.make_async_remote_copy(
            src_ref=src, dst_ref=dst, send_sem=send_sem, recv_sem=recv_sem, device_id=device, device_id_type=MESH
        )

    def rows(phase, h):
        return pl.ds(K_HALF * phase + 80 * h, 80 - 16 * h)

    def on_core(h, condition=True):
        return pl.when((core == h) & condition)

    def send_half(phase, j, h):
        return remote(
            half.at[j, rows(phase, h)], held.at[z, rows(phase, h)],
            hsend.at[8 * phase + 2 * j + h], hrecv.at[N_ROW * phase + z], (2 * chip + h, 4 * core + j),
        )

    def not_to_self(j, h):
        return pl.when(jnp.logical_not((4 * core + j == z) & (core == h)))

    def stay(phase, h):
        part = rows(phase, h)
        return pltpu.make_async_copy(half.at[lax.rem(z, 4), part], held.at[z, part], lsem.at[phase])

    for phase in range(2):
        for j in range(4):
            for h in range(2):
                @not_to_self(j, h)
                def _():
                    send_half(phase, j, h).start()

        for h in range(2):
            @on_core(h, takes_own)
            def _():
                stay(phase, h).start()

    def swap(phase, r, h):
        part = rows(phase, h)
        n = N_ROW * phase + r
        return remote(held.at[r, part], held.at[r, part], ssend.at[n], srecv.at[n], (other, z))

    def await_part(part, semaphore):
        pltpu.make_async_copy(part, part, semaphore).wait()

    def pass_on(phase, i):
        r = lax.rem(z + i, N_ROW)
        for h in range(2):
            def arrived_here(phase=phase, h=h):
                await_part(held.at[r, rows(phase, h)], hrecv.at[N_ROW * phase + r])

            if i == 0:
                @on_core(h, takes_own)
                def _():
                    stay(phase, h).wait()

                on_core(h, jnp.logical_not(takes_own))(arrived_here)
            else:
                on_core(h)(arrived_here)

            @on_core(h)
            def _():
                swap(phase, r, h).start()

    def arrived(phase, i):
        r = lax.rem(z + i, N_ROW)
        for h in range(2):
            @on_core(h)
            def _():
                await_part(held.at[r, rows(phase, 1 - h)], srecv.at[N_ROW * phase + r])
        return r

    pl.semaphore_wait(x_sem, 3)
    for i in range(1, 4):
        pl.semaphore_signal(y_sem, inc=1, device_id=along_y(i), device_id_type=MESH)

    height = N_VEC * CHUNK // 2
    row = lax.broadcasted_iota(I32, (height, K_HALF), 0)
    source = lax.broadcasted_iota(I32, (height, K_HALF), 1)
    inside = row % CHUNK
    base = row // CHUNK * NO_V
    for t in range(3):
        picks[t] = ((inside // NO_V == t) & (base + inside % NO_V == source)).astype(BF16)

    place = chip * N_ROW + z

    def start_final(phase):
        def body(i, carry):
            n = lax.rem(i * 37 + v * 4, 2 * N_VEC)
            to, q = n // 4 + N_VEC // 2 * phase, lax.rem(n, 4)
            src = chunk.at[q, pl.ds(pl.multiple_of(to * CHUNK, CHUNK), CHUNK)]
            dst = taken.at[pl.ds(pl.multiple_of(place * CHUNK, CHUNK), CHUNK)]
            device = (to, 4 * core + q)
            own = (to == v) & (device[1] == z)

            @pl.when(jnp.logical_not(own))
            def _():
                remote(src, dst, csend, crecv, device).start()

            @pl.when(own)
            def _():
                pltpu.make_async_copy(src, dst, lsem.at[2]).start()

            return carry

        lax.fori_loop(0, 2 * N_VEC, body, 0)

    sequence = (0, 1, 7, 2, 6, 3, 5, 4)
    for load in loads:
        load.wait()
    for phase in range(2):
        here = slice(K_HALF * phase, K_HALF * phase + K_HALF)
        for n in range(4):
            first, second = sequence[2 * n], sequence[2 * n + 1]
            pass_on(phase, first)
            pass_on(phase, second)
            a, b = arrived(phase, first), arrived(phase, second)
            deep = jnp.concatenate([held[a, here], held[b, here]], axis=1)
            for g in range(3):
                four, cols = slice(4 * g, 4 * g + 4), slice(512 * g, 512 * g + 512)
                block = jnp.concatenate([w[a, four].reshape(SPAN, 512), w[b, four].reshape(SPAN, 512)], axis=0)
                product = jnp.dot(deep, block, preferred_element_type=F32)
                if n == 0:
                    total[:, cols] = product
                else:
                    total[:, cols] += product
        stacked = jnp.zeros((height, 4 * BLK), F32)
        for t in range(3):
            if t < 2:
                addend = jnp.concatenate([total[:, 512 + 256 * q + BLK * t:640 + 256 * q + BLK * t] for q in range(4)], axis=1)
            else:
                addend = total[:, :512]
            stacked = stacked + jnp.dot(picks[t], addend.astype(BF16), preferred_element_type=F32)
        for q in range(4):
            chunk[q, height * phase:height * phase + height] = stacked[:, BLK * q:BLK * q + BLK].astype(BF16)
        if phase == 0:
            pl.semaphore_wait(y_sem, 3)
        start_final(phase)

    for phase in range(2):
        for j in range(4):
            for h in range(2):
                @not_to_self(j, h)
                def _():
                    send_half(phase, j, h).wait_send()

        for h in range(2):
            @on_core(h)
            def _():
                def wait_swap(r, carry):
                    swap(phase, r, h).wait_send()
                    return carry

                lax.fori_loop(0, N_ROW, wait_swap, 0)

    def wait_chunks(count):
        part = taken.at[pl.ds(0, count * CHUNK)]
        pltpu.make_async_copy(part, part, crecv).wait()
        pltpu.make_async_copy(part, part, csend).wait()

    @pl.when(takes_own)
    def _():
        wait_chunks(4 * N_VEC - 1)
        part = taken.at[pl.ds(0, CHUNK)]
        pltpu.make_async_copy(part, part, lsem.at[2]).wait()

    @pl.when(jnp.logical_not(takes_own))
    def _():
        wait_chunks(4 * N_VEC)


def finish(half, w):
    return pl.pallas_call(
        finish_kernel,
        out_shape=jax.ShapeDtypeStruct((BLK * CHUNK, BLK), BF16),
        in_specs=[ANY, ANY],
        out_specs=ANY,
        scratch_shapes=[
            VMEM((N_ROW,) + W_SHAPE, BF16),
            VMEM((N_ROW, NO, SPAN), BF16),
            VMEM((K_HALF, WIDE), F32),
            VMEM((3, N_VEC * CHUNK // 2, K_HALF), BF16),
            VMEM((4, N_VEC * CHUNK, BLK), BF16),
            DMA((N_ROW,)),
            DMA((3,)),
            DMA((2 * 8,)),
            DMA((2 * N_ROW,)),
            DMA((2 * N_ROW,)),
            DMA((2 * N_ROW,)),
            DMA,
            DMA,
            pltpu.SemaphoreType.REGULAR,
            pltpu.SemaphoreType.REGULAR,
        ],
        compiler_params=pltpu.CompilerParams(
            collective_id=1, has_side_effects=True, vmem_limit_bytes=LIMIT
        ),
        name="finish",
    )(half, w)


def arrange_kernel(taken, ov_ref, oo_ref, wide):
    wide[...] = taken[...].astype(F32)
    for t in range(3):
        for k in range(NO_V):
            block = wide[pl.ds(NO_V * t + k, BLK, stride=CHUNK), :].T.astype(BF16)
            if t < 2:
                ov_ref[k, BLK * t:BLK * t + BLK, :] = block
            else:
                ov_ref[k, 256:NV_R, :] = block[:NV_R - 256]
                oo_ref[k] = block[NV_R - 256:W_R - 256 - 12]


def arrange(taken):
    return pl.pallas_call(
        arrange_kernel,
        out_shape=(
            jax.ShapeDtypeStruct((NO_V, NV_R, BLK), BF16),
            jax.ShapeDtypeStruct((NO_V, NO_R, BLK), BF16),
        ),
        in_specs=[IN_VMEM],
        out_specs=(IN_VMEM, IN_VMEM),
        scratch_shapes=[VMEM((BLK * CHUNK, BLK), F32)],
        compiler_params=pltpu.CompilerParams(vmem_limit_bytes=LIMIT),
        name="arrange",
    )(taken)


def on_device(blocks, block_vector, block_pair, block_count, occ_order, occ_coeffs, vir_coeffs):
    send, code, w = prepare(
        block_vector, block_pair, block_count, occ_order, occ_coeffs.T, vir_coeffs, blocks
    )
    tiles, codes, w_all, occ = exchange(send.reshape(N_VEC, CAP, BLK, BLK), code, w)
    half = half_transform(codes, tiles.reshape(SLOTS, BLK, BLK), occ)
    ov, oo = arrange(finish(half, w_all))
    return ov.transpose(1, 0, 2), oo.transpose(1, 0, 2)


def solution(mesh):
    placed = (
        P("vec", "row", None),
        P("row", "vec"),
        P("row", "vec"),
        P("row", "vec"),
        P(),
        P("row", None),
        P("row", None),
    )
    return jax.shard_map(
        on_device,
        mesh=mesh,
        in_specs=placed,
        out_specs=(P("row", "vec", None), P("row", "vec", None)),
        check_vma=False,
    )
```

```python
import jax
import jax.numpy as jnp
from jax import lax
from jax.experimental import pallas as pl
from jax.experimental.pallas import tpu as pltpu
from jax.sharding import PartitionSpec as P

MESH = pl.DeviceIdType.MESH
F32, BF16, I32 = jnp.float32, jnp.bfloat16, jnp.int32

N_VEC, N_ROW, N_CHIP = 32, 8, 16
CAP, SLOTS, BLK = 8, 256, 128
GROUP = 32
NAO, NO, NV, SPAN = 3072, 288, 2688, 384
VEC_DEV, PAIRS, ACROSS, TALL = 4, 72, 24, 3
NV_R, NO_R, NO_V = NV // N_ROW, NO // N_ROW, NO // N_VEC
W_R = 384
WIDE = 4 * W_R
K_HALF = NO // 2
CHUNK = 32
PARTS = 8
Q = 12
W_SHAPE = (Q, SPAN // 4, 512)
VMEM = pltpu.VMEM
LIMIT = 60 * 2**20
ANY = pl.BlockSpec(memory_space=pl.ANY)
IN_VMEM = pl.BlockSpec(memory_space=pltpu.VMEM)
DMA = pltpu.SemaphoreType.DMA


def prepare_kernel(vec_hbm, pair_hbm, count_ref, order_hbm, occ_hbm, vir_hbm, blocks_ref,
                   send_ref, code_hbm, w_hbm, vec_ref, pair_ref, order_ref, occ_ref, vir_ref,
                   code_ref, w_ref, tiles, pos_vmem, pos_smem, sem, pos_sem, in_sems, out_sems):
    loads = [
        pltpu.make_async_copy(src, dst, in_sems.at[n])
        for n, (src, dst) in enumerate(
            ((vec_hbm, vec_ref), (pair_hbm, pair_ref), (order_hbm, order_ref), (occ_hbm, occ_ref), (vir_hbm, vir_ref))
        )
    ]
    for load in loads:
        load.start()
    core = lax.rem(lax.axis_index("vec"), 2)
    count = count_ref[0, 0]
    loads[0].wait()
    vectors = vec_ref[...]
    owner = vectors // VEC_DEV
    above = lax.broadcasted_iota(I32, (SLOTS, SLOTS), 0)
    across = lax.broadcasted_iota(I32, (SLOTS, SLOTS), 1)
    owner_col = jnp.sum(jnp.where(above == across, owner, 0), axis=1, keepdims=True)
    earlier = (owner_col == owner) & (above < across)
    rank = jnp.sum(jnp.where(earlier, 1, 0), axis=0, keepdims=True)
    place = jnp.where(across[:1] < count, owner * CAP + rank, SLOTS)
    place_col = jnp.sum(jnp.where(above == across, place, 0), axis=1, keepdims=True)
    pos_vmem[...] = jnp.sum(jnp.where(place_col == across, above + 1, 0), axis=0, keepdims=True)
    to_smem = pltpu.make_async_copy(pos_vmem, pos_smem, pos_sem)
    to_smem.start()
    to_smem.wait()

    def load_group(group):
        def begin(i, total):
            target = group * GROUP + i
            slot = pos_smem[0, target]

            @pl.when(slot > 0)
            def _():
                pltpu.make_async_copy(blocks_ref.at[slot - 1], tiles.at[target], sem.at[group]).start()

            return total + jnp.where(slot > 0, 1, 0)

        return lax.fori_loop(0, GROUP, begin, 0)

    def write_group(group):
        part = pl.ds(group * GROUP, GROUP)
        return pltpu.make_async_copy(tiles.at[part], send_ref.at[part], sem.at[group])

    def pass_group(group, loaded):
        def end(i, carry):
            pltpu.make_async_copy(blocks_ref.at[0], tiles.at[0], sem.at[group]).wait()
            return carry

        lax.fori_loop(0, loaded, end, 0)
        write_group(group).start()

    groups = SLOTS // GROUP
    loaded = []
    for group in range(groups):
        loaded.append(load_group(group))
        if group >= 2:
            pass_group(group - 2, loaded[group - 2])

    loads[1].wait()
    pairs = pair_ref[...]
    code = (vectors % VEC_DEV * TALL + pairs // ACROSS) * 32 + pairs % ACROSS + 1
    valid = lax.broadcasted_iota(I32, (1, SLOTS), 1) < count
    owners = lax.broadcasted_iota(I32, (N_VEC, SLOTS), 0)
    lane = lax.broadcasted_iota(I32, (N_VEC, BLK), 1)
    mine = (owners == owner) & valid
    table = jnp.zeros((N_VEC, BLK), I32)
    for r in range(CAP):
        picked = jnp.sum(jnp.where(mine & (rank == r), code, 0), axis=1, keepdims=True)
        table = jnp.where(lane == r, picked, table)
    code_ref[...] = jnp.broadcast_to(table[:, None, :], (N_VEC, 8, BLK))
    code_out = pltpu.make_async_copy(code_ref, code_hbm, out_sems.at[0])
    code_out.start()

    for load in loads[2:]:
        load.wait()
    pick = (lax.broadcasted_iota(I32, (NO, NO), 0) == order_ref[...].reshape(1, NO)).astype(BF16)
    perm = lax.dot_general(occ_ref[...], pick, (((0,), (0,)), ((), ())), preferred_element_type=F32)
    for half in range(2):
        @pl.when(core == half)
        def _():
            for q in range(4):
                r = 4 * half + q
                head = vir_ref[:, NV_R * r:NV_R * r + 256]
                tail = vir_ref[:, NV_R * r + 256:NV_R * r + NV_R].astype(F32)
                occ = perm[:, NO_R * r:NO_R * r + NO_R]
                zero = jnp.zeros((SPAN, 12), F32)
                last = jnp.concatenate([tail, occ, zero], axis=1).astype(BF16)
                for b in range(4):
                    rows = slice(96 * b, 96 * b + 96)
                    w_ref[4 + 4 * (q // 2) + b, :, 256 * (q % 2):256 * (q % 2) + 256] = head[rows]
                    w_ref[b, :, BLK * q:BLK * q + BLK] = last[rows]
    w_out = pltpu.make_async_copy(w_ref, w_hbm, out_sems.at[1])
    w_out.start()

    for group in (groups - 2, groups - 1):
        pass_group(group, loaded[group])
    for group in range(groups):
        write_group(group).wait()
    code_out.wait()
    w_out.wait()


def prepare(vectors, pairs, count, order, occ, vir, blocks):
    return pl.pallas_call(
        prepare_kernel,
        out_shape=(
            jax.ShapeDtypeStruct((N_VEC * CAP, BLK, BLK), BF16),
            jax.ShapeDtypeStruct((N_VEC, 8, BLK), I32),
            jax.ShapeDtypeStruct(W_SHAPE, BF16),
        ),
        in_specs=[ANY, ANY, pl.BlockSpec(memory_space=pltpu.SMEM), ANY, ANY, ANY, ANY],
        out_specs=(ANY, ANY, ANY),
        scratch_shapes=[
            VMEM((1, SLOTS), I32),
            VMEM((1, SLOTS), I32),
            VMEM((NO,), I32),
            VMEM((NO, SPAN), BF16),
            VMEM((SPAN, NV), BF16),
            VMEM((N_VEC, 8, BLK), I32),
            VMEM(W_SHAPE, BF16),
            VMEM((N_VEC * CAP, BLK, BLK), BF16),
            VMEM((1, SLOTS), I32),
            pltpu.SMEM((1, SLOTS), I32),
            DMA((SLOTS // GROUP,)),
            DMA,
            DMA((5,)),
            DMA((2,)),
        ],
        compiler_params=pltpu.CompilerParams(vmem_limit_bytes=LIMIT),
        name="prepare",
    )(vectors, pairs, count, order, occ, vir, blocks)


def exchange_kernel(send, code, w, recv, code_out, wfull, occ_hbm, tile_bounce, rcode, codes, w_bounce, mine, theirs, occ,
                    lsem, tsend, trecv, csend, crecv, us, ur, ds, dr, os, orc, ol):
    v, z = lax.axis_index("vec"), lax.axis_index("row")
    core, x, y = lax.rem(v, 2), lax.rem(v // 2, 4), v // 8
    up, down = lax.rem(z + 1, N_ROW), lax.rem(z + N_ROW - 1, N_ROW)
    barrier = pltpu.get_barrier_semaphore()

    def greet(i, carry):
        pl.semaphore_signal(barrier, inc=1, device_id=(lax.rem(v + i, N_VEC), z), device_id_type=MESH)
        return carry

    lax.fori_loop(1, N_VEC, greet, 0)
    pl.semaphore_signal(barrier, inc=1, device_id=(v, up), device_id_type=MESH)
    pl.semaphore_signal(barrier, inc=1, device_id=(v, down), device_id_type=MESH)
    pl.semaphore_wait(barrier, N_VEC + 1)

    own = [(send.at[v], tile_bounce, recv.at[v]), (w, w_bounce, wfull.at[z])]
    own_in = [pltpu.make_async_copy(a, b, lsem.at[n]) for n, (a, b, c) in enumerate(own)]
    own_out = [pltpu.make_async_copy(b, c, lsem.at[n]) for n, (a, b, c) in enumerate(own)]
    own_code = pltpu.make_async_copy(code.at[v], rcode.at[v], lsem.at[2])
    own_code.start()
    for copy in own_in:
        copy.start()

    def remote(src, dst, send_sem, recv_sem, device):
        return pltpu.make_async_remote_copy(
            src_ref=src, dst_ref=dst, send_sem=send_sem, recv_sem=recv_sem, device_id=device, device_id_type=MESH
        )

    last = pl.ds(0, 4)

    def swap(origin, src):
        return remote(src.at[last], theirs.at[origin], os.at[origin], orc.at[origin], (v + 1 - 2 * core, z))

    def fetch(origin, src):
        return pltpu.make_async_copy(src.at[last], mine.at[origin], ol.at[origin])

    line = lax.broadcasted_iota(I32, (NO, 512), 0)
    inner = line % K_HALF
    index = (2 * (inner // NO_V) + line // K_HALF) * NO_V + inner % NO_V
    column = lax.broadcasted_iota(I32, (NO, 512), 1)
    lane = column % BLK - (NV_R - 256)
    found = (lane >= 0) & (lane < NO_R)
    wanted = index - NO_R * (column // BLK) - lane
    pick_mine = (found & (wanted == 4 * NO_R * core)).astype(BF16)
    pick_theirs = (found & (wanted == 4 * NO_R * (1 - core))).astype(BF16)
    across = (((1,), (1,)), ((), ()))

    def pick_occ(origin):
        fetch(origin, w).wait()
        swap(origin, w).wait_recv()
        part = lax.dot_general(
            pick_mine, mine[origin].reshape(SPAN, 512), across, preferred_element_type=F32
        ) + lax.dot_general(pick_theirs, theirs[origin].reshape(SPAN, 512), across, preferred_element_type=F32)
        occ[:, pl.ds(pl.multiple_of(origin * SPAN, SPAN), SPAN)] = part.astype(BF16)

    def ring(step, piece, sign):
        origin = lax.rem(z - sign * step + 2 * N_ROW, N_ROW)
        src = w.at[piece] if step == 0 else wfull.at[origin, piece]
        ssem, rsem, to = (us, ur, up) if sign > 0 else (ds, dr, down)
        return remote(src, wfull.at[origin, piece], ssem.at[step * Q + piece], rsem.at[step * Q + piece], (v, to))

    def pieces(step, sign):
        if step < 3:
            return 0, Q
        return (0, Q // 2) if sign > 0 else (Q // 2, Q)

    def first(piece, carry):
        ring(0, piece, 1).start()
        ring(0, piece, -1).start()
        return carry

    lax.fori_loop(0, Q, first, 0)
    swap(z, w).start()
    fetch(z, w).start()

    def target(j):
        return ((y + j // 8) % 4) * 8 + ((x + j // 2) % 4) * 2 + lax.rem(core + j, 2)

    def give(n, carry):
        part = n // (N_VEC - 1)
        j = 1 + lax.rem(n * 11, N_VEC - 1)
        d = target(j)
        spot = pl.ds(part * (CAP // PARTS), CAP // PARTS)
        remote(send.at[d, spot], recv.at[v, spot], tsend, trecv, (d, z)).start()
        return carry

    def give_code(j, carry):
        d = target(j)
        remote(code.at[d], rcode.at[v], csend, crecv, (d, z)).start()
        return carry

    lax.fori_loop(0, PARTS * (N_VEC - 1), give, 0)
    lax.fori_loop(1, N_VEC, give_code, 0)

    for n in range(2):
        own_in[n].wait()
        own_out[n].start()

    def origin_of(step, sign):
        return lax.rem(z - sign * step + N_ROW, N_ROW)

    def pass_occ(step, sign):
        origin = origin_of(step, sign)
        swap(origin, wfull.at[origin]).start()
        fetch(origin, wfull.at[origin]).start()

    for step in range(1, 4):
        for piece in range(Q):
            for sign in (1, -1):
                low, high = pieces(step, sign)
                ring(step - 1, piece, sign).wait_recv()
                if low <= piece < high:
                    ring(step, piece, sign).start()
                if piece == 3:
                    pass_occ(step, sign)
        if step == 2:
            pick_occ(z)
            pick_occ(origin_of(1, 1))
            pick_occ(origin_of(1, -1))
    for piece in range(4):
        ring(3, piece, 1).wait_recv()
    pass_occ(4, 1)
    for step in (2, 3):
        for sign in (1, -1):
            pick_occ(origin_of(step, sign))
    pick_occ(origin_of(4, 1))
    occ_out = pltpu.make_async_copy(occ, occ_hbm, lsem.at[3])
    occ_out.start()
    for sign in (1, -1):
        low, high = pieces(3, sign)
        for piece in range(max(low, 4), high):
            ring(3, piece, sign).wait_recv()
    for sign in (1, -1):
        for step in range(4):
            low, high = pieces(step, sign)
            for piece in range(low, high):
                ring(step, piece, sign).wait_send()
    for origin in range(N_ROW):
        swap(origin, w).wait_send()
    tile_part, code_part = recv.at[pl.ds(0, N_VEC - 1)], rcode.at[pl.ds(0, N_VEC - 1)]
    for part, semaphore in ((tile_part, tsend), (code_part, csend), (tile_part, trecv), (code_part, crecv)):
        pltpu.make_async_copy(part, part, semaphore).wait()
    own_code.wait()
    codes[...] = rcode[:, 0, :]
    codes_out = pltpu.make_async_copy(codes, code_out, lsem.at[2])
    codes_out.start()
    for copy in own_out:
        copy.wait()
    occ_out.wait()
    codes_out.wait()


def exchange(send, code, w):
    return pl.pallas_call(
        exchange_kernel,
        out_shape=(
            jax.ShapeDtypeStruct(send.shape, BF16),
            jax.ShapeDtypeStruct((N_VEC, BLK), I32),
            jax.ShapeDtypeStruct((N_ROW,) + w.shape, BF16),
            jax.ShapeDtypeStruct((NO, NAO), BF16),
        ),
        in_specs=[ANY] * 3,
        out_specs=(ANY,) * 4,
        scratch_shapes=[
            VMEM((CAP, BLK, BLK), BF16),
            VMEM((N_VEC, 8, BLK), I32),
            VMEM((N_VEC, BLK), I32),
            VMEM(W_SHAPE, BF16),
            VMEM((N_ROW, 4) + W_SHAPE[1:], BF16),
            VMEM((N_ROW, 4) + W_SHAPE[1:], BF16),
            VMEM((NO, NAO), BF16),
            DMA((4,)),
        ]
        + [DMA] * 4
        + [DMA((4 * Q,))] * 4
        + [DMA((N_ROW,))] * 3,
        compiler_params=pltpu.CompilerParams(collective_id=0, has_side_effects=True, vmem_limit_bytes=LIMIT),
        name="exchange",
    )(send, code, w)


def half_kernel(code_hbm, tiles_ref, occ_hbm, out_ref, tiles, dense, occ, code_ref, sems, more):
    group = 32
    others = [
        pltpu.make_async_copy(code_hbm, code_ref, more.at[0]),
        pltpu.make_async_copy(occ_hbm, occ, more.at[1]),
    ]
    for load in others:
        load.start()
    loads = [
        pltpu.make_async_copy(
            tiles_ref.at[pl.ds(n * group, group)], tiles.at[pl.ds(n * group, group)], sems.at[n]
        )
        for n in range(SLOTS // group)
    ]
    for load in loads:
        load.start()

    def clear(n, carry):
        dense[n] = jnp.zeros((BLK, NAO), F32)
        return carry

    lax.fori_loop(0, VEC_DEV * TALL, clear, 0)
    for load in others:
        load.wait()

    def place(n, carry):
        for r in range(CAP):
            code = code_ref[n, r] - 1

            @pl.when(code >= 0)
            def _():
                block = lax.shift_right_logical(code, 5)
                column = pl.ds(pl.multiple_of((code & 31) * BLK, BLK), BLK)
                dense[block, :, column] += tiles[n * CAP + r].astype(F32)

        return carry

    for n, load in enumerate(loads):
        load.wait()
        lax.fori_loop(n * group // CAP, (n + 1) * group // CAP, place, 0)

    for pair in range(VEC_DEV * TALL // 2):
        rows = jnp.concatenate([dense[2 * pair], dense[2 * pair + 1]], axis=0).astype(BF16)
        product = lax.dot_general(
            occ[...], rows, (((1,), (1,)), ((), ())), preferred_element_type=F32
        ).astype(BF16)
        for n in range(2):
            j, block = divmod(2 * pair + n, TALL)
            out_ref[j, :, BLK * block:BLK * block + BLK] = product[:, BLK * n:BLK * n + BLK]


def half_transform(code, tiles, occ):
    return pl.pallas_call(
        half_kernel,
        out_shape=jax.ShapeDtypeStruct((VEC_DEV, NO, SPAN), BF16),
        in_specs=[ANY] * 3,
        out_specs=IN_VMEM,
        scratch_shapes=[
            VMEM((SLOTS, BLK, BLK), BF16),
            VMEM((VEC_DEV * TALL, BLK, NAO), F32),
            VMEM((NO, NAO), BF16),
            pltpu.SMEM((N_VEC, BLK), I32),
            DMA((SLOTS // 32,)),
            DMA((2,)),
        ],
        compiler_params=pltpu.CompilerParams(vmem_limit_bytes=LIMIT),
        name="half",
    )(code, tiles, occ)


def finish_kernel(half, w_hbm, taken, w, held, total, picks, chunk, wsem, lsem, hsend, hrecv, ssend, srecv, csend, crecv, x_sem, y_sem):
    v, z = lax.axis_index("vec"), lax.axis_index("row")
    chip, core = v // 2, lax.rem(v, 2)
    giver = z // 4
    takes_own = giver == core
    other = 2 * chip + 1 - core

    loads = [pltpu.make_async_copy(w_hbm.at[r], w.at[r], wsem.at[r]) for r in range(N_ROW)]
    for load in loads:
        load.start()

    barrier = pltpu.get_barrier_semaphore()

    def greet(device):
        pl.semaphore_signal(barrier, inc=1, device_id=device, device_id_type=MESH)

    x, y = lax.rem(chip, 4), chip // 4

    def line(i, carry):
        greet((v, lax.rem(z + i, N_ROW)))
        return carry

    def other_line(i, carry):
        greet((other, lax.rem(z + i, N_ROW)))
        return carry

    def along_x(i):
        return (y * 8 + lax.rem(x + i, 4) * 2 + core, z)

    def along_y(i):
        return (lax.rem(y + i, 4) * 8 + x * 2 + core, z)

    lax.fori_loop(1, N_ROW, line, 0)
    lax.fori_loop(0, N_ROW, other_line, 0)
    for i in range(1, 4):
        greet(along_x(i))
        greet(along_y(i))
    pl.semaphore_wait(barrier, 7 + 8 + 6)
    for i in range(1, 4):
        pl.semaphore_signal(x_sem, inc=1, device_id=along_x(i), device_id_type=MESH)

    def remote(src, dst, send_sem, recv_sem, device):
        return pltpu.make_async_remote_copy(
            src_ref=src, dst_ref=dst, send_sem=send_sem, recv_sem=recv_sem, device_id=device, device_id_type=MESH
        )

    def rows(phase, h):
        return pl.ds(K_HALF * phase + 80 * h, 80 - 16 * h)

    def on_core(h, condition=True):
        return pl.when((core == h) & condition)

    def send_half(phase, j, h):
        return remote(
            half.at[j, rows(phase, h)], held.at[z, rows(phase, h)],
            hsend.at[8 * phase + 2 * j + h], hrecv.at[N_ROW * phase + z], (2 * chip + h, 4 * core + j),
        )

    def not_to_self(j, h):
        return pl.when(jnp.logical_not((4 * core + j == z) & (core == h)))

    def stay(phase, h):
        part = rows(phase, h)
        return pltpu.make_async_copy(half.at[lax.rem(z, 4), part], held.at[z, part], lsem.at[phase])

    for phase in range(2):
        for turn in range(4):
            j = lax.rem(z + turn, 4)
            for h in range(2):
                @not_to_self(j, h)
                def _():
                    send_half(phase, j, h).start()

        for h in range(2):
            @on_core(h, takes_own)
            def _():
                stay(phase, h).start()

    def swap(phase, r, h):
        part = rows(phase, h)
        n = N_ROW * phase + r
        return remote(held.at[r, part], held.at[r, part], ssend.at[n], srecv.at[n], (other, z))

    def await_part(part, semaphore):
        pltpu.make_async_copy(part, part, semaphore).wait()

    def pass_on(phase, i):
        r = lax.rem(z + i, N_ROW)
        for h in range(2):
            def arrived_here(phase=phase, h=h):
                await_part(held.at[r, rows(phase, h)], hrecv.at[N_ROW * phase + r])

            if i == 0:
                @on_core(h, takes_own)
                def _():
                    stay(phase, h).wait()

                on_core(h, jnp.logical_not(takes_own))(arrived_here)
            else:
                on_core(h)(arrived_here)

            @on_core(h)
            def _():
                swap(phase, r, h).start()

    def arrived(phase, i):
        r = lax.rem(z + i, N_ROW)
        for h in range(2):
            @on_core(h)
            def _():
                await_part(held.at[r, rows(phase, 1 - h)], srecv.at[N_ROW * phase + r])
        return r

    pl.semaphore_wait(x_sem, 3)
    for i in range(1, 4):
        pl.semaphore_signal(y_sem, inc=1, device_id=along_y(i), device_id_type=MESH)

    height = N_VEC * CHUNK // 2
    row = lax.broadcasted_iota(I32, (height, K_HALF), 0)
    source = lax.broadcasted_iota(I32, (height, K_HALF), 1)
    inside = row % CHUNK
    base = row // CHUNK * NO_V
    for t in range(3):
        picks[t] = ((inside // NO_V == t) & (base + inside % NO_V == source)).astype(BF16)

    place = chip * N_ROW + z

    def start_final(phase):
        def body(i, carry):
            n = lax.rem(i * 37 + v * 4, 2 * N_VEC)
            to, q = 2 * (n // 4) + phase, lax.rem(n + z, 4)
            src = chunk.at[q, pl.ds(pl.multiple_of(height * phase + n // 4 * CHUNK, CHUNK), CHUNK)]
            dst = taken.at[pl.ds(pl.multiple_of(place * CHUNK, CHUNK), CHUNK)]
            device = (to, 4 * core + q)
            own = (to == v) & (device[1] == z)

            @pl.when(jnp.logical_not(own))
            def _():
                remote(src, dst, csend, crecv, device).start()

            @pl.when(own)
            def _():
                pltpu.make_async_copy(src, dst, lsem.at[2]).start()

            return carry

        lax.fori_loop(0, 2 * N_VEC, body, 0)

    sequence = (0, 1, 7, 2, 6, 3, 5, 4)
    for load in loads:
        load.wait()
    for phase in range(2):
        here = slice(K_HALF * phase, K_HALF * phase + K_HALF)
        for n in range(4):
            first, second = sequence[2 * n], sequence[2 * n + 1]
            pass_on(phase, first)
            pass_on(phase, second)
            a, b = arrived(phase, first), arrived(phase, second)
            deep = jnp.concatenate([held[a, here], held[b, here]], axis=1)
            for g in range(3):
                four, cols = slice(4 * g, 4 * g + 4), slice(512 * g, 512 * g + 512)
                block = jnp.concatenate([w[a, four].reshape(SPAN, 512), w[b, four].reshape(SPAN, 512)], axis=0)
                product = jnp.dot(deep, block, preferred_element_type=F32)
                if n == 0:
                    total[:, cols] = product
                else:
                    total[:, cols] += product
        stacked = jnp.zeros((height, 4 * BLK), F32)
        for t in range(3):
            if t < 2:
                addend = jnp.concatenate([total[:, 512 + 256 * q + BLK * t:640 + 256 * q + BLK * t] for q in range(4)], axis=1)
            else:
                addend = total[:, :512]
            stacked = stacked + jnp.dot(picks[t], addend.astype(BF16), preferred_element_type=F32)
        for q in range(4):
            chunk[q, height * phase:height * phase + height] = stacked[:, BLK * q:BLK * q + BLK].astype(BF16)
        if phase == 0:
            pl.semaphore_wait(y_sem, 3)
        start_final(phase)

    for phase in range(2):
        for j in range(4):
            for h in range(2):
                @not_to_self(j, h)
                def _():
                    send_half(phase, j, h).wait_send()

        for h in range(2):
            @on_core(h)
            def _():
                def wait_swap(r, carry):
                    swap(phase, r, h).wait_send()
                    return carry

                lax.fori_loop(0, N_ROW, wait_swap, 0)

    def wait_chunks(count):
        part = taken.at[pl.ds(0, count * CHUNK)]
        pltpu.make_async_copy(part, part, crecv).wait()
        pltpu.make_async_copy(part, part, csend).wait()

    @pl.when(takes_own)
    def _():
        wait_chunks(4 * N_VEC - 1)
        part = taken.at[pl.ds(0, CHUNK)]
        pltpu.make_async_copy(part, part, lsem.at[2]).wait()

    @pl.when(jnp.logical_not(takes_own))
    def _():
        wait_chunks(4 * N_VEC)


def finish(half, w):
    return pl.pallas_call(
        finish_kernel,
        out_shape=jax.ShapeDtypeStruct((BLK * CHUNK, BLK), BF16),
        in_specs=[ANY, ANY],
        out_specs=ANY,
        scratch_shapes=[
            VMEM((N_ROW,) + W_SHAPE, BF16),
            VMEM((N_ROW, NO, SPAN), BF16),
            VMEM((K_HALF, WIDE), F32),
            VMEM((3, N_VEC * CHUNK // 2, K_HALF), BF16),
            VMEM((4, N_VEC * CHUNK, BLK), BF16),
            DMA((N_ROW,)),
            DMA((3,)),
            DMA((2 * 8,)),
            DMA((2 * N_ROW,)),
            DMA((2 * N_ROW,)),
            DMA((2 * N_ROW,)),
            DMA,
            DMA,
            pltpu.SemaphoreType.REGULAR,
            pltpu.SemaphoreType.REGULAR,
        ],
        compiler_params=pltpu.CompilerParams(
            collective_id=1, has_side_effects=True, vmem_limit_bytes=LIMIT
        ),
        name="finish",
    )(half, w)


def arrange_kernel(taken, ov_ref, oo_ref, wide):
    wide[...] = taken[...].astype(F32)
    for t in range(3):
        for k in range(NO_V):
            block = wide[pl.ds(NO_V * t + k, BLK, stride=CHUNK), :].T.astype(BF16)
            if t < 2:
                ov_ref[k, BLK * t:BLK * t + BLK, :] = block
            else:
                ov_ref[k, 256:NV_R, :] = block[:NV_R - 256]
                oo_ref[k] = block[NV_R - 256:W_R - 256 - 12]


def arrange(taken):
    return pl.pallas_call(
        arrange_kernel,
        out_shape=(
            jax.ShapeDtypeStruct((NO_V, NV_R, BLK), BF16),
            jax.ShapeDtypeStruct((NO_V, NO_R, BLK), BF16),
        ),
        in_specs=[IN_VMEM],
        out_specs=(IN_VMEM, IN_VMEM),
        scratch_shapes=[VMEM((BLK * CHUNK, BLK), F32)],
        compiler_params=pltpu.CompilerParams(vmem_limit_bytes=LIMIT),
        name="arrange",
    )(taken)


def on_device(blocks, block_vector, block_pair, block_count, occ_order, occ_coeffs, vir_coeffs):
    send, code, w = prepare(
        block_vector, block_pair, block_count, occ_order, occ_coeffs.T, vir_coeffs, blocks
    )
    tiles, codes, w_all, occ = exchange(send.reshape(N_VEC, CAP, BLK, BLK), code, w)
    half = half_transform(codes, tiles.reshape(SLOTS, BLK, BLK), occ)
    ov, oo = arrange(finish(half, w_all))
    return ov.transpose(1, 0, 2), oo.transpose(1, 0, 2)


def solution(mesh):
    placed = (
        P("vec", "row", None),
        P("row", "vec"),
        P("row", "vec"),
        P("row", "vec"),
        P(),
        P("row", None),
        P("row", None),
    )
    return jax.shard_map(
        on_device,
        mesh=mesh,
        in_specs=placed,
        out_specs=(P("row", "vec", None), P("row", "vec", None)),
        check_vma=False,
    )
```

```python
import jax
import jax.numpy as jnp
from jax import lax
from jax.experimental import pallas as pl
from jax.experimental.pallas import tpu as pltpu
from jax.sharding import PartitionSpec as P

MESH = pl.DeviceIdType.MESH
F32, BF16, I32 = jnp.float32, jnp.bfloat16, jnp.int32

N_VEC, N_ROW, N_CHIP = 32, 8, 16
CAP, SLOTS, BLK = 8, 256, 128
NAO, NO, NV, SPAN = 3072, 288, 2688, 384
VEC_DEV, PAIRS, ACROSS, TALL = 4, 72, 24, 3
NV_R, NO_R, NO_V = NV // N_ROW, NO // N_ROW, NO // N_VEC
W_R = 384
WIDE = 4 * W_R
K_HALF = NO // 2
CHUNK = 32
Q = 12
W_SHAPE = (Q, SPAN // 4, 512)
VMEM = pltpu.VMEM
LIMIT = 60 * 2**20
ANY = pl.BlockSpec(memory_space=pl.ANY)
IN_VMEM = pl.BlockSpec(memory_space=pltpu.VMEM)
DMA = pltpu.SemaphoreType.DMA


def prepare_kernel(vec_hbm, pair_hbm, count_ref, order_hbm, occ_hbm, vir_hbm,
                   source_hbm, code_hbm, w_hbm, vec_ref, pair_ref, order_ref, occ_ref, vir_ref,
                   code_ref, w_ref, source_ref, in_sems, out_sems):
    loads = [
        pltpu.make_async_copy(src, dst, in_sems.at[n])
        for n, (src, dst) in enumerate(
            ((vec_hbm, vec_ref), (pair_hbm, pair_ref), (order_hbm, order_ref), (occ_hbm, occ_ref), (vir_hbm, vir_ref))
        )
    ]
    for load in loads:
        load.start()
    core = lax.rem(lax.axis_index("vec"), 2)
    count = count_ref[0, 0]
    loads[0].wait()
    vectors = vec_ref[...]
    owner = vectors // VEC_DEV
    above = lax.broadcasted_iota(I32, (SLOTS, SLOTS), 0)
    across = lax.broadcasted_iota(I32, (SLOTS, SLOTS), 1)
    owner_col = jnp.sum(jnp.where(above == across, owner, 0), axis=1, keepdims=True)
    earlier = (owner_col == owner) & (above < across)
    rank = jnp.sum(jnp.where(earlier, 1, 0), axis=0, keepdims=True)
    place = jnp.where(across[:1] < count, owner * CAP + rank, SLOTS)
    place_col = jnp.sum(jnp.where(above == across, place, 0), axis=1, keepdims=True)
    source = jnp.sum(jnp.where(place_col == across, above, 0), axis=0, keepdims=True)
    source_ref[...] = jnp.broadcast_to(source, (8, SLOTS))
    source_out = pltpu.make_async_copy(source_ref, source_hbm, out_sems.at[2])
    source_out.start()

    loads[1].wait()
    pairs = pair_ref[...]
    code = (vectors % VEC_DEV * TALL + pairs // ACROSS) * 32 + pairs % ACROSS + 1
    valid = lax.broadcasted_iota(I32, (1, SLOTS), 1) < count
    owners = lax.broadcasted_iota(I32, (N_VEC, SLOTS), 0)
    lane = lax.broadcasted_iota(I32, (N_VEC, BLK), 1)
    mine = (owners == owner) & valid
    table = jnp.zeros((N_VEC, BLK), I32)
    for r in range(CAP):
        picked = jnp.sum(jnp.where(mine & (rank == r), code, 0), axis=1, keepdims=True)
        table = jnp.where(lane == r, picked, table)
    code_ref[...] = jnp.broadcast_to(table[:, None, :], (N_VEC, 8, BLK))
    code_out = pltpu.make_async_copy(code_ref, code_hbm, out_sems.at[0])
    code_out.start()

    for load in loads[2:]:
        load.wait()
    pick = (lax.broadcasted_iota(I32, (NO, NO), 0) == order_ref[...].reshape(1, NO)).astype(BF16)
    perm = lax.dot_general(occ_ref[...], pick, (((0,), (0,)), ((), ())), preferred_element_type=F32)
    for half in range(2):
        @pl.when(core == half)
        def _():
            for q in range(4):
                r = 4 * half + q
                head = vir_ref[:, NV_R * r:NV_R * r + 256]
                tail = vir_ref[:, NV_R * r + 256:NV_R * r + NV_R].astype(F32)
                occ = perm[:, NO_R * r:NO_R * r + NO_R]
                zero = jnp.zeros((SPAN, 12), F32)
                last = jnp.concatenate([tail, occ, zero], axis=1).astype(BF16)
                for b in range(4):
                    rows = slice(96 * b, 96 * b + 96)
                    w_ref[4 + 4 * (q // 2) + b, :, 256 * (q % 2):256 * (q % 2) + 256] = head[rows]
                    w_ref[b, :, BLK * q:BLK * q + BLK] = last[rows]
    w_out = pltpu.make_async_copy(w_ref, w_hbm, out_sems.at[1])
    w_out.start()

    source_out.wait()
    code_out.wait()
    w_out.wait()


def prepare(vectors, pairs, count, order, occ, vir):
    return pl.pallas_call(
        prepare_kernel,
        out_shape=(
            jax.ShapeDtypeStruct((8, SLOTS), I32),
            jax.ShapeDtypeStruct((N_VEC, 8, BLK), I32),
            jax.ShapeDtypeStruct(W_SHAPE, BF16),
        ),
        in_specs=[ANY, ANY, pl.BlockSpec(memory_space=pltpu.SMEM), ANY, ANY, ANY],
        out_specs=(ANY, ANY, ANY),
        scratch_shapes=[
            VMEM((1, SLOTS), I32),
            VMEM((1, SLOTS), I32),
            VMEM((NO,), I32),
            VMEM((NO, SPAN), BF16),
            VMEM((SPAN, NV), BF16),
            VMEM((N_VEC, 8, BLK), I32),
            VMEM(W_SHAPE, BF16),
            VMEM((8, SLOTS), I32),
            DMA((5,)),
            DMA((3,)),
        ],
        compiler_params=pltpu.CompilerParams(vmem_limit_bytes=LIMIT),
        name="prepare",
    )(vectors, pairs, count, order, occ, vir)


def exchange_kernel(blocks, source_hbm, code, w, recv, code_out, wfull, occ_hbm, tiles, send, source, rcode, codes, w_bounce, mine, theirs, occ,
                    lsem, tsend, trecv, csend, crecv, us, ur, ds, dr, os, orc, ol):
    v, z = lax.axis_index("vec"), lax.axis_index("row")
    core, x, y = lax.rem(v, 2), lax.rem(v // 2, 4), v // 8
    up, down = lax.rem(z + 1, N_ROW), lax.rem(z + N_ROW - 1, N_ROW)
    tiles_in = pltpu.make_async_copy(blocks, tiles, lsem.at[4])
    source_in = pltpu.make_async_copy(source_hbm, source, lsem.at[5])
    tiles_in.start()
    source_in.start()
    barrier = pltpu.get_barrier_semaphore()

    def greet(i, carry):
        pl.semaphore_signal(barrier, inc=1, device_id=(lax.rem(v + i, N_VEC), z), device_id_type=MESH)
        return carry

    lax.fori_loop(1, N_VEC, greet, 0)
    pl.semaphore_signal(barrier, inc=1, device_id=(v, up), device_id_type=MESH)
    pl.semaphore_signal(barrier, inc=1, device_id=(v, down), device_id_type=MESH)
    pl.semaphore_wait(barrier, N_VEC + 1)

    own_w_in = pltpu.make_async_copy(w, w_bounce, lsem.at[1])
    own_w_out = pltpu.make_async_copy(w_bounce, wfull.at[z], lsem.at[1])
    own_tiles_out = pltpu.make_async_copy(send.at[v], recv.at[v], lsem.at[0])
    own_code = pltpu.make_async_copy(code.at[v], rcode.at[v], lsem.at[2])
    own_code.start()
    own_w_in.start()

    def remote(src, dst, send_sem, recv_sem, device):
        return pltpu.make_async_remote_copy(
            src_ref=src, dst_ref=dst, send_sem=send_sem, recv_sem=recv_sem, device_id=device, device_id_type=MESH
        )

    last = pl.ds(0, 4)

    def swap(origin, src):
        return remote(src.at[last], theirs.at[origin], os.at[origin], orc.at[origin], (v + 1 - 2 * core, z))

    def fetch(origin, src):
        return pltpu.make_async_copy(src.at[last], mine.at[origin], ol.at[origin])

    index = lax.broadcasted_iota(I32, (NO, 512), 0)
    column = lax.broadcasted_iota(I32, (NO, 512), 1)
    lane = column % BLK - (NV_R - 256)
    found = (lane >= 0) & (lane < NO_R)
    wanted = index - NO_R * (column // BLK) - lane
    pick_mine = (found & (wanted == 4 * NO_R * core)).astype(BF16)
    pick_theirs = (found & (wanted == 4 * NO_R * (1 - core))).astype(BF16)
    across = (((1,), (1,)), ((), ()))

    def pick_occ(origin):
        fetch(origin, w).wait()
        swap(origin, w).wait_recv()
        part = lax.dot_general(
            pick_mine, mine[origin].reshape(SPAN, 512), across, preferred_element_type=F32
        ) + lax.dot_general(pick_theirs, theirs[origin].reshape(SPAN, 512), across, preferred_element_type=F32)
        occ[:, pl.ds(pl.multiple_of(origin * SPAN, SPAN), SPAN)] = part.astype(BF16)

    def ring(step, piece, sign):
        origin = lax.rem(z - sign * step + 2 * N_ROW, N_ROW)
        src = w.at[piece] if step == 0 else wfull.at[origin, piece]
        ssem, rsem, to = (us, ur, up) if sign > 0 else (ds, dr, down)
        return remote(src, wfull.at[origin, piece], ssem.at[step * Q + piece], rsem.at[step * Q + piece], (v, to))

    def pieces(step, sign):
        if step < 3:
            return 0, Q
        return (0, Q // 2) if sign > 0 else (Q // 2, Q)

    def first(piece, carry):
        ring(0, piece, 1).start()
        ring(0, piece, -1).start()
        return carry

    lax.fori_loop(0, Q, first, 0)
    swap(z, w).start()
    fetch(z, w).start()

    def target(j):
        return ((y + j // 8) % 4) * 8 + ((x + j // 2) % 4) * 2 + lax.rem(core + j, 2)

    def stage(d, rank):
        send[d, rank] = tiles[source[0, d * CAP + rank]]

    def give(n, carry):
        part = n // (N_VEC - 1)
        j = 1 + lax.rem(n * 11, N_VEC - 1)
        d = target(j)
        stage(d, part)
        remote(send.at[d, part], recv.at[v, part], tsend, trecv, (d, z)).start()
        return carry

    def give_code(j, carry):
        d = target(j)
        remote(code.at[d], rcode.at[v], csend, crecv, (d, z)).start()
        return carry

    tiles_in.wait()
    source_in.wait()
    lax.fori_loop(0, CAP * (N_VEC - 1), give, 0)
    lax.fori_loop(1, N_VEC, give_code, 0)

    def stage_own(rank, carry):
        stage(v, rank)
        return carry

    lax.fori_loop(0, CAP, stage_own, 0)
    own_tiles_out.start()
    own_w_in.wait()
    own_w_out.start()

    def origin_of(step, sign):
        return lax.rem(z - sign * step + N_ROW, N_ROW)

    def pass_occ(step, sign):
        origin = origin_of(step, sign)
        swap(origin, wfull.at[origin]).start()
        fetch(origin, wfull.at[origin]).start()

    for step in range(1, 4):
        for piece in range(Q):
            for sign in (1, -1):
                low, high = pieces(step, sign)
                ring(step - 1, piece, sign).wait_recv()
                if low <= piece < high:
                    ring(step, piece, sign).start()
                if piece == 3:
                    pass_occ(step, sign)
        if step == 2:
            pick_occ(z)
            pick_occ(origin_of(1, 1))
            pick_occ(origin_of(1, -1))
    for piece in range(4):
        ring(3, piece, 1).wait_recv()
    pass_occ(4, 1)
    for step in (2, 3):
        for sign in (1, -1):
            pick_occ(origin_of(step, sign))
    pick_occ(origin_of(4, 1))
    occ_out = pltpu.make_async_copy(occ, occ_hbm, lsem.at[3])
    occ_out.start()
    for sign in (1, -1):
        low, high = pieces(3, sign)
        for piece in range(max(low, 4), high):
            ring(3, piece, sign).wait_recv()
    for sign in (1, -1):
        for step in range(4):
            low, high = pieces(step, sign)
            for piece in range(low, high):
                ring(step, piece, sign).wait_send()
    for origin in range(N_ROW):
        swap(origin, w).wait_send()
    tile_part, code_part = recv.at[pl.ds(0, N_VEC - 1)], rcode.at[pl.ds(0, N_VEC - 1)]
    for part, semaphore in ((tile_part, tsend), (code_part, csend), (tile_part, trecv), (code_part, crecv)):
        pltpu.make_async_copy(part, part, semaphore).wait()
    own_code.wait()
    codes[...] = rcode[:, 0, :]
    codes_out = pltpu.make_async_copy(codes, code_out, lsem.at[2])
    codes_out.start()
    own_tiles_out.wait()
    own_w_out.wait()
    occ_out.wait()
    codes_out.wait()


def exchange(blocks, source, code, w):
    return pl.pallas_call(
        exchange_kernel,
        out_shape=(
            jax.ShapeDtypeStruct((N_VEC, CAP, BLK, BLK), BF16),
            jax.ShapeDtypeStruct((N_VEC, BLK), I32),
            jax.ShapeDtypeStruct((N_ROW,) + w.shape, BF16),
            jax.ShapeDtypeStruct((NO, NAO), BF16),
        ),
        in_specs=[ANY] * 4,
        out_specs=(ANY,) * 4,
        scratch_shapes=[
            VMEM((SLOTS, BLK, BLK), BF16),
            VMEM((N_VEC, CAP, BLK, BLK), BF16),
            pltpu.SMEM((8, SLOTS), I32),
            VMEM((N_VEC, 8, BLK), I32),
            VMEM((N_VEC, BLK), I32),
            VMEM(W_SHAPE, BF16),
            VMEM((N_ROW, 4) + W_SHAPE[1:], BF16),
            VMEM((N_ROW, 4) + W_SHAPE[1:], BF16),
            VMEM((NO, NAO), BF16),
            DMA((6,)),
        ]
        + [DMA] * 4
        + [DMA((4 * Q,))] * 4
        + [DMA((N_ROW,))] * 3,
        compiler_params=pltpu.CompilerParams(collective_id=0, has_side_effects=True, vmem_limit_bytes=LIMIT),
        name="exchange",
    )(blocks, source, code, w)


def half_kernel(code_hbm, tiles_ref, occ_hbm, out_ref, tiles, dense, occ, code_ref, sems, more):
    group = 32
    others = [
        pltpu.make_async_copy(code_hbm, code_ref, more.at[0]),
        pltpu.make_async_copy(occ_hbm, occ, more.at[1]),
    ]
    for load in others:
        load.start()
    loads = [
        pltpu.make_async_copy(
            tiles_ref.at[pl.ds(n * group, group)], tiles.at[pl.ds(n * group, group)], sems.at[n]
        )
        for n in range(SLOTS // group)
    ]
    for load in loads:
        load.start()

    def clear(n, carry):
        dense[n] = jnp.zeros((BLK, NAO), F32)
        return carry

    lax.fori_loop(0, VEC_DEV * TALL, clear, 0)
    for load in others:
        load.wait()

    def place(n, carry):
        for r in range(CAP):
            code = code_ref[n, r] - 1

            @pl.when(code >= 0)
            def _():
                block = lax.shift_right_logical(code, 5)
                column = pl.ds(pl.multiple_of((code & 31) * BLK, BLK), BLK)
                dense[block, :, column] += tiles[n * CAP + r].astype(F32)

        return carry

    for n, load in enumerate(loads):
        load.wait()
        lax.fori_loop(n * group // CAP, (n + 1) * group // CAP, place, 0)

    for pair in range(VEC_DEV * TALL // 2):
        rows = jnp.concatenate([dense[2 * pair], dense[2 * pair + 1]], axis=0).astype(BF16)
        product = lax.dot_general(
            occ[...], rows, (((1,), (1,)), ((), ())), preferred_element_type=F32
        ).astype(BF16)
        for n in range(2):
            j, block = divmod(2 * pair + n, TALL)
            out_ref[j, :, BLK * block:BLK * block + BLK] = product[:, BLK * n:BLK * n + BLK]


def half_transform(code, tiles, occ):
    return pl.pallas_call(
        half_kernel,
        out_shape=jax.ShapeDtypeStruct((VEC_DEV, NO, SPAN), BF16),
        in_specs=[ANY] * 3,
        out_specs=IN_VMEM,
        scratch_shapes=[
            VMEM((SLOTS, BLK, BLK), BF16),
            VMEM((VEC_DEV * TALL, BLK, NAO), F32),
            VMEM((NO, NAO), BF16),
            pltpu.SMEM((N_VEC, BLK), I32),
            DMA((SLOTS // 32,)),
            DMA((2,)),
        ],
        compiler_params=pltpu.CompilerParams(vmem_limit_bytes=LIMIT),
        name="half",
    )(code, tiles, occ)


def finish_kernel(half, w_hbm, taken, w, held, total, picks, chunk, wsem, lsem, hsend, hrecv, ssend, srecv, csend, crecv, x_sem, y_sem):
    v, z = lax.axis_index("vec"), lax.axis_index("row")
    chip, core = v // 2, lax.rem(v, 2)
    giver = z // 4
    takes_own = giver == core
    other = 2 * chip + 1 - core

    loads = [pltpu.make_async_copy(w_hbm.at[r], w.at[r], wsem.at[r]) for r in range(N_ROW)]
    for load in loads:
        load.start()

    barrier = pltpu.get_barrier_semaphore()

    def greet(device):
        pl.semaphore_signal(barrier, inc=1, device_id=device, device_id_type=MESH)

    x, y = lax.rem(chip, 4), chip // 4

    def line(i, carry):
        greet((v, lax.rem(z + i, N_ROW)))
        return carry

    def other_line(i, carry):
        greet((other, lax.rem(z + i, N_ROW)))
        return carry

    def along_x(i):
        return (y * 8 + lax.rem(x + i, 4) * 2 + core, z)

    def along_y(i):
        return (lax.rem(y + i, 4) * 8 + x * 2 + core, z)

    lax.fori_loop(1, N_ROW, line, 0)
    lax.fori_loop(0, N_ROW, other_line, 0)
    for i in range(1, 4):
        greet(along_x(i))
        greet(along_y(i))
    pl.semaphore_wait(barrier, 7 + 8 + 6)
    for i in range(1, 4):
        pl.semaphore_signal(x_sem, inc=1, device_id=along_x(i), device_id_type=MESH)

    def remote(src, dst, send_sem, recv_sem, device):
        return pltpu.make_async_remote_copy(
            src_ref=src, dst_ref=dst, send_sem=send_sem, recv_sem=recv_sem, device_id=device, device_id_type=MESH
        )

    def rows(phase, h):
        return pl.ds(K_HALF * phase + 80 * h, 80 - 16 * h)

    def on_core(h, condition=True):
        return pl.when((core == h) & condition)

    def send_half(phase, j, h):
        return remote(
            half.at[j, rows(phase, h)], held.at[z, rows(phase, h)],
            hsend.at[8 * phase + 2 * j + h], hrecv.at[N_ROW * phase + z], (2 * chip + h, 4 * core + j),
        )

    def not_to_self(j, h):
        return pl.when(jnp.logical_not((4 * core + j == z) & (core == h)))

    def stay(phase, h):
        part = rows(phase, h)
        return pltpu.make_async_copy(half.at[lax.rem(z, 4), part], held.at[z, part], lsem.at[phase])

    for phase in range(2):
        for j in range(4):
            for h in range(2):
                @not_to_self(j, h)
                def _():
                    send_half(phase, j, h).start()

        for h in range(2):
            @on_core(h, takes_own)
            def _():
                stay(phase, h).start()

    def swap(phase, r, h):
        part = rows(phase, h)
        n = N_ROW * phase + r
        return remote(held.at[r, part], held.at[r, part], ssend.at[n], srecv.at[n], (other, z))

    def await_part(part, semaphore):
        pltpu.make_async_copy(part, part, semaphore).wait()

    def pass_on(phase, i):
        r = lax.rem(z + i, N_ROW)
        for h in range(2):
            def arrived_here(phase=phase, h=h):
                await_part(held.at[r, rows(phase, h)], hrecv.at[N_ROW * phase + r])

            if i == 0:
                @on_core(h, takes_own)
                def _():
                    stay(phase, h).wait()

                on_core(h, jnp.logical_not(takes_own))(arrived_here)
            else:
                on_core(h)(arrived_here)

            @on_core(h)
            def _():
                swap(phase, r, h).start()

    def arrived(phase, i):
        r = lax.rem(z + i, N_ROW)
        for h in range(2):
            @on_core(h)
            def _():
                await_part(held.at[r, rows(phase, 1 - h)], srecv.at[N_ROW * phase + r])
        return r

    pl.semaphore_wait(x_sem, 3)
    for i in range(1, 4):
        pl.semaphore_signal(y_sem, inc=1, device_id=along_y(i), device_id_type=MESH)

    height = N_VEC * CHUNK // 2
    row = lax.broadcasted_iota(I32, (height, K_HALF), 0)
    source = lax.broadcasted_iota(I32, (height, K_HALF), 1)
    inside = row % CHUNK
    base = row // CHUNK * NO_V
    for t in range(3):
        picks[t] = ((inside // NO_V == t) & (base + inside % NO_V == source)).astype(BF16)

    place = chip * N_ROW + z

    def start_final(phase):
        def body(i, carry):
            n = lax.rem(i * 37 + v * 4, 2 * N_VEC)
            to, q = n // 4 + N_VEC // 2 * phase, lax.rem(n, 4)
            src = chunk.at[q, pl.ds(pl.multiple_of(to * CHUNK, CHUNK), CHUNK)]
            dst = taken.at[pl.ds(pl.multiple_of(place * CHUNK, CHUNK), CHUNK)]
            device = (to, 4 * core + q)
            own = (to == v) & (device[1] == z)

            @pl.when(jnp.logical_not(own))
            def _():
                remote(src, dst, csend, crecv, device).start()

            @pl.when(own)
            def _():
                pltpu.make_async_copy(src, dst, lsem.at[2]).start()

            return carry

        lax.fori_loop(0, 2 * N_VEC, body, 0)

    sequence = (0, 1, 7, 2, 6, 3, 5, 4)
    for load in loads:
        load.wait()
    for phase in range(2):
        here = slice(K_HALF * phase, K_HALF * phase + K_HALF)
        for n in range(4):
            first, second = sequence[2 * n], sequence[2 * n + 1]
            pass_on(phase, first)
            pass_on(phase, second)
            a, b = arrived(phase, first), arrived(phase, second)
            deep = jnp.concatenate([held[a, here], held[b, here]], axis=1)
            for g in range(3):
                four, cols = slice(4 * g, 4 * g + 4), slice(512 * g, 512 * g + 512)
                block = jnp.concatenate([w[a, four].reshape(SPAN, 512), w[b, four].reshape(SPAN, 512)], axis=0)
                product = jnp.dot(deep, block, preferred_element_type=F32)
                if n == 0:
                    total[:, cols] = product
                else:
                    total[:, cols] += product
        stacked = jnp.zeros((height, 4 * BLK), F32)
        for t in range(3):
            if t < 2:
                addend = jnp.concatenate([total[:, 512 + 256 * q + BLK * t:640 + 256 * q + BLK * t] for q in range(4)], axis=1)
            else:
                addend = total[:, :512]
            stacked = stacked + jnp.dot(picks[t], addend.astype(BF16), preferred_element_type=F32)
        for q in range(4):
            chunk[q, height * phase:height * phase + height] = stacked[:, BLK * q:BLK * q + BLK].astype(BF16)
        if phase == 0:
            pl.semaphore_wait(y_sem, 3)
        start_final(phase)

    for phase in range(2):
        for j in range(4):
            for h in range(2):
                @not_to_self(j, h)
                def _():
                    send_half(phase, j, h).wait_send()

        for h in range(2):
            @on_core(h)
            def _():
                def wait_swap(r, carry):
                    swap(phase, r, h).wait_send()
                    return carry

                lax.fori_loop(0, N_ROW, wait_swap, 0)

    def wait_chunks(count):
        part = taken.at[pl.ds(0, count * CHUNK)]
        pltpu.make_async_copy(part, part, crecv).wait()
        pltpu.make_async_copy(part, part, csend).wait()

    @pl.when(takes_own)
    def _():
        wait_chunks(4 * N_VEC - 1)
        part = taken.at[pl.ds(0, CHUNK)]
        pltpu.make_async_copy(part, part, lsem.at[2]).wait()

    @pl.when(jnp.logical_not(takes_own))
    def _():
        wait_chunks(4 * N_VEC)


def finish(half, w):
    return pl.pallas_call(
        finish_kernel,
        out_shape=jax.ShapeDtypeStruct((BLK * CHUNK, BLK), BF16),
        in_specs=[ANY, ANY],
        out_specs=ANY,
        scratch_shapes=[
            VMEM((N_ROW,) + W_SHAPE, BF16),
            VMEM((N_ROW, NO, SPAN), BF16),
            VMEM((K_HALF, WIDE), F32),
            VMEM((3, N_VEC * CHUNK // 2, K_HALF), BF16),
            VMEM((4, N_VEC * CHUNK, BLK), BF16),
            DMA((N_ROW,)),
            DMA((3,)),
            DMA((2 * 8,)),
            DMA((2 * N_ROW,)),
            DMA((2 * N_ROW,)),
            DMA((2 * N_ROW,)),
            DMA,
            DMA,
            pltpu.SemaphoreType.REGULAR,
            pltpu.SemaphoreType.REGULAR,
        ],
        compiler_params=pltpu.CompilerParams(
            collective_id=1, has_side_effects=True, vmem_limit_bytes=LIMIT
        ),
        name="finish",
    )(half, w)


def arrange_kernel(taken, ov_ref, oo_ref, wide):
    wide[...] = taken[...].astype(F32)
    for t in range(3):
        for k in range(NO_V):
            block = wide[pl.ds(NO_V * t + k, BLK, stride=CHUNK), :].T.astype(BF16)
            if t < 2:
                ov_ref[k, BLK * t:BLK * t + BLK, :] = block
            else:
                ov_ref[k, 256:NV_R, :] = block[:NV_R - 256]
                oo_ref[k] = block[NV_R - 256:W_R - 256 - 12]


def arrange(taken):
    return pl.pallas_call(
        arrange_kernel,
        out_shape=(
            jax.ShapeDtypeStruct((NO_V, NV_R, BLK), BF16),
            jax.ShapeDtypeStruct((NO_V, NO_R, BLK), BF16),
        ),
        in_specs=[IN_VMEM],
        out_specs=(IN_VMEM, IN_VMEM),
        scratch_shapes=[VMEM((BLK * CHUNK, BLK), F32)],
        compiler_params=pltpu.CompilerParams(vmem_limit_bytes=LIMIT),
        name="arrange",
    )(taken)


def on_device(blocks, block_vector, block_pair, block_count, occ_order, occ_coeffs, vir_coeffs):
    source, code, w = prepare(block_vector, block_pair, block_count, occ_order, occ_coeffs.T, vir_coeffs)
    tiles, codes, w_all, occ = exchange(blocks, source, code, w)
    half = half_transform(codes, tiles.reshape(SLOTS, BLK, BLK), occ)
    ov, oo = arrange(finish(half, w_all))
    return ov.transpose(1, 0, 2), oo.transpose(1, 0, 2)


def solution(mesh):
    placed = (
        P("vec", "row", None),
        P("row", "vec"),
        P("row", "vec"),
        P("row", "vec"),
        P(),
        P("row", None),
        P("row", None),
    )
    return jax.shard_map(
        on_device,
        mesh=mesh,
        in_specs=placed,
        out_specs=(P("row", "vec", None), P("row", "vec", None)),
        check_vma=False,
    )
```

```python
import jax
import jax.numpy as jnp
from jax import lax
from jax.experimental import pallas as pl
from jax.experimental.pallas import tpu as pltpu
from jax.sharding import PartitionSpec as P

MESH = pl.DeviceIdType.MESH
F32, BF16, I32 = jnp.float32, jnp.bfloat16, jnp.int32

N_VEC, N_ROW, N_CHIP = 32, 8, 16
CAP, SLOTS, BLK = 8, 256, 128
NAO, NO, NV, SPAN = 3072, 288, 2688, 384
VEC_DEV, PAIRS, ACROSS, TALL = 4, 72, 24, 3
NV_R, NO_R, NO_V = NV // N_ROW, NO // N_ROW, NO // N_VEC
W_R = 384
WIDE = 4 * W_R
K_HALF = NO // 2
CHUNK = 32
Q = 12
W_SHAPE = (Q, SPAN // 4, 512)
VMEM = pltpu.VMEM
LIMIT = 60 * 2**20
ANY = pl.BlockSpec(memory_space=pl.ANY)
IN_VMEM = pl.BlockSpec(memory_space=pltpu.VMEM)
DMA = pltpu.SemaphoreType.DMA


def exchange_kernel(vec_hbm, pair_hbm, count_ref, order_hbm, occ_part, vir_hbm, blocks, recv, code_out, wfull, occ_hbm,
                    vec_ref, pair_ref, order_ref, occ_in, vir_ref, code_ref, w_ref, source_ref,
                    tiles, send, source, rcode, codes, mine, theirs, occ, in_sems,
                    lsem, tsend, trecv, csend, crecv, us, ur, ds, dr, os, orc, ol):
    v, z = lax.axis_index("vec"), lax.axis_index("row")
    core, x, y = lax.rem(v, 2), lax.rem(v // 2, 4), v // 8
    up, down = lax.rem(z + 1, N_ROW), lax.rem(z + N_ROW - 1, N_ROW)
    loads = [
        pltpu.make_async_copy(src, dst, in_sems.at[n])
        for n, (src, dst) in enumerate(
            ((vec_hbm, vec_ref), (pair_hbm, pair_ref), (order_hbm, order_ref), (occ_part, occ_in), (vir_hbm, vir_ref))
        )
    ]
    for load in loads:
        load.start()
    tiles_in = pltpu.make_async_copy(blocks, tiles, lsem.at[4])
    tiles_in.start()
    barrier = pltpu.get_barrier_semaphore()

    def greet(i, carry):
        pl.semaphore_signal(barrier, inc=1, device_id=(lax.rem(v + i, N_VEC), z), device_id_type=MESH)
        return carry

    lax.fori_loop(1, N_VEC, greet, 0)
    pl.semaphore_signal(barrier, inc=1, device_id=(v, up), device_id_type=MESH)
    pl.semaphore_signal(barrier, inc=1, device_id=(v, down), device_id_type=MESH)

    count = count_ref[0, 0]
    loads[0].wait()
    vectors = vec_ref[...]
    owner = vectors // VEC_DEV
    above = lax.broadcasted_iota(I32, (SLOTS, SLOTS), 0)
    across = lax.broadcasted_iota(I32, (SLOTS, SLOTS), 1)
    owner_col = jnp.sum(jnp.where(above == across, owner, 0), axis=1, keepdims=True)
    earlier = (owner_col == owner) & (above < across)
    rank = jnp.sum(jnp.where(earlier, 1, 0), axis=0, keepdims=True)
    place = jnp.where(across[:1] < count, owner * CAP + rank, SLOTS)
    place_col = jnp.sum(jnp.where(above == across, place, 0), axis=1, keepdims=True)
    sources = jnp.sum(jnp.where(place_col == across, above, 0), axis=0, keepdims=True)
    source_ref[...] = jnp.broadcast_to(sources, (8, SLOTS))
    source_in = pltpu.make_async_copy(source_ref, source, lsem.at[5])
    source_in.start()

    loads[1].wait()
    pairs = pair_ref[...]
    code = (vectors % VEC_DEV * TALL + pairs // ACROSS) * 32 + pairs % ACROSS + 1
    valid = lax.broadcasted_iota(I32, (1, SLOTS), 1) < count
    owners = lax.broadcasted_iota(I32, (N_VEC, SLOTS), 0)
    lane = lax.broadcasted_iota(I32, (N_VEC, BLK), 1)
    hits = (owners == owner) & valid
    table = jnp.zeros((N_VEC, BLK), I32)
    for r in range(CAP):
        picked = jnp.sum(jnp.where(hits & (rank == r), code, 0), axis=1, keepdims=True)
        table = jnp.where(lane == r, picked, table)
    code_ref[...] = jnp.broadcast_to(table[:, None, :], (N_VEC, 8, BLK))
    for load in loads[2:]:
        load.wait()
    pick = (lax.broadcasted_iota(I32, (NO, NO), 0) == order_ref[...].reshape(1, NO)).astype(BF16)
    perm = lax.dot_general(occ_in[...], pick, (((0,), (0,)), ((), ())), preferred_element_type=F32)
    for half in range(2):
        @pl.when(core == half)
        def _():
            for q in range(4):
                r = 4 * half + q
                head = vir_ref[:, NV_R * r:NV_R * r + 256]
                tail = vir_ref[:, NV_R * r + 256:NV_R * r + NV_R].astype(F32)
                occ = perm[:, NO_R * r:NO_R * r + NO_R]
                zero = jnp.zeros((SPAN, 12), F32)
                last = jnp.concatenate([tail, occ, zero], axis=1).astype(BF16)
                for b in range(4):
                    rows = slice(96 * b, 96 * b + 96)
                    w_ref[4 + 4 * (q // 2) + b, :, 256 * (q % 2):256 * (q % 2) + 256] = head[rows]
                    w_ref[b, :, BLK * q:BLK * q + BLK] = last[rows]
    code, w = code_ref, w_ref
    pl.semaphore_wait(barrier, N_VEC + 1)

    own_w_out = pltpu.make_async_copy(w, wfull.at[z], lsem.at[1])
    own_tiles_out = pltpu.make_async_copy(send.at[v], recv.at[v], lsem.at[0])
    own_code = pltpu.make_async_copy(code.at[v], rcode.at[v], lsem.at[2])
    own_code.start()
    own_w_out.start()

    def remote(src, dst, send_sem, recv_sem, device):
        return pltpu.make_async_remote_copy(
            src_ref=src, dst_ref=dst, send_sem=send_sem, recv_sem=recv_sem, device_id=device, device_id_type=MESH
        )

    last = pl.ds(0, 4)

    def swap(origin, src):
        return remote(src.at[last], theirs.at[origin], os.at[origin], orc.at[origin], (v + 1 - 2 * core, z))

    def fetch(origin, src):
        return pltpu.make_async_copy(src.at[last], mine.at[origin], ol.at[origin])

    index = lax.broadcasted_iota(I32, (NO, 512), 0)
    column = lax.broadcasted_iota(I32, (NO, 512), 1)
    lane = column % BLK - (NV_R - 256)
    found = (lane >= 0) & (lane < NO_R)
    wanted = index - NO_R * (column // BLK) - lane
    pick_mine = (found & (wanted == 4 * NO_R * core)).astype(BF16)
    pick_theirs = (found & (wanted == 4 * NO_R * (1 - core))).astype(BF16)
    across = (((1,), (1,)), ((), ()))

    def pick_occ(origin):
        fetch(origin, w).wait()
        swap(origin, w).wait_recv()
        part = lax.dot_general(
            pick_mine, mine[origin].reshape(SPAN, 512), across, preferred_element_type=F32
        ) + lax.dot_general(pick_theirs, theirs[origin].reshape(SPAN, 512), across, preferred_element_type=F32)
        occ[:, pl.ds(pl.multiple_of(origin * SPAN, SPAN), SPAN)] = part.astype(BF16)

    def ring(step, piece, sign):
        origin = lax.rem(z - sign * step + 2 * N_ROW, N_ROW)
        src = w.at[piece] if step == 0 else wfull.at[origin, piece]
        ssem, rsem, to = (us, ur, up) if sign > 0 else (ds, dr, down)
        return remote(src, wfull.at[origin, piece], ssem.at[step * Q + piece], rsem.at[step * Q + piece], (v, to))

    def pieces(step, sign):
        if step < 3:
            return 0, Q
        return (0, Q // 2) if sign > 0 else (Q // 2, Q)

    def first(piece, carry):
        ring(0, piece, 1).start()
        ring(0, piece, -1).start()
        return carry

    lax.fori_loop(0, Q, first, 0)
    swap(z, w).start()
    fetch(z, w).start()

    def target(j):
        return ((y + j // 8) % 4) * 8 + ((x + j // 2) % 4) * 2 + lax.rem(core + j, 2)

    def stage(d, rank):
        send[d, rank] = tiles[source[0, d * CAP + rank]]

    def give(n, carry):
        part = n // (N_VEC - 1)
        j = 1 + lax.rem(n * 11, N_VEC - 1)
        d = target(j)
        stage(d, part)
        remote(send.at[d, part], recv.at[v, part], tsend, trecv, (d, z)).start()
        return carry

    def give_code(j, carry):
        d = target(j)
        remote(code.at[d], rcode.at[v], csend, crecv, (d, z)).start()
        return carry

    tiles_in.wait()
    source_in.wait()
    lax.fori_loop(0, CAP * (N_VEC - 1), give, 0)
    lax.fori_loop(1, N_VEC, give_code, 0)

    def stage_own(rank, carry):
        stage(v, rank)
        return carry

    lax.fori_loop(0, CAP, stage_own, 0)
    own_tiles_out.start()

    def origin_of(step, sign):
        return lax.rem(z - sign * step + N_ROW, N_ROW)

    def pass_occ(step, sign):
        origin = origin_of(step, sign)
        swap(origin, wfull.at[origin]).start()
        fetch(origin, wfull.at[origin]).start()

    for step in range(1, 4):
        for piece in range(Q):
            for sign in (1, -1):
                low, high = pieces(step, sign)
                ring(step - 1, piece, sign).wait_recv()
                if low <= piece < high:
                    ring(step, piece, sign).start()
                if piece == 3:
                    pass_occ(step, sign)
        if step == 2:
            pick_occ(z)
            pick_occ(origin_of(1, 1))
            pick_occ(origin_of(1, -1))
    for piece in range(4):
        ring(3, piece, 1).wait_recv()
    pass_occ(4, 1)
    for step in (2, 3):
        for sign in (1, -1):
            pick_occ(origin_of(step, sign))
    pick_occ(origin_of(4, 1))
    occ_out = pltpu.make_async_copy(occ, occ_hbm, lsem.at[3])
    occ_out.start()
    for sign in (1, -1):
        low, high = pieces(3, sign)
        for piece in range(max(low, 4), high):
            ring(3, piece, sign).wait_recv()
    for sign in (1, -1):
        for step in range(4):
            low, high = pieces(step, sign)
            for piece in range(low, high):
                ring(step, piece, sign).wait_send()
    for origin in range(N_ROW):
        swap(origin, w).wait_send()
    tile_part, code_part = recv.at[pl.ds(0, N_VEC - 1)], rcode.at[pl.ds(0, N_VEC - 1)]
    for part, semaphore in ((tile_part, tsend), (code_part, csend), (tile_part, trecv), (code_part, crecv)):
        pltpu.make_async_copy(part, part, semaphore).wait()
    own_code.wait()
    codes[...] = rcode[:, 0, :]
    codes_out = pltpu.make_async_copy(codes, code_out, lsem.at[2])
    codes_out.start()
    own_tiles_out.wait()
    own_w_out.wait()
    occ_out.wait()
    codes_out.wait()


def exchange(vectors, pairs, count, order, occ, vir, blocks):
    return pl.pallas_call(
        exchange_kernel,
        out_shape=(
            jax.ShapeDtypeStruct((N_VEC, CAP, BLK, BLK), BF16),
            jax.ShapeDtypeStruct((N_VEC, BLK), I32),
            jax.ShapeDtypeStruct((N_ROW,) + W_SHAPE, BF16),
            jax.ShapeDtypeStruct((NO, NAO), BF16),
        ),
        in_specs=[ANY, ANY, pl.BlockSpec(memory_space=pltpu.SMEM), ANY, ANY, ANY, ANY],
        out_specs=(ANY,) * 4,
        scratch_shapes=[
            VMEM((1, SLOTS), I32),
            VMEM((1, SLOTS), I32),
            VMEM((NO,), I32),
            VMEM((NO, SPAN), BF16),
            VMEM((SPAN, NV), BF16),
            VMEM((N_VEC, 8, BLK), I32),
            VMEM(W_SHAPE, BF16),
            VMEM((8, SLOTS), I32),
            VMEM((SLOTS, BLK, BLK), BF16),
            VMEM((N_VEC, CAP, BLK, BLK), BF16),
            pltpu.SMEM((8, SLOTS), I32),
            VMEM((N_VEC, 8, BLK), I32),
            VMEM((N_VEC, BLK), I32),
            VMEM((N_ROW, 4) + W_SHAPE[1:], BF16),
            VMEM((N_ROW, 4) + W_SHAPE[1:], BF16),
            VMEM((NO, NAO), BF16),
            DMA((5,)),
            DMA((6,)),
        ]
        + [DMA] * 4
        + [DMA((4 * Q,))] * 4
        + [DMA((N_ROW,))] * 3,
        compiler_params=pltpu.CompilerParams(collective_id=0, has_side_effects=True, vmem_limit_bytes=LIMIT),
        name="exchange",
    )(vectors, pairs, count, order, occ, vir, blocks)


def half_kernel(code_hbm, tiles_ref, occ_hbm, out_ref, tiles, dense, occ, code_ref, sems, more):
    group = 32
    others = [
        pltpu.make_async_copy(code_hbm, code_ref, more.at[0]),
        pltpu.make_async_copy(occ_hbm, occ, more.at[1]),
    ]
    for load in others:
        load.start()
    loads = [
        pltpu.make_async_copy(
            tiles_ref.at[pl.ds(n * group, group)], tiles.at[pl.ds(n * group, group)], sems.at[n]
        )
        for n in range(SLOTS // group)
    ]
    for load in loads:
        load.start()

    def clear(n, carry):
        dense[n] = jnp.zeros((BLK, NAO), F32)
        return carry

    lax.fori_loop(0, VEC_DEV * TALL, clear, 0)
    for load in others:
        load.wait()

    def place(n, carry):
        for r in range(CAP):
            code = code_ref[n, r] - 1

            @pl.when(code >= 0)
            def _():
                block = lax.shift_right_logical(code, 5)
                column = pl.ds(pl.multiple_of((code & 31) * BLK, BLK), BLK)
                dense[block, :, column] += tiles[n * CAP + r].astype(F32)

        return carry

    for n, load in enumerate(loads):
        load.wait()
        lax.fori_loop(n * group // CAP, (n + 1) * group // CAP, place, 0)

    for pair in range(VEC_DEV * TALL // 2):
        rows = jnp.concatenate([dense[2 * pair], dense[2 * pair + 1]], axis=0).astype(BF16)
        product = lax.dot_general(
            occ[...], rows, (((1,), (1,)), ((), ())), preferred_element_type=F32
        ).astype(BF16)
        for n in range(2):
            j, block = divmod(2 * pair + n, TALL)
            out_ref[j, :, BLK * block:BLK * block + BLK] = product[:, BLK * n:BLK * n + BLK]


def half_transform(code, tiles, occ):
    return pl.pallas_call(
        half_kernel,
        out_shape=jax.ShapeDtypeStruct((VEC_DEV, NO, SPAN), BF16),
        in_specs=[ANY] * 3,
        out_specs=IN_VMEM,
        scratch_shapes=[
            VMEM((SLOTS, BLK, BLK), BF16),
            VMEM((VEC_DEV * TALL, BLK, NAO), F32),
            VMEM((NO, NAO), BF16),
            pltpu.SMEM((N_VEC, BLK), I32),
            DMA((SLOTS // 32,)),
            DMA((2,)),
        ],
        compiler_params=pltpu.CompilerParams(vmem_limit_bytes=LIMIT),
        name="half",
    )(code, tiles, occ)


def finish_kernel(half, w_hbm, taken, w, held, total, picks, chunk, wsem, lsem, hsend, hrecv, ssend, srecv, csend, crecv, x_sem, y_sem):
    v, z = lax.axis_index("vec"), lax.axis_index("row")
    chip, core = v // 2, lax.rem(v, 2)
    giver = z // 4
    takes_own = giver == core
    other = 2 * chip + 1 - core

    loads = [pltpu.make_async_copy(w_hbm.at[r], w.at[r], wsem.at[r]) for r in range(N_ROW)]
    for load in loads:
        load.start()

    barrier = pltpu.get_barrier_semaphore()

    def greet(device):
        pl.semaphore_signal(barrier, inc=1, device_id=device, device_id_type=MESH)

    x, y = lax.rem(chip, 4), chip // 4

    def line(i, carry):
        greet((v, lax.rem(z + i, N_ROW)))
        return carry

    def other_line(i, carry):
        greet((other, lax.rem(z + i, N_ROW)))
        return carry

    def along_x(i):
        return (y * 8 + lax.rem(x + i, 4) * 2 + core, z)

    def along_y(i):
        return (lax.rem(y + i, 4) * 8 + x * 2 + core, z)

    lax.fori_loop(1, N_ROW, line, 0)
    lax.fori_loop(0, N_ROW, other_line, 0)
    for i in range(1, 4):
        greet(along_x(i))
        greet(along_y(i))
    pl.semaphore_wait(barrier, 7 + 8 + 6)
    for i in range(1, 4):
        pl.semaphore_signal(x_sem, inc=1, device_id=along_x(i), device_id_type=MESH)

    def remote(src, dst, send_sem, recv_sem, device):
        return pltpu.make_async_remote_copy(
            src_ref=src, dst_ref=dst, send_sem=send_sem, recv_sem=recv_sem, device_id=device, device_id_type=MESH
        )

    def rows(phase, h):
        return pl.ds(K_HALF * phase + 80 * h, 80 - 16 * h)

    def on_core(h, condition=True):
        return pl.when((core == h) & condition)

    def send_half(phase, j, h):
        return remote(
            half.at[j, rows(phase, h)], held.at[z, rows(phase, h)],
            hsend.at[8 * phase + 2 * j + h], hrecv.at[N_ROW * phase + z], (2 * chip + h, 4 * core + j),
        )

    def not_to_self(j, h):
        return pl.when(jnp.logical_not((4 * core + j == z) & (core == h)))

    def stay(phase, h):
        part = rows(phase, h)
        return pltpu.make_async_copy(half.at[lax.rem(z, 4), part], held.at[z, part], lsem.at[phase])

    for phase in range(2):
        for j in range(4):
            for h in range(2):
                @not_to_self(j, h)
                def _():
                    send_half(phase, j, h).start()

        for h in range(2):
            @on_core(h, takes_own)
            def _():
                stay(phase, h).start()

    def swap(phase, r, h):
        part = rows(phase, h)
        n = N_ROW * phase + r
        return remote(held.at[r, part], held.at[r, part], ssend.at[n], srecv.at[n], (other, z))

    def await_part(part, semaphore):
        pltpu.make_async_copy(part, part, semaphore).wait()

    def pass_on(phase, i):
        r = lax.rem(z + i, N_ROW)
        for h in range(2):
            def arrived_here(phase=phase, h=h):
                await_part(held.at[r, rows(phase, h)], hrecv.at[N_ROW * phase + r])

            if i == 0:
                @on_core(h, takes_own)
                def _():
                    stay(phase, h).wait()

                on_core(h, jnp.logical_not(takes_own))(arrived_here)
            else:
                on_core(h)(arrived_here)

            @on_core(h)
            def _():
                swap(phase, r, h).start()

    def arrived(phase, i):
        r = lax.rem(z + i, N_ROW)
        for h in range(2):
            @on_core(h)
            def _():
                await_part(held.at[r, rows(phase, 1 - h)], srecv.at[N_ROW * phase + r])
        return r

    pl.semaphore_wait(x_sem, 3)
    for i in range(1, 4):
        pl.semaphore_signal(y_sem, inc=1, device_id=along_y(i), device_id_type=MESH)

    height = N_VEC * CHUNK // 2
    row = lax.broadcasted_iota(I32, (height, K_HALF), 0)
    source = lax.broadcasted_iota(I32, (height, K_HALF), 1)
    inside = row % CHUNK
    base = row // CHUNK * NO_V
    for t in range(3):
        picks[t] = ((inside // NO_V == t) & (base + inside % NO_V == source)).astype(BF16)

    place = chip * N_ROW + z

    def start_final(phase):
        def body(i, carry):
            n = lax.rem(i * 37 + v * 4, 2 * N_VEC)
            to, q = n // 4 + N_VEC // 2 * phase, lax.rem(n, 4)
            src = chunk.at[q, pl.ds(pl.multiple_of(to * CHUNK, CHUNK), CHUNK)]
            dst = taken.at[pl.ds(pl.multiple_of(place * CHUNK, CHUNK), CHUNK)]
            device = (to, 4 * core + q)
            own = (to == v) & (device[1] == z)

            @pl.when(jnp.logical_not(own))
            def _():
                remote(src, dst, csend, crecv, device).start()

            @pl.when(own)
            def _():
                pltpu.make_async_copy(src, dst, lsem.at[2]).start()

            return carry

        lax.fori_loop(0, 2 * N_VEC, body, 0)

    sequence = (0, 1, 7, 2, 6, 3, 5, 4)
    for load in loads:
        load.wait()
    for phase in range(2):
        here = slice(K_HALF * phase, K_HALF * phase + K_HALF)
        for n in range(4):
            first, second = sequence[2 * n], sequence[2 * n + 1]
            pass_on(phase, first)
            pass_on(phase, second)
            a, b = arrived(phase, first), arrived(phase, second)
            deep = jnp.concatenate([held[a, here], held[b, here]], axis=1)
            for g in range(3):
                four, cols = slice(4 * g, 4 * g + 4), slice(512 * g, 512 * g + 512)
                block = jnp.concatenate([w[a, four].reshape(SPAN, 512), w[b, four].reshape(SPAN, 512)], axis=0)
                product = jnp.dot(deep, block, preferred_element_type=F32)
                if n == 0:
                    total[:, cols] = product
                else:
                    total[:, cols] += product
        stacked = jnp.zeros((height, 4 * BLK), F32)
        for t in range(3):
            if t < 2:
                addend = jnp.concatenate([total[:, 512 + 256 * q + BLK * t:640 + 256 * q + BLK * t] for q in range(4)], axis=1)
            else:
                addend = total[:, :512]
            stacked = stacked + jnp.dot(picks[t], addend.astype(BF16), preferred_element_type=F32)
        for q in range(4):
            chunk[q, height * phase:height * phase + height] = stacked[:, BLK * q:BLK * q + BLK].astype(BF16)
        if phase == 0:
            pl.semaphore_wait(y_sem, 3)
        start_final(phase)

    for phase in range(2):
        for j in range(4):
            for h in range(2):
                @not_to_self(j, h)
                def _():
                    send_half(phase, j, h).wait_send()

        for h in range(2):
            @on_core(h)
            def _():
                def wait_swap(r, carry):
                    swap(phase, r, h).wait_send()
                    return carry

                lax.fori_loop(0, N_ROW, wait_swap, 0)

    def wait_chunks(count):
        part = taken.at[pl.ds(0, count * CHUNK)]
        pltpu.make_async_copy(part, part, crecv).wait()
        pltpu.make_async_copy(part, part, csend).wait()

    @pl.when(takes_own)
    def _():
        wait_chunks(4 * N_VEC - 1)
        part = taken.at[pl.ds(0, CHUNK)]
        pltpu.make_async_copy(part, part, lsem.at[2]).wait()

    @pl.when(jnp.logical_not(takes_own))
    def _():
        wait_chunks(4 * N_VEC)


def finish(half, w):
    return pl.pallas_call(
        finish_kernel,
        out_shape=jax.ShapeDtypeStruct((BLK * CHUNK, BLK), BF16),
        in_specs=[ANY, ANY],
        out_specs=ANY,
        scratch_shapes=[
            VMEM((N_ROW,) + W_SHAPE, BF16),
            VMEM((N_ROW, NO, SPAN), BF16),
            VMEM((K_HALF, WIDE), F32),
            VMEM((3, N_VEC * CHUNK // 2, K_HALF), BF16),
            VMEM((4, N_VEC * CHUNK, BLK), BF16),
            DMA((N_ROW,)),
            DMA((3,)),
            DMA((2 * 8,)),
            DMA((2 * N_ROW,)),
            DMA((2 * N_ROW,)),
            DMA((2 * N_ROW,)),
            DMA,
            DMA,
            pltpu.SemaphoreType.REGULAR,
            pltpu.SemaphoreType.REGULAR,
        ],
        compiler_params=pltpu.CompilerParams(
            collective_id=1, has_side_effects=True, vmem_limit_bytes=LIMIT
        ),
        name="finish",
    )(half, w)


def arrange_kernel(taken, ov_ref, oo_ref, wide):
    wide[...] = taken[...].astype(F32)
    for t in range(3):
        for k in range(NO_V):
            block = wide[pl.ds(NO_V * t + k, BLK, stride=CHUNK), :].T.astype(BF16)
            if t < 2:
                ov_ref[k, BLK * t:BLK * t + BLK, :] = block
            else:
                ov_ref[k, 256:NV_R, :] = block[:NV_R - 256]
                oo_ref[k] = block[NV_R - 256:W_R - 256 - 12]


def arrange(taken):
    return pl.pallas_call(
        arrange_kernel,
        out_shape=(
            jax.ShapeDtypeStruct((NO_V, NV_R, BLK), BF16),
            jax.ShapeDtypeStruct((NO_V, NO_R, BLK), BF16),
        ),
        in_specs=[IN_VMEM],
        out_specs=(IN_VMEM, IN_VMEM),
        scratch_shapes=[VMEM((BLK * CHUNK, BLK), F32)],
        compiler_params=pltpu.CompilerParams(vmem_limit_bytes=LIMIT),
        name="arrange",
    )(taken)


def on_device(blocks, block_vector, block_pair, block_count, occ_order, occ_coeffs, vir_coeffs):
    tiles, codes, w_all, occ = exchange(
        block_vector, block_pair, block_count, occ_order, occ_coeffs.T, vir_coeffs, blocks
    )
    half = half_transform(codes, tiles.reshape(SLOTS, BLK, BLK), occ)
    ov, oo = arrange(finish(half, w_all))
    return ov.transpose(1, 0, 2), oo.transpose(1, 0, 2)


def solution(mesh):
    placed = (
        P("vec", "row", None),
        P("row", "vec"),
        P("row", "vec"),
        P("row", "vec"),
        P(),
        P("row", None),
        P("row", None),
    )
    return jax.shard_map(
        on_device,
        mesh=mesh,
        in_specs=placed,
        out_specs=(P("row", "vec", None), P("row", "vec", None)),
        check_vma=False,
    )
```

```python
import jax
import jax.numpy as jnp
from jax import lax
from jax.experimental import pallas as pl
from jax.experimental.pallas import tpu as pltpu
from jax.sharding import PartitionSpec as P

MESH = pl.DeviceIdType.MESH
F32, BF16, I32 = jnp.float32, jnp.bfloat16, jnp.int32

N_VEC, N_ROW, N_CHIP = 32, 8, 16
CAP, SLOTS, BLK = 8, 256, 128
NAO, NO, NV, SPAN = 3072, 288, 2688, 384
VEC_DEV, PAIRS, ACROSS, TALL = 4, 72, 24, 3
NV_R, NO_R, NO_V = NV // N_ROW, NO // N_ROW, NO // N_VEC
W_R = 384
WIDE = 4 * W_R
K_HALF = NO // 2
CHUNK = 32
Q = 12
W_SHAPE = (Q, SPAN // 4, 512)
VMEM = pltpu.VMEM
LIMIT = 60 * 2**20
ANY = pl.BlockSpec(memory_space=pl.ANY)
IN_VMEM = pl.BlockSpec(memory_space=pltpu.VMEM)
DMA = pltpu.SemaphoreType.DMA


def exchange_kernel(vec_hbm, pair_hbm, count_ref, order_hbm, occ_part, vir_hbm, blocks, recv, code_out, wfull, occ_hbm,
                    vec_ref, pair_ref, order_ref, occ_in, vir_ref, code_ref, w_ref, source_ref,
                    tiles, send, source, rcode, codes, mine, theirs, occ, in_sems,
                    lsem, tsend, trecv, csend, crecv, us, ur, ds, dr, os, orc, ol):
    v, z = lax.axis_index("vec"), lax.axis_index("row")
    core, x, y = lax.rem(v, 2), lax.rem(v // 2, 4), v // 8
    up, down = lax.rem(z + 1, N_ROW), lax.rem(z + N_ROW - 1, N_ROW)
    loads = [
        pltpu.make_async_copy(src, dst, in_sems.at[n])
        for n, (src, dst) in enumerate(
            ((vec_hbm, vec_ref), (pair_hbm, pair_ref), (order_hbm, order_ref), (occ_part, occ_in), (vir_hbm, vir_ref))
        )
    ]
    for load in loads:
        load.start()
    tiles_in = pltpu.make_async_copy(blocks, tiles, lsem.at[4])
    tiles_in.start()
    barrier = pltpu.get_barrier_semaphore()

    def greet(i, carry):
        pl.semaphore_signal(barrier, inc=1, device_id=(lax.rem(v + i, N_VEC), z), device_id_type=MESH)
        return carry

    lax.fori_loop(1, N_VEC, greet, 0)
    pl.semaphore_signal(barrier, inc=1, device_id=(v, up), device_id_type=MESH)
    pl.semaphore_signal(barrier, inc=1, device_id=(v, down), device_id_type=MESH)

    count = count_ref[0, 0]
    loads[0].wait()
    vectors = vec_ref[...]
    owner = vectors // VEC_DEV
    above = lax.broadcasted_iota(I32, (SLOTS, SLOTS), 0)
    across = lax.broadcasted_iota(I32, (SLOTS, SLOTS), 1)
    owner_col = jnp.sum(jnp.where(above == across, owner, 0), axis=1, keepdims=True)
    earlier = (owner_col == owner) & (above < across)
    rank = jnp.sum(jnp.where(earlier, 1, 0), axis=0, keepdims=True)
    place = jnp.where(across[:1] < count, owner * CAP + rank, SLOTS)
    place_col = jnp.sum(jnp.where(above == across, place, 0), axis=1, keepdims=True)
    sources = jnp.sum(jnp.where(place_col == across, above, 0), axis=0, keepdims=True)
    source_ref[...] = jnp.broadcast_to(sources, (8, SLOTS))
    source_in = pltpu.make_async_copy(source_ref, source, lsem.at[5])
    source_in.start()

    loads[1].wait()
    pairs = pair_ref[...]
    code = (vectors % VEC_DEV * TALL + pairs // ACROSS) * 32 + pairs % ACROSS + 1
    valid = lax.broadcasted_iota(I32, (1, SLOTS), 1) < count
    owners = lax.broadcasted_iota(I32, (N_VEC, SLOTS), 0)
    lane = lax.broadcasted_iota(I32, (N_VEC, BLK), 1)
    hits = (owners == owner) & valid
    table = jnp.zeros((N_VEC, BLK), I32)
    for r in range(CAP):
        picked = jnp.sum(jnp.where(hits & (rank == r), code, 0), axis=1, keepdims=True)
        table = jnp.where(lane == r, picked, table)
    code_ref[...] = jnp.broadcast_to(table[:, None, :], (N_VEC, 8, BLK))
    for load in loads[2:]:
        load.wait()
    pick = (lax.broadcasted_iota(I32, (NO, NO), 0) == order_ref[...].reshape(1, NO)).astype(BF16)
    perm = lax.dot_general(occ_in[...], pick, (((0,), (0,)), ((), ())), preferred_element_type=F32)
    for half in range(2):
        @pl.when(core == half)
        def _():
            for q in range(4):
                r = 4 * half + q
                head = vir_ref[:, NV_R * r:NV_R * r + 256]
                tail = vir_ref[:, NV_R * r + 256:NV_R * r + NV_R].astype(F32)
                occ = perm[:, NO_R * r:NO_R * r + NO_R]
                zero = jnp.zeros((SPAN, 12), F32)
                last = jnp.concatenate([tail, occ, zero], axis=1).astype(BF16)
                for b in range(4):
                    rows = slice(96 * b, 96 * b + 96)
                    w_ref[4 + 4 * (q // 2) + b, :, 256 * (q % 2):256 * (q % 2) + 256] = head[rows]
                    w_ref[b, :, BLK * q:BLK * q + BLK] = last[rows]
    code, w = code_ref, w_ref
    pl.semaphore_wait(barrier, N_VEC + 1)

    own_w_out = pltpu.make_async_copy(w, wfull.at[z], lsem.at[1])
    own_tiles_out = pltpu.make_async_copy(send.at[v], recv.at[v], lsem.at[0])
    own_code = pltpu.make_async_copy(code.at[v], rcode.at[v], lsem.at[2])
    own_code.start()
    own_w_out.start()

    def remote(src, dst, send_sem, recv_sem, device):
        return pltpu.make_async_remote_copy(
            src_ref=src, dst_ref=dst, send_sem=send_sem, recv_sem=recv_sem, device_id=device, device_id_type=MESH
        )

    last = pl.ds(0, 4)

    def swap(origin, src):
        return remote(src.at[last], theirs.at[origin], os.at[origin], orc.at[origin], (v + 1 - 2 * core, z))

    def fetch(origin, src):
        return pltpu.make_async_copy(src.at[last], mine.at[origin], ol.at[origin])

    index = lax.broadcasted_iota(I32, (NO, 512), 0)
    column = lax.broadcasted_iota(I32, (NO, 512), 1)
    lane = column % BLK - (NV_R - 256)
    found = (lane >= 0) & (lane < NO_R)
    wanted = index - NO_R * (column // BLK) - lane
    pick_mine = (found & (wanted == 4 * NO_R * core)).astype(BF16)
    pick_theirs = (found & (wanted == 4 * NO_R * (1 - core))).astype(BF16)
    across = (((1,), (1,)), ((), ()))

    def pick_occ(origin):
        fetch(origin, w).wait()
        swap(origin, w).wait_recv()
        part = lax.dot_general(
            pick_mine, mine[origin].reshape(SPAN, 512), across, preferred_element_type=F32
        ) + lax.dot_general(pick_theirs, theirs[origin].reshape(SPAN, 512), across, preferred_element_type=F32)
        occ[:, pl.ds(pl.multiple_of(origin * SPAN, SPAN), SPAN)] = part.astype(BF16)

    def ring(step, piece, sign):
        origin = lax.rem(z - sign * step + 2 * N_ROW, N_ROW)
        src = w.at[piece] if step == 0 else wfull.at[origin, piece]
        ssem, rsem, to = (us, ur, up) if sign > 0 else (ds, dr, down)
        return remote(src, wfull.at[origin, piece], ssem.at[step * Q + piece], rsem.at[step * Q + piece], (v, to))

    def pieces(step, sign):
        if step < 3:
            return 0, Q
        return (0, Q // 2) if sign > 0 else (Q // 2, Q)

    def first(piece, carry):
        ring(0, piece, 1).start()
        ring(0, piece, -1).start()
        return carry

    lax.fori_loop(0, Q, first, 0)
    swap(z, w).start()
    fetch(z, w).start()

    def target(j):
        return ((y + j // 8) % 4) * 8 + ((x + j // 2) % 4) * 2 + lax.rem(core + j, 2)

    def stage(d, rank):
        send[d, rank] = tiles[source[0, d * CAP + rank]]

    def give(n, carry):
        part = n // (N_VEC - 1)
        j = 1 + lax.rem(n * 11, N_VEC - 1)
        d = target(j)
        stage(d, part)
        remote(send.at[d, part], recv.at[v, part], tsend, trecv, (d, z)).start()
        return carry

    def give_code(j, carry):
        d = target(j)
        remote(code.at[d], rcode.at[v], csend, crecv, (d, z)).start()
        return carry

    tiles_in.wait()
    source_in.wait()
    lax.fori_loop(0, CAP * (N_VEC - 1), give, 0)
    lax.fori_loop(1, N_VEC, give_code, 0)

    def stage_own(rank, carry):
        stage(v, rank)
        return carry

    lax.fori_loop(0, CAP, stage_own, 0)
    own_tiles_out.start()

    def origin_of(step, sign):
        return lax.rem(z - sign * step + N_ROW, N_ROW)

    def pass_occ(step, sign):
        origin = origin_of(step, sign)
        swap(origin, wfull.at[origin]).start()
        fetch(origin, wfull.at[origin]).start()

    for step in range(1, 4):
        for piece in range(Q):
            for sign in (1, -1):
                low, high = pieces(step, sign)
                ring(step - 1, piece, sign).wait_recv()
                if low <= piece < high:
                    ring(step, piece, sign).start()
                if piece == 3:
                    pass_occ(step, sign)
        if step == 2:
            pick_occ(z)
            pick_occ(origin_of(1, 1))
            pick_occ(origin_of(1, -1))
    for piece in range(4):
        ring(3, piece, 1).wait_recv()
    pass_occ(4, 1)
    for step in (2, 3):
        for sign in (1, -1):
            pick_occ(origin_of(step, sign))
    pick_occ(origin_of(4, 1))
    occ_out = pltpu.make_async_copy(occ, occ_hbm, lsem.at[3])
    occ_out.start()
    for sign in (1, -1):
        low, high = pieces(3, sign)
        for piece in range(max(low, 4), high):
            ring(3, piece, sign).wait_recv()
    for sign in (1, -1):
        for step in range(4):
            low, high = pieces(step, sign)
            for piece in range(low, high):
                ring(step, piece, sign).wait_send()
    for origin in range(N_ROW):
        swap(origin, w).wait_send()
    tile_part, code_part = recv.at[pl.ds(0, N_VEC - 1)], rcode.at[pl.ds(0, N_VEC - 1)]
    for part, semaphore in ((tile_part, tsend), (code_part, csend), (tile_part, trecv), (code_part, crecv)):
        pltpu.make_async_copy(part, part, semaphore).wait()
    own_code.wait()
    codes[...] = rcode[:, 0, :]
    codes_out = pltpu.make_async_copy(codes, code_out, lsem.at[2])
    codes_out.start()
    own_tiles_out.wait()
    own_w_out.wait()
    occ_out.wait()
    codes_out.wait()


def exchange(vectors, pairs, count, order, occ, vir, blocks):
    return pl.pallas_call(
        exchange_kernel,
        out_shape=(
            jax.ShapeDtypeStruct((N_VEC, CAP, BLK, BLK), BF16),
            jax.ShapeDtypeStruct((N_VEC, BLK), I32),
            jax.ShapeDtypeStruct((N_ROW,) + W_SHAPE, BF16),
            jax.ShapeDtypeStruct((NO, NAO), BF16),
        ),
        in_specs=[ANY, ANY, pl.BlockSpec(memory_space=pltpu.SMEM), ANY, ANY, ANY, ANY],
        out_specs=(ANY,) * 4,
        scratch_shapes=[
            VMEM((1, SLOTS), I32),
            VMEM((1, SLOTS), I32),
            VMEM((NO,), I32),
            VMEM((NO, SPAN), BF16),
            VMEM((SPAN, NV), BF16),
            VMEM((N_VEC, 8, BLK), I32),
            VMEM(W_SHAPE, BF16),
            VMEM((8, SLOTS), I32),
            VMEM((SLOTS, BLK, BLK), BF16),
            VMEM((N_VEC, CAP, BLK, BLK), BF16),
            pltpu.SMEM((8, SLOTS), I32),
            VMEM((N_VEC, 8, BLK), I32),
            VMEM((N_VEC, BLK), I32),
            VMEM((N_ROW, 4) + W_SHAPE[1:], BF16),
            VMEM((N_ROW, 4) + W_SHAPE[1:], BF16),
            VMEM((NO, NAO), BF16),
            DMA((5,)),
            DMA((6,)),
        ]
        + [DMA] * 4
        + [DMA((4 * Q,))] * 4
        + [DMA((N_ROW,))] * 3,
        compiler_params=pltpu.CompilerParams(collective_id=0, has_side_effects=True, vmem_limit_bytes=LIMIT),
        name="exchange",
    )(vectors, pairs, count, order, occ, vir, blocks)


def half_kernel(code_hbm, tiles_ref, occ_hbm, out_ref, tiles, dense, occ, code_ref, sems, more):
    group = 64
    others = [
        pltpu.make_async_copy(code_hbm, code_ref, more.at[0]),
        pltpu.make_async_copy(occ_hbm, occ, more.at[1]),
    ]
    for load in others:
        load.start()
    loads = [
        pltpu.make_async_copy(
            tiles_ref.at[pl.ds(n * group, group)], tiles.at[pl.ds(n * group, group)], sems.at[n]
        )
        for n in range(SLOTS // group)
    ]
    for load in loads:
        load.start()

    def clear(n, carry):
        dense[n] = jnp.zeros((BLK, NAO), F32)
        return carry

    lax.fori_loop(0, VEC_DEV * TALL, clear, 0)
    for load in others:
        load.wait()

    def place(n, carry):
        for r in range(CAP):
            code = code_ref[n, r] - 1

            @pl.when(code >= 0)
            def _():
                block = lax.shift_right_logical(code, 5)
                column = pl.ds(pl.multiple_of((code & 31) * BLK, BLK), BLK)
                dense[block, :, column] += tiles[n * CAP + r].astype(F32)

        return carry

    for n, load in enumerate(loads):
        load.wait()
        lax.fori_loop(n * group // CAP, (n + 1) * group // CAP, place, 0)

    for pair in range(VEC_DEV * TALL // 2):
        rows = jnp.concatenate([dense[2 * pair], dense[2 * pair + 1]], axis=0).astype(BF16)
        product = lax.dot_general(
            occ[...], rows, (((1,), (1,)), ((), ())), preferred_element_type=F32
        ).astype(BF16)
        for n in range(2):
            j, block = divmod(2 * pair + n, TALL)
            out_ref[j, :, BLK * block:BLK * block + BLK] = product[:, BLK * n:BLK * n + BLK]


def half_transform(code, tiles, occ):
    return pl.pallas_call(
        half_kernel,
        out_shape=jax.ShapeDtypeStruct((VEC_DEV, NO, SPAN), BF16),
        in_specs=[ANY] * 3,
        out_specs=IN_VMEM,
        scratch_shapes=[
            VMEM((SLOTS, BLK, BLK), BF16),
            VMEM((VEC_DEV * TALL, BLK, NAO), F32),
            VMEM((NO, NAO), BF16),
            pltpu.SMEM((N_VEC, BLK), I32),
            DMA((SLOTS // 64,)),
            DMA((2,)),
        ],
        compiler_params=pltpu.CompilerParams(vmem_limit_bytes=LIMIT),
        name="half",
    )(code, tiles, occ)


def finish_kernel(half, w_hbm, taken, w, held, total, picks, chunk, wsem, lsem, hsend, hrecv, ssend, srecv, csend, crecv, x_sem, y_sem):
    v, z = lax.axis_index("vec"), lax.axis_index("row")
    chip, core = v // 2, lax.rem(v, 2)
    giver = z // 4
    takes_own = giver == core
    other = 2 * chip + 1 - core

    loads = [pltpu.make_async_copy(w_hbm.at[r], w.at[r], wsem.at[r]) for r in range(N_ROW)]
    for load in loads:
        load.start()

    barrier = pltpu.get_barrier_semaphore()

    def greet(device):
        pl.semaphore_signal(barrier, inc=1, device_id=device, device_id_type=MESH)

    x, y = lax.rem(chip, 4), chip // 4

    def line(i, carry):
        greet((v, lax.rem(z + i, N_ROW)))
        return carry

    def other_line(i, carry):
        greet((other, lax.rem(z + i, N_ROW)))
        return carry

    def along_x(i):
        return (y * 8 + lax.rem(x + i, 4) * 2 + core, z)

    def along_y(i):
        return (lax.rem(y + i, 4) * 8 + x * 2 + core, z)

    lax.fori_loop(1, N_ROW, line, 0)
    lax.fori_loop(0, N_ROW, other_line, 0)
    for i in range(1, 4):
        greet(along_x(i))
        greet(along_y(i))
    pl.semaphore_wait(barrier, 7 + 8 + 6)
    for i in range(1, 4):
        pl.semaphore_signal(x_sem, inc=1, device_id=along_x(i), device_id_type=MESH)

    def remote(src, dst, send_sem, recv_sem, device):
        return pltpu.make_async_remote_copy(
            src_ref=src, dst_ref=dst, send_sem=send_sem, recv_sem=recv_sem, device_id=device, device_id_type=MESH
        )

    def rows(phase, h):
        return pl.ds(K_HALF * phase + 80 * h, 80 - 16 * h)

    def on_core(h, condition=True):
        return pl.when((core == h) & condition)

    def send_half(phase, j, h):
        return remote(
            half.at[j, rows(phase, h)], held.at[z, rows(phase, h)],
            hsend.at[8 * phase + 2 * j + h], hrecv.at[N_ROW * phase + z], (2 * chip + h, 4 * core + j),
        )

    def not_to_self(j, h):
        return pl.when(jnp.logical_not((4 * core + j == z) & (core == h)))

    def stay(phase, h):
        part = rows(phase, h)
        return pltpu.make_async_copy(half.at[lax.rem(z, 4), part], held.at[z, part], lsem.at[phase])

    for phase in range(2):
        for j in range(4):
            for h in range(2):
                @not_to_self(j, h)
                def _():
                    send_half(phase, j, h).start()

        for h in range(2):
            @on_core(h, takes_own)
            def _():
                stay(phase, h).start()

    def swap(phase, r, h):
        part = rows(phase, h)
        n = N_ROW * phase + r
        return remote(held.at[r, part], held.at[r, part], ssend.at[n], srecv.at[n], (other, z))

    def await_part(part, semaphore):
        pltpu.make_async_copy(part, part, semaphore).wait()

    def pass_on(phase, i):
        r = lax.rem(z + i, N_ROW)
        for h in range(2):
            def arrived_here(phase=phase, h=h):
                await_part(held.at[r, rows(phase, h)], hrecv.at[N_ROW * phase + r])

            if i == 0:
                @on_core(h, takes_own)
                def _():
                    stay(phase, h).wait()

                on_core(h, jnp.logical_not(takes_own))(arrived_here)
            else:
                on_core(h)(arrived_here)

            @on_core(h)
            def _():
                swap(phase, r, h).start()

    def arrived(phase, i):
        r = lax.rem(z + i, N_ROW)
        for h in range(2):
            @on_core(h)
            def _():
                await_part(held.at[r, rows(phase, 1 - h)], srecv.at[N_ROW * phase + r])
        return r

    pl.semaphore_wait(x_sem, 3)
    for i in range(1, 4):
        pl.semaphore_signal(y_sem, inc=1, device_id=along_y(i), device_id_type=MESH)

    height = N_VEC * CHUNK // 2
    row = lax.broadcasted_iota(I32, (height, K_HALF), 0)
    source = lax.broadcasted_iota(I32, (height, K_HALF), 1)
    inside = row % CHUNK
    base = row // CHUNK * NO_V
    for t in range(3):
        picks[t] = ((inside // NO_V == t) & (base + inside % NO_V == source)).astype(BF16)

    place = chip * N_ROW + z

    def start_final(phase):
        def body(i, carry):
            n = lax.rem(i * 37 + v * 4, 2 * N_VEC)
            to, q = n // 4 + N_VEC // 2 * phase, lax.rem(n, 4)
            src = chunk.at[q, pl.ds(pl.multiple_of(to * CHUNK, CHUNK), CHUNK)]
            dst = taken.at[pl.ds(pl.multiple_of(place * CHUNK, CHUNK), CHUNK)]
            device = (to, 4 * core + q)
            own = (to == v) & (device[1] == z)

            @pl.when(jnp.logical_not(own))
            def _():
                remote(src, dst, csend, crecv, device).start()

            @pl.when(own)
            def _():
                pltpu.make_async_copy(src, dst, lsem.at[2]).start()

            return carry

        lax.fori_loop(0, 2 * N_VEC, body, 0)

    sequence = (0, 1, 7, 2, 6, 3, 5, 4)
    for load in loads:
        load.wait()
    for phase in range(2):
        here = slice(K_HALF * phase, K_HALF * phase + K_HALF)
        for n in range(4):
            first, second = sequence[2 * n], sequence[2 * n + 1]
            pass_on(phase, first)
            pass_on(phase, second)
            a, b = arrived(phase, first), arrived(phase, second)
            deep = jnp.concatenate([held[a, here], held[b, here]], axis=1)
            for g in range(3):
                four, cols = slice(4 * g, 4 * g + 4), slice(512 * g, 512 * g + 512)
                block = jnp.concatenate([w[a, four].reshape(SPAN, 512), w[b, four].reshape(SPAN, 512)], axis=0)
                product = jnp.dot(deep, block, preferred_element_type=F32)
                if n == 0:
                    total[:, cols] = product
                else:
                    total[:, cols] += product
        stacked = jnp.zeros((height, 4 * BLK), F32)
        for t in range(3):
            if t < 2:
                addend = jnp.concatenate([total[:, 512 + 256 * q + BLK * t:640 + 256 * q + BLK * t] for q in range(4)], axis=1)
            else:
                addend = total[:, :512]
            stacked = stacked + jnp.dot(picks[t], addend.astype(BF16), preferred_element_type=F32)
        for q in range(4):
            chunk[q, height * phase:height * phase + height] = stacked[:, BLK * q:BLK * q + BLK].astype(BF16)
        if phase == 0:
            pl.semaphore_wait(y_sem, 3)
        start_final(phase)

    for phase in range(2):
        for j in range(4):
            for h in range(2):
                @not_to_self(j, h)
                def _():
                    send_half(phase, j, h).wait_send()

        for h in range(2):
            @on_core(h)
            def _():
                def wait_swap(r, carry):
                    swap(phase, r, h).wait_send()
                    return carry

                lax.fori_loop(0, N_ROW, wait_swap, 0)

    def wait_chunks(count):
        part = taken.at[pl.ds(0, count * CHUNK)]
        pltpu.make_async_copy(part, part, crecv).wait()
        pltpu.make_async_copy(part, part, csend).wait()

    @pl.when(takes_own)
    def _():
        wait_chunks(4 * N_VEC - 1)
        part = taken.at[pl.ds(0, CHUNK)]
        pltpu.make_async_copy(part, part, lsem.at[2]).wait()

    @pl.when(jnp.logical_not(takes_own))
    def _():
        wait_chunks(4 * N_VEC)


def finish(half, w):
    return pl.pallas_call(
        finish_kernel,
        out_shape=jax.ShapeDtypeStruct((BLK * CHUNK, BLK), BF16),
        in_specs=[ANY, ANY],
        out_specs=ANY,
        scratch_shapes=[
            VMEM((N_ROW,) + W_SHAPE, BF16),
            VMEM((N_ROW, NO, SPAN), BF16),
            VMEM((K_HALF, WIDE), F32),
            VMEM((3, N_VEC * CHUNK // 2, K_HALF), BF16),
            VMEM((4, N_VEC * CHUNK, BLK), BF16),
            DMA((N_ROW,)),
            DMA((3,)),
            DMA((2 * 8,)),
            DMA((2 * N_ROW,)),
            DMA((2 * N_ROW,)),
            DMA((2 * N_ROW,)),
            DMA,
            DMA,
            pltpu.SemaphoreType.REGULAR,
            pltpu.SemaphoreType.REGULAR,
        ],
        compiler_params=pltpu.CompilerParams(
            collective_id=1, has_side_effects=True, vmem_limit_bytes=LIMIT
        ),
        name="finish",
    )(half, w)


def arrange_kernel(taken_hbm, ov_hbm, oo_hbm, taken, ov, oo, wide, in_sems, ov_sems, oo_sems):
    pieces = 4
    height = BLK * CHUNK // pieces
    loads = []
    for n in range(pieces):
        part = pl.ds(n * height, height)
        loads.append(pltpu.make_async_copy(taken_hbm.at[part], taken.at[part], in_sems.at[n]))
        loads[n].start()
    for n in range(pieces):
        loads[n].wait()
        wide[n * height:n * height + height] = taken[n * height:n * height + height].astype(F32)
    writes = []
    for k in range(NO_V):
        for t in range(3):
            block = wide[pl.ds(NO_V * t + k, BLK, stride=CHUNK), :].T.astype(BF16)
            if t < 2:
                ov[k, BLK * t:BLK * t + BLK, :] = block
            else:
                ov[k, 256:NV_R, :] = block[:NV_R - 256]
                oo[k] = block[NV_R - 256:W_R - 256 - 12]
        for source, target, sems in ((ov, ov_hbm, ov_sems), (oo, oo_hbm, oo_sems)):
            writes.append(pltpu.make_async_copy(source.at[k], target.at[k], sems.at[k]))
            writes[-1].start()
    for write in writes:
        write.wait()


def arrange(taken):
    return pl.pallas_call(
        arrange_kernel,
        out_shape=(
            jax.ShapeDtypeStruct((NO_V, NV_R, BLK), BF16),
            jax.ShapeDtypeStruct((NO_V, NO_R, BLK), BF16),
        ),
        in_specs=[ANY],
        out_specs=(ANY, ANY),
        scratch_shapes=[
            VMEM((BLK * CHUNK, BLK), BF16),
            VMEM((NO_V, NV_R, BLK), BF16),
            VMEM((NO_V, NO_R, BLK), BF16),
            VMEM((BLK * CHUNK, BLK), F32),
            DMA((4,)),
            DMA((NO_V,)),
            DMA((NO_V,)),
        ],
        compiler_params=pltpu.CompilerParams(vmem_limit_bytes=LIMIT),
        name="arrange",
    )(taken)


def on_device(blocks, block_vector, block_pair, block_count, occ_order, occ_coeffs, vir_coeffs):
    tiles, codes, w_all, occ = exchange(
        block_vector, block_pair, block_count, occ_order, occ_coeffs.T, vir_coeffs, blocks
    )
    half = half_transform(codes, tiles.reshape(SLOTS, BLK, BLK), occ)
    ov, oo = arrange(finish(half, w_all))
    return ov.transpose(1, 0, 2), oo.transpose(1, 0, 2)


def solution(mesh):
    placed = (
        P("vec", "row", None),
        P("row", "vec"),
        P("row", "vec"),
        P("row", "vec"),
        P(),
        P("row", None),
        P("row", None),
    )
    return jax.shard_map(
        on_device,
        mesh=mesh,
        in_specs=placed,
        out_specs=(P("row", "vec", None), P("row", "vec", None)),
        check_vma=False,
    )
```

```python
import jax
import jax.numpy as jnp
from jax import lax
from jax.experimental import pallas as pl
from jax.experimental.pallas import tpu as pltpu
from jax.sharding import PartitionSpec as P

MESH = pl.DeviceIdType.MESH
F32, BF16, I32 = jnp.float32, jnp.bfloat16, jnp.int32

N_VEC, N_ROW, N_CHIP = 32, 8, 16
CAP, SLOTS, BLK = 8, 256, 128
NAO, NO, NV, SPAN = 3072, 288, 2688, 384
VEC_DEV, PAIRS, ACROSS, TALL = 4, 72, 24, 3
NV_R, NO_R, NO_V = NV // N_ROW, NO // N_ROW, NO // N_VEC
W_R = 384
WIDE = 4 * W_R
K_HALF = NO // 2
CHUNK = 32
Q = 12
W_SHAPE = (Q, SPAN // 4, 512)
VMEM = pltpu.VMEM
LIMIT = 60 * 2**20
ANY = pl.BlockSpec(memory_space=pl.ANY)
IN_VMEM = pl.BlockSpec(memory_space=pltpu.VMEM)
DMA = pltpu.SemaphoreType.DMA


def exchange_kernel(vec_hbm, pair_hbm, count_ref, order_hbm, occ_part, vir_hbm, blocks, recv, code_out, wfull, occ_hbm,
                    vec_ref, pair_ref, order_ref, occ_in, vir_ref, code_ref, w_ref, source_ref,
                    tiles, send, source, rcode, codes, mine, theirs, occ, in_sems,
                    lsem, tsend, trecv, csend, crecv, us, ur, ds, dr, os, orc, ol):
    v, z = lax.axis_index("vec"), lax.axis_index("row")
    core, x, y = lax.rem(v, 2), lax.rem(v // 2, 4), v // 8
    up, down = lax.rem(z + 1, N_ROW), lax.rem(z + N_ROW - 1, N_ROW)
    loads = [
        pltpu.make_async_copy(src, dst, in_sems.at[n])
        for n, (src, dst) in enumerate(
            ((vec_hbm, vec_ref), (pair_hbm, pair_ref), (order_hbm, order_ref), (occ_part, occ_in), (vir_hbm, vir_ref))
        )
    ]
    for load in loads:
        load.start()
    tiles_in = pltpu.make_async_copy(blocks, tiles, lsem.at[4])
    tiles_in.start()
    barrier = pltpu.get_barrier_semaphore()

    def greet(i, carry):
        pl.semaphore_signal(barrier, inc=1, device_id=(lax.rem(v + i, N_VEC), z), device_id_type=MESH)
        return carry

    lax.fori_loop(1, N_VEC, greet, 0)
    pl.semaphore_signal(barrier, inc=1, device_id=(v, up), device_id_type=MESH)
    pl.semaphore_signal(barrier, inc=1, device_id=(v, down), device_id_type=MESH)

    count = count_ref[0, 0]
    loads[0].wait()
    vectors = vec_ref[...]
    owner = vectors // VEC_DEV
    above = lax.broadcasted_iota(I32, (SLOTS, SLOTS), 0)
    across = lax.broadcasted_iota(I32, (SLOTS, SLOTS), 1)
    owner_col = jnp.sum(jnp.where(above == across, owner, 0), axis=1, keepdims=True)
    earlier = (owner_col == owner) & (above < across)
    rank = jnp.sum(jnp.where(earlier, 1, 0), axis=0, keepdims=True)
    place = jnp.where(across[:1] < count, owner * CAP + rank, SLOTS)
    place_col = jnp.sum(jnp.where(above == across, place, 0), axis=1, keepdims=True)
    sources = jnp.sum(jnp.where(place_col == across, above, 0), axis=0, keepdims=True)
    source_ref[...] = jnp.broadcast_to(sources, (8, SLOTS))
    source_in = pltpu.make_async_copy(source_ref, source, lsem.at[5])
    source_in.start()

    loads[1].wait()
    pairs = pair_ref[...]
    code = (vectors % VEC_DEV * TALL + pairs // ACROSS) * 32 + pairs % ACROSS + 1
    valid = lax.broadcasted_iota(I32, (1, SLOTS), 1) < count
    owners = lax.broadcasted_iota(I32, (N_VEC, SLOTS), 0)
    lane = lax.broadcasted_iota(I32, (N_VEC, BLK), 1)
    hits = (owners == owner) & valid
    table = jnp.zeros((N_VEC, BLK), I32)
    for r in range(CAP):
        picked = jnp.sum(jnp.where(hits & (rank == r), code, 0), axis=1, keepdims=True)
        table = jnp.where(lane == r, picked, table)
    code_ref[...] = jnp.broadcast_to(table[:, None, :], (N_VEC, 8, BLK))
    for load in loads[2:]:
        load.wait()
    pick = (lax.broadcasted_iota(I32, (NO, NO), 0) == order_ref[...].reshape(1, NO)).astype(BF16)
    perm = lax.dot_general(occ_in[...], pick, (((0,), (0,)), ((), ())), preferred_element_type=F32)
    for half in range(2):
        @pl.when(core == half)
        def _():
            for q in range(4):
                r = 4 * half + q
                head = vir_ref[:, NV_R * r:NV_R * r + 256]
                tail = vir_ref[:, NV_R * r + 256:NV_R * r + NV_R].astype(F32)
                occ = perm[:, NO_R * r:NO_R * r + NO_R]
                zero = jnp.zeros((SPAN, 12), F32)
                last = jnp.concatenate([tail, occ, zero], axis=1).astype(BF16)
                for b in range(4):
                    rows = slice(96 * b, 96 * b + 96)
                    w_ref[4 + 4 * (q // 2) + b, :, 256 * (q % 2):256 * (q % 2) + 256] = head[rows]
                    w_ref[b, :, BLK * q:BLK * q + BLK] = last[rows]
    code, w = code_ref, w_ref
    pl.semaphore_wait(barrier, N_VEC + 1)

    own_w_out = pltpu.make_async_copy(w, wfull.at[z], lsem.at[1])
    own_tiles_out = pltpu.make_async_copy(send.at[v], recv.at[v], lsem.at[0])
    own_code = pltpu.make_async_copy(code.at[v], rcode.at[v], lsem.at[2])
    own_code.start()
    own_w_out.start()

    def remote(src, dst, send_sem, recv_sem, device):
        return pltpu.make_async_remote_copy(
            src_ref=src, dst_ref=dst, send_sem=send_sem, recv_sem=recv_sem, device_id=device, device_id_type=MESH
        )

    last = pl.ds(0, 4)

    def swap(origin, src):
        return remote(src.at[last], theirs.at[origin], os.at[origin], orc.at[origin], (v + 1 - 2 * core, z))

    def fetch(origin, src):
        return pltpu.make_async_copy(src.at[last], mine.at[origin], ol.at[origin])

    index = lax.broadcasted_iota(I32, (NO, 512), 0)
    column = lax.broadcasted_iota(I32, (NO, 512), 1)
    lane = column % BLK - (NV_R - 256)
    found = (lane >= 0) & (lane < NO_R)
    wanted = index - NO_R * (column // BLK) - lane
    pick_mine = (found & (wanted == 4 * NO_R * core)).astype(BF16)
    pick_theirs = (found & (wanted == 4 * NO_R * (1 - core))).astype(BF16)
    across = (((1,), (1,)), ((), ()))

    def pick_occ(origin):
        fetch(origin, w).wait()
        swap(origin, w).wait_recv()
        part = lax.dot_general(
            pick_mine, mine[origin].reshape(SPAN, 512), across, preferred_element_type=F32
        ) + lax.dot_general(pick_theirs, theirs[origin].reshape(SPAN, 512), across, preferred_element_type=F32)
        occ[:, pl.ds(pl.multiple_of(origin * SPAN, SPAN), SPAN)] = part.astype(BF16)

    def ring(step, piece, sign):
        origin = lax.rem(z - sign * step + 2 * N_ROW, N_ROW)
        src = w.at[piece] if step == 0 else wfull.at[origin, piece]
        ssem, rsem, to = (us, ur, up) if sign > 0 else (ds, dr, down)
        return remote(src, wfull.at[origin, piece], ssem.at[step * Q + piece], rsem.at[step * Q + piece], (v, to))

    def pieces(step, sign):
        if step < 3:
            return 0, Q
        return (0, Q // 2) if sign > 0 else (Q // 2, Q)

    def first(piece, carry):
        ring(0, piece, 1).start()
        ring(0, piece, -1).start()
        return carry

    swap(z, w).start()
    fetch(z, w).start()

    def target(j):
        return ((y + j // 8) % 4) * 8 + ((x + j // 2) % 4) * 2 + lax.rem(core + j, 2)

    def stage(d, rank):
        send[d, rank] = tiles[source[0, d * CAP + rank]]

    def give(n, carry):
        part = n // (N_VEC - 1)
        j = 1 + lax.rem(n * 11, N_VEC - 1)
        d = target(j)
        stage(d, part)
        remote(send.at[d, part], recv.at[v, part], tsend, trecv, (d, z)).start()
        return carry

    def give_code(j, carry):
        d = target(j)
        remote(code.at[d], rcode.at[v], csend, crecv, (d, z)).start()
        return carry

    tiles_in.wait()
    source_in.wait()
    lax.fori_loop(0, N_VEC - 1, give, 0)
    lax.fori_loop(0, Q, first, 0)
    lax.fori_loop(N_VEC - 1, CAP * (N_VEC - 1), give, 0)
    lax.fori_loop(1, N_VEC, give_code, 0)

    def stage_own(rank, carry):
        stage(v, rank)
        return carry

    lax.fori_loop(0, CAP, stage_own, 0)
    own_tiles_out.start()

    def origin_of(step, sign):
        return lax.rem(z - sign * step + N_ROW, N_ROW)

    def pass_occ(step, sign):
        origin = origin_of(step, sign)
        swap(origin, wfull.at[origin]).start()
        fetch(origin, wfull.at[origin]).start()

    for step in range(1, 4):
        for piece in range(Q):
            for sign in (1, -1):
                low, high = pieces(step, sign)
                ring(step - 1, piece, sign).wait_recv()
                if low <= piece < high:
                    ring(step, piece, sign).start()
                if piece == 3:
                    pass_occ(step, sign)
        if step == 2:
            pick_occ(z)
            pick_occ(origin_of(1, 1))
            pick_occ(origin_of(1, -1))
    for piece in range(4):
        ring(3, piece, 1).wait_recv()
    pass_occ(4, 1)
    for step in (2, 3):
        for sign in (1, -1):
            pick_occ(origin_of(step, sign))
    pick_occ(origin_of(4, 1))
    occ_out = pltpu.make_async_copy(occ, occ_hbm, lsem.at[3])
    occ_out.start()
    for sign in (1, -1):
        low, high = pieces(3, sign)
        for piece in range(max(low, 4), high):
            ring(3, piece, sign).wait_recv()
    for sign in (1, -1):
        for step in range(4):
            low, high = pieces(step, sign)
            for piece in range(low, high):
                ring(step, piece, sign).wait_send()
    for origin in range(N_ROW):
        swap(origin, w).wait_send()
    tile_part, code_part = recv.at[pl.ds(0, N_VEC - 1)], rcode.at[pl.ds(0, N_VEC - 1)]
    for part, semaphore in ((tile_part, tsend), (code_part, csend), (tile_part, trecv), (code_part, crecv)):
        pltpu.make_async_copy(part, part, semaphore).wait()
    own_code.wait()
    codes[...] = rcode[:, 0, :]
    codes_out = pltpu.make_async_copy(codes, code_out, lsem.at[2])
    codes_out.start()
    own_tiles_out.wait()
    own_w_out.wait()
    occ_out.wait()
    codes_out.wait()


def exchange(vectors, pairs, count, order, occ, vir, blocks):
    return pl.pallas_call(
        exchange_kernel,
        out_shape=(
            jax.ShapeDtypeStruct((N_VEC, CAP, BLK, BLK), BF16),
            jax.ShapeDtypeStruct((N_VEC, BLK), I32),
            jax.ShapeDtypeStruct((N_ROW,) + W_SHAPE, BF16),
            jax.ShapeDtypeStruct((NO, NAO), BF16),
        ),
        in_specs=[ANY, ANY, pl.BlockSpec(memory_space=pltpu.SMEM), ANY, ANY, ANY, ANY],
        out_specs=(ANY,) * 4,
        scratch_shapes=[
            VMEM((1, SLOTS), I32),
            VMEM((1, SLOTS), I32),
            VMEM((NO,), I32),
            VMEM((NO, SPAN), BF16),
            VMEM((SPAN, NV), BF16),
            VMEM((N_VEC, 8, BLK), I32),
            VMEM(W_SHAPE, BF16),
            VMEM((8, SLOTS), I32),
            VMEM((SLOTS, BLK, BLK), BF16),
            VMEM((N_VEC, CAP, BLK, BLK), BF16),
            pltpu.SMEM((8, SLOTS), I32),
            VMEM((N_VEC, 8, BLK), I32),
            VMEM((N_VEC, BLK), I32),
            VMEM((N_ROW, 4) + W_SHAPE[1:], BF16),
            VMEM((N_ROW, 4) + W_SHAPE[1:], BF16),
            VMEM((NO, NAO), BF16),
            DMA((5,)),
            DMA((6,)),
        ]
        + [DMA] * 4
        + [DMA((4 * Q,))] * 4
        + [DMA((N_ROW,))] * 3,
        compiler_params=pltpu.CompilerParams(collective_id=0, has_side_effects=True, vmem_limit_bytes=LIMIT),
        name="exchange",
    )(vectors, pairs, count, order, occ, vir, blocks)


def half_kernel(code_hbm, tiles_ref, occ_hbm, out_ref, tiles, dense, occ, code_ref, sems, more):
    group = 64
    others = [
        pltpu.make_async_copy(code_hbm, code_ref, more.at[0]),
        pltpu.make_async_copy(occ_hbm, occ, more.at[1]),
    ]
    for load in others:
        load.start()
    loads = [
        pltpu.make_async_copy(
            tiles_ref.at[pl.ds(n * group, group)], tiles.at[pl.ds(n * group, group)], sems.at[n]
        )
        for n in range(SLOTS // group)
    ]
    for load in loads:
        load.start()

    def clear(n, carry):
        dense[n] = jnp.zeros((BLK, NAO), F32)
        return carry

    lax.fori_loop(0, VEC_DEV * TALL, clear, 0)
    for load in others:
        load.wait()

    def place(n, carry):
        for r in range(CAP):
            code = code_ref[n, r] - 1

            @pl.when(code >= 0)
            def _():
                block = lax.shift_right_logical(code, 5)
                column = pl.ds(pl.multiple_of((code & 31) * BLK, BLK), BLK)
                dense[block, :, column] += tiles[n * CAP + r].astype(F32)

        return carry

    for n, load in enumerate(loads):
        load.wait()
        lax.fori_loop(n * group // CAP, (n + 1) * group // CAP, place, 0)

    for pair in range(VEC_DEV * TALL // 2):
        rows = jnp.concatenate([dense[2 * pair], dense[2 * pair + 1]], axis=0).astype(BF16)
        product = lax.dot_general(
            occ[...], rows, (((1,), (1,)), ((), ())), preferred_element_type=F32
        ).astype(BF16)
        for n in range(2):
            j, block = divmod(2 * pair + n, TALL)
            out_ref[j, :, BLK * block:BLK * block + BLK] = product[:, BLK * n:BLK * n + BLK]


def half_transform(code, tiles, occ):
    return pl.pallas_call(
        half_kernel,
        out_shape=jax.ShapeDtypeStruct((VEC_DEV, NO, SPAN), BF16),
        in_specs=[ANY] * 3,
        out_specs=IN_VMEM,
        scratch_shapes=[
            VMEM((SLOTS, BLK, BLK), BF16),
            VMEM((VEC_DEV * TALL, BLK, NAO), F32),
            VMEM((NO, NAO), BF16),
            pltpu.SMEM((N_VEC, BLK), I32),
            DMA((SLOTS // 64,)),
            DMA((2,)),
        ],
        compiler_params=pltpu.CompilerParams(vmem_limit_bytes=LIMIT),
        name="half",
    )(code, tiles, occ)


def finish_kernel(half, w_hbm, taken, w, held, total, picks, chunk, wsem, lsem, hsend, hrecv, ssend, srecv, csend, crecv, x_sem, y_sem):
    v, z = lax.axis_index("vec"), lax.axis_index("row")
    chip, core = v // 2, lax.rem(v, 2)
    giver = z // 4
    takes_own = giver == core
    other = 2 * chip + 1 - core

    loads = [pltpu.make_async_copy(w_hbm.at[r], w.at[r], wsem.at[r]) for r in range(N_ROW)]
    for load in loads:
        load.start()

    barrier = pltpu.get_barrier_semaphore()

    def greet(device):
        pl.semaphore_signal(barrier, inc=1, device_id=device, device_id_type=MESH)

    x, y = lax.rem(chip, 4), chip // 4

    def line(i, carry):
        greet((v, lax.rem(z + i, N_ROW)))
        return carry

    def other_line(i, carry):
        greet((other, lax.rem(z + i, N_ROW)))
        return carry

    def along_x(i):
        return (y * 8 + lax.rem(x + i, 4) * 2 + core, z)

    def along_y(i):
        return (lax.rem(y + i, 4) * 8 + x * 2 + core, z)

    lax.fori_loop(1, N_ROW, line, 0)
    lax.fori_loop(0, N_ROW, other_line, 0)
    for i in range(1, 4):
        greet(along_x(i))
        greet(along_y(i))
    pl.semaphore_wait(barrier, 7 + 8 + 6)
    for i in range(1, 4):
        pl.semaphore_signal(x_sem, inc=1, device_id=along_x(i), device_id_type=MESH)

    def remote(src, dst, send_sem, recv_sem, device):
        return pltpu.make_async_remote_copy(
            src_ref=src, dst_ref=dst, send_sem=send_sem, recv_sem=recv_sem, device_id=device, device_id_type=MESH
        )

    def rows(phase, h):
        return pl.ds(K_HALF * phase + 80 * h, 80 - 16 * h)

    def on_core(h, condition=True):
        return pl.when((core == h) & condition)

    def send_half(phase, j, h):
        return remote(
            half.at[j, rows(phase, h)], held.at[z, rows(phase, h)],
            hsend.at[8 * phase + 2 * j + h], hrecv.at[N_ROW * phase + z], (2 * chip + h, 4 * core + j),
        )

    def not_to_self(j, h):
        return pl.when(jnp.logical_not((4 * core + j == z) & (core == h)))

    def stay(phase, h):
        part = rows(phase, h)
        return pltpu.make_async_copy(half.at[lax.rem(z, 4), part], held.at[z, part], lsem.at[phase])

    for phase in range(2):
        for j in range(4):
            for h in range(2):
                @not_to_self(j, h)
                def _():
                    send_half(phase, j, h).start()

        for h in range(2):
            @on_core(h, takes_own)
            def _():
                stay(phase, h).start()

    def swap(phase, r, h):
        part = rows(phase, h)
        n = N_ROW * phase + r
        return remote(held.at[r, part], held.at[r, part], ssend.at[n], srecv.at[n], (other, z))

    def await_part(part, semaphore):
        pltpu.make_async_copy(part, part, semaphore).wait()

    def pass_on(phase, i):
        r = lax.rem(z + i, N_ROW)
        for h in range(2):
            def arrived_here(phase=phase, h=h):
                await_part(held.at[r, rows(phase, h)], hrecv.at[N_ROW * phase + r])

            if i == 0:
                @on_core(h, takes_own)
                def _():
                    stay(phase, h).wait()

                on_core(h, jnp.logical_not(takes_own))(arrived_here)
            else:
                on_core(h)(arrived_here)

            @on_core(h)
            def _():
                swap(phase, r, h).start()

    def arrived(phase, i):
        r = lax.rem(z + i, N_ROW)
        for h in range(2):
            @on_core(h)
            def _():
                await_part(held.at[r, rows(phase, 1 - h)], srecv.at[N_ROW * phase + r])
        return r

    pl.semaphore_wait(x_sem, 3)
    for i in range(1, 4):
        pl.semaphore_signal(y_sem, inc=1, device_id=along_y(i), device_id_type=MESH)

    height = N_VEC * CHUNK // 2
    row = lax.broadcasted_iota(I32, (height, K_HALF), 0)
    source = lax.broadcasted_iota(I32, (height, K_HALF), 1)
    inside = row % CHUNK
    base = row // CHUNK * NO_V
    for t in range(3):
        picks[t] = ((inside // NO_V == t) & (base + inside % NO_V == source)).astype(BF16)

    place = chip * N_ROW + z

    def start_final(phase):
        def body(i, carry):
            n = lax.rem(i * 37 + v * 4, 2 * N_VEC)
            to, q = n // 4 + N_VEC // 2 * phase, lax.rem(n, 4)
            src = chunk.at[q, pl.ds(pl.multiple_of(to * CHUNK, CHUNK), CHUNK)]
            dst = taken.at[pl.ds(pl.multiple_of(place * CHUNK, CHUNK), CHUNK)]
            device = (to, 4 * core + q)
            own = (to == v) & (device[1] == z)

            @pl.when(jnp.logical_not(own))
            def _():
                remote(src, dst, csend, crecv, device).start()

            @pl.when(own)
            def _():
                pltpu.make_async_copy(src, dst, lsem.at[2]).start()

            return carry

        lax.fori_loop(0, 2 * N_VEC, body, 0)

    sequence = (0, 1, 7, 2, 6, 3, 5, 4)
    for load in loads:
        load.wait()
    for phase in range(2):
        here = slice(K_HALF * phase, K_HALF * phase + K_HALF)
        for n in range(4):
            first, second = sequence[2 * n], sequence[2 * n + 1]
            pass_on(phase, first)
            pass_on(phase, second)
            a, b = arrived(phase, first), arrived(phase, second)
            deep = jnp.concatenate([held[a, here], held[b, here]], axis=1)
            for g in range(3):
                four, cols = slice(4 * g, 4 * g + 4), slice(512 * g, 512 * g + 512)
                block = jnp.concatenate([w[a, four].reshape(SPAN, 512), w[b, four].reshape(SPAN, 512)], axis=0)
                product = jnp.dot(deep, block, preferred_element_type=F32)
                if n == 0:
                    total[:, cols] = product
                else:
                    total[:, cols] += product
        stacked = jnp.zeros((height, 4 * BLK), F32)
        for t in range(3):
            if t < 2:
                addend = jnp.concatenate([total[:, 512 + 256 * q + BLK * t:640 + 256 * q + BLK * t] for q in range(4)], axis=1)
            else:
                addend = total[:, :512]
            stacked = stacked + jnp.dot(picks[t], addend.astype(BF16), preferred_element_type=F32)
        for q in range(4):
            chunk[q, height * phase:height * phase + height] = stacked[:, BLK * q:BLK * q + BLK].astype(BF16)
        if phase == 0:
            pl.semaphore_wait(y_sem, 3)
        start_final(phase)

    for phase in range(2):
        for j in range(4):
            for h in range(2):
                @not_to_self(j, h)
                def _():
                    send_half(phase, j, h).wait_send()

        for h in range(2):
            @on_core(h)
            def _():
                def wait_swap(r, carry):
                    swap(phase, r, h).wait_send()
                    return carry

                lax.fori_loop(0, N_ROW, wait_swap, 0)

    def wait_chunks(count):
        part = taken.at[pl.ds(0, count * CHUNK)]
        pltpu.make_async_copy(part, part, crecv).wait()
        pltpu.make_async_copy(part, part, csend).wait()

    @pl.when(takes_own)
    def _():
        wait_chunks(4 * N_VEC - 1)
        part = taken.at[pl.ds(0, CHUNK)]
        pltpu.make_async_copy(part, part, lsem.at[2]).wait()

    @pl.when(jnp.logical_not(takes_own))
    def _():
        wait_chunks(4 * N_VEC)


def finish(half, w):
    return pl.pallas_call(
        finish_kernel,
        out_shape=jax.ShapeDtypeStruct((BLK * CHUNK, BLK), BF16),
        in_specs=[ANY, ANY],
        out_specs=ANY,
        scratch_shapes=[
            VMEM((N_ROW,) + W_SHAPE, BF16),
            VMEM((N_ROW, NO, SPAN), BF16),
            VMEM((K_HALF, WIDE), F32),
            VMEM((3, N_VEC * CHUNK // 2, K_HALF), BF16),
            VMEM((4, N_VEC * CHUNK, BLK), BF16),
            DMA((N_ROW,)),
            DMA((3,)),
            DMA((2 * 8,)),
            DMA((2 * N_ROW,)),
            DMA((2 * N_ROW,)),
            DMA((2 * N_ROW,)),
            DMA,
            DMA,
            pltpu.SemaphoreType.REGULAR,
            pltpu.SemaphoreType.REGULAR,
        ],
        compiler_params=pltpu.CompilerParams(
            collective_id=1, has_side_effects=True, vmem_limit_bytes=LIMIT
        ),
        name="finish",
    )(half, w)


def arrange_kernel(taken_hbm, ov_hbm, oo_hbm, taken, ov, oo, wide, in_sems, ov_sems, oo_sems):
    pieces = 4
    height = BLK * CHUNK // pieces
    loads = []
    for n in range(pieces):
        part = pl.ds(n * height, height)
        loads.append(pltpu.make_async_copy(taken_hbm.at[part], taken.at[part], in_sems.at[n]))
        loads[n].start()
    for n in range(pieces):
        loads[n].wait()
        wide[n * height:n * height + height] = taken[n * height:n * height + height].astype(F32)
    writes = []
    for k in range(NO_V):
        for t in range(3):
            block = wide[pl.ds(NO_V * t + k, BLK, stride=CHUNK), :].T.astype(BF16)
            if t < 2:
                ov[k, BLK * t:BLK * t + BLK, :] = block
            else:
                ov[k, 256:NV_R, :] = block[:NV_R - 256]
                oo[k] = block[NV_R - 256:W_R - 256 - 12]
        for source, target, sems in ((ov, ov_hbm, ov_sems), (oo, oo_hbm, oo_sems)):
            writes.append(pltpu.make_async_copy(source.at[k], target.at[k], sems.at[k]))
            writes[-1].start()
    for write in writes:
        write.wait()


def arrange(taken):
    return pl.pallas_call(
        arrange_kernel,
        out_shape=(
            jax.ShapeDtypeStruct((NO_V, NV_R, BLK), BF16),
            jax.ShapeDtypeStruct((NO_V, NO_R, BLK), BF16),
        ),
        in_specs=[ANY],
        out_specs=(ANY, ANY),
        scratch_shapes=[
            VMEM((BLK * CHUNK, BLK), BF16),
            VMEM((NO_V, NV_R, BLK), BF16),
            VMEM((NO_V, NO_R, BLK), BF16),
            VMEM((BLK * CHUNK, BLK), F32),
            DMA((4,)),
            DMA((NO_V,)),
            DMA((NO_V,)),
        ],
        compiler_params=pltpu.CompilerParams(vmem_limit_bytes=LIMIT),
        name="arrange",
    )(taken)


def on_device(blocks, block_vector, block_pair, block_count, occ_order, occ_coeffs, vir_coeffs):
    tiles, codes, w_all, occ = exchange(
        block_vector, block_pair, block_count, occ_order, occ_coeffs.T, vir_coeffs, blocks
    )
    half = half_transform(codes, tiles.reshape(SLOTS, BLK, BLK), occ)
    ov, oo = arrange(finish(half, w_all))
    return ov.transpose(1, 0, 2), oo.transpose(1, 0, 2)


def solution(mesh):
    placed = (
        P("vec", "row", None),
        P("row", "vec"),
        P("row", "vec"),
        P("row", "vec"),
        P(),
        P("row", None),
        P("row", None),
    )
    return jax.shard_map(
        on_device,
        mesh=mesh,
        in_specs=placed,
        out_specs=(P("row", "vec", None), P("row", "vec", None)),
        check_vma=False,
    )
```
